32 devices in a mesh: pose: 2 (over y), aux: 4 (over z), orb: 2 (over x), ao: 2 (over core).
Axes of the slice: x: 2, y: 2, z: 4, core: 2. Of those that a mesh axis runs over, the one named last changes fastest.
Arguments:
- blocks: bfloat16 [32, 512, 512], P(('pose', 'aux', 'orb'), None, 'ao'), parts along dimension 0, may hold values from -6 to 6
- pattern: int32 [16, 4, 4], P(('pose', 'aux', 'orb'), None, 'ao'), parts along dimension 0, may hold values 0 or 1
- occupied: bfloat16 [512, 1024], P(None, 'orb'), may hold values from -0.25 to 0.25
- ligand: bfloat16 [512, 256], P(None, 'pose'), parts along dimension 1, may hold values from -0.25 to 0.25
Outputs:
- density: float32 [32], P(('pose', 'aux', 'orb')), parts along dimension 0
- cross_terms: float32 [2048, 512, 128], P(('pose', 'aux', 'orb'), 'ao'), parts along dimension 0
The draws below stay inside these ranges and needn't reach their ends.
There are 2 independent parts, one for each index of `pose`. The reference program is written for one: setup_inputs(seed, part) draws one part's arguments, and reference() takes and returns one part's arrays. A program takes and returns all parts, laid end to end along the dimension named above; an argument that names none is the same for every part. Nothing has to cross between parts.
All inputs are finite; a program needn't handle non-finite values. No bound on the sum of `pattern` on one device may be relied on, other than what follows from the above.
Results may differ from the reference program's by a relative error of at most 0.0049.
Values may be sent and summed in bfloat16 or wider, within the bound.
No kernel may reach another device: no remote copies, remote signals or barrier semaphores. Data moves between devices by JAX's collectives and lax.ppermute only.
A program may use at most 64 MiB of HBM per device.

```python
import math
import jax
import jax.numpy as jnp
from jax import lax

NOCC = 1024
NOCCB = 128
BLK = 128
NBLK = 4
NB = 512
NQB = 8
QTOT = 16


def touch_ends(result, stream_key, smallest, top_value):
    index_at = [jax.random.randint(jax.random.fold_in(stream_key, axis), (), 0, length) for axis, length in enumerate(result.shape)]
    widest = result.shape.index(max(result.shape))
    next_to = index_at[:widest] + [(index_at[widest] + 1) % result.shape[widest]] + index_at[widest + 1:]
    return result.at[tuple(index_at)].set(smallest).at[tuple(next_to)].set(top_value)


def levels(own_key, shape, shards, smallest, top_value):
    level = 1.0
    for dim, shards_of in shards:
        draws = jax.random.uniform(jax.random.fold_in(jax.random.fold_in(own_key, 6), dim), (shards_of,), jnp.float32, smallest / len(shards), top_value / len(shards))
        level = level * jnp.repeat(jnp.exp(draws), shape[dim] // shards_of).reshape((-1,) + (1,) * (len(shape) - 1 - dim))
    return level


def gaussian(key, extent, spread, bound, split=(), kind=jnp.bfloat16):
    factor_of = levels(key, extent, split, -0.22, 0.18) if split else 1.0
    drawn = jax.random.normal(key, extent, jnp.float32) * spread * factor_of
    return jnp.minimum(jnp.maximum(drawn, -bound), bound).astype(kind)


def setup_inputs(seed: int = 0, part: int = 0) -> dict:
    key_of = jax.random.split(jax.random.key(seed), 5)
    part_keys = jax.random.split(jax.random.fold_in(key_of[4], part), 5)
    blocks = gaussian(part_keys[0], (QTOT, NB, NB), 1.0, 6.0, ((0, 8), (2, 2)))
    pattern = touch_ends((jax.random.randint(part_keys[1], (NQB, NBLK, NBLK), 0, 4) < 3).astype(jnp.int32), jax.random.fold_in(part_keys[1], 1), 0, 1)
    occupied = gaussian(key_of[2], (NB, NOCC), NB ** -0.5, 0.25, ((1, 2),))
    ligand = gaussian(part_keys[3], (NB, NOCCB), NB ** -0.5, 0.25)
    return dict(blocks=blocks, pattern=pattern, occupied=occupied, ligand=ligand)


panel_width = 64

def reference(blocks, pattern, occupied, ligand):
    aux_blocks = pattern.shape[0]
    opened = jnp.repeat(jnp.repeat(pattern, BLK, axis=1), BLK, axis=2).astype(jnp.bfloat16)
    masked = (blocks.reshape(aux_blocks, QTOT // aux_blocks, NB, NB) * opened[:, None]).reshape(QTOT, NB, NB)
    stacked = masked.transpose(1, 0, 2).reshape(NB, QTOT * NB)
    panel_set = occupied.reshape(NB, NOCC // panel_width, panel_width).transpose(1, 0, 2)

    def per_panel(panel):
        halfway = jnp.dot(panel.T, stacked, preferred_element_type=jnp.float32).astype(jnp.bfloat16)
        halfway = halfway.reshape(panel_width, QTOT, NB)
        partials = jnp.einsum('iqn,ni->q', halfway.astype(jnp.float32), panel.astype(jnp.float32))
        mixed_pairs = jnp.dot(halfway.reshape(panel_width * QTOT, NB), ligand, preferred_element_type=jnp.float32)
        mixed_pairs = mixed_pairs.astype(jnp.bfloat16).reshape(panel_width, QTOT, NOCCB)
        crossed = jnp.einsum('iqn,iqj->inj', halfway.astype(jnp.float32), mixed_pairs.astype(jnp.float32))
        return (partials, crossed)
    partials, crossed = lax.map(per_panel, panel_set)
    density = lax.optimization_barrier(jnp.sum(partials, axis=0)) / math.sqrt(NOCC)
    cross_terms = crossed.reshape(NOCC, NB, NOCCB) / math.sqrt(QTOT)
    return (density, cross_terms)
```

```python
import functools
import math

import jax
import jax.numpy as jnp
from jax import lax
from jax.experimental import pallas as pl
from jax.experimental.pallas import tpu as pltpu
from jax.sharding import PartitionSpec as P

NOCC = 1024
BLK = 128
NBLK = 4
NB = 512
GROUP = 16
VMEM_LIMIT = 48 * 1024 * 1024


def half_kernel(place, pattern, blocks, *refs):
    panels, (out, masked) = refs[:-2], refs[-2:]
    aux_rows, _, nu_width = blocks.shape
    ni = out.shape[2]
    per_panel = panels[0].shape[1] // ni
    for q in range(aux_rows):
        for m in range(NBLK):
            for n in range(nu_width // BLK):
                rows, columns = pl.ds(m * BLK, BLK), pl.ds(n * BLK, BLK)
                tile = blocks[q, rows, columns]
                keep = pattern[0, m, n] != 0
                masked[rows, pl.ds(q * nu_width + n * BLK, BLK)] = jnp.where(keep, tile, jnp.zeros_like(tile))
    for k, panel in enumerate(panels):
        first = lax.rem(place[0] + k, len(panels)) * per_panel
        for s in range(per_panel):
            turned = panel[:, s * ni : (s + 1) * ni].T
            result = jnp.dot(turned, masked[...], preferred_element_type=jnp.float32).astype(jnp.bfloat16)
            for q in range(aux_rows):
                out[first + s, q] = result[:, q * nu_width : (q + 1) * nu_width]


def density_kernel(place, half, *refs):
    panels, out = refs[:-1], refs[-1]
    _, aux_rows, ni, nu_width = half.shape
    per_panel = panels[0].shape[1] // ni
    eye = lax.broadcasted_iota(jnp.int32, (nu_width, nu_width), 0) == lax.broadcasted_iota(
        jnp.int32, (nu_width, nu_width), 1
    )
    for q in range(aux_rows):
        total = jnp.zeros((nu_width, nu_width), jnp.float32)
        for k, panel in enumerate(panels):
            first = lax.rem(place[0] + k, len(panels)) * per_panel
            for s in range(per_panel):
                total += jnp.dot(
                    panel[:, s * ni : (s + 1) * ni], half[first + s, q], preferred_element_type=jnp.float32
                )
        value = jnp.sum(jnp.where(eye, total, 0.0))
        out[q] = jnp.full(out.shape[1:], value, jnp.float32)


def pair_kernel(place, arrived, ligand, out, sent):
    rows = arrived.shape[0] * arrived.shape[1]
    part = jnp.dot(
        arrived[...].reshape(rows, arrived.shape[2]), ligand[...], preferred_element_type=jnp.float32
    )
    part = part.reshape(out.shape)
    out[...] = part
    sent[...] = part.astype(jnp.bfloat16)


def cross_kernel(scale, arrived, own, other, out):
    q_total, group, nu_width = arrived.shape
    width = own.shape[2]
    depth = q_total * group
    turned = arrived[...].reshape(depth, nu_width).T
    pairs = (own[...] + other[...].astype(jnp.float32)).astype(jnp.bfloat16).reshape(depth, width)
    row = lax.broadcasted_iota(jnp.int32, (depth, width), 0) % group
    zero = jnp.zeros_like(pairs)
    for i in range(0, group, 2):
        both = jnp.concatenate([jnp.where(row == i, pairs, zero), jnp.where(row == i + 1, pairs, zero)], axis=1)
        result = jnp.dot(turned, both, preferred_element_type=jnp.float32) * scale
        out[i] = result[:, :width]
        out[i + 1] = result[:, width:]


def params():
    return pltpu.CompilerParams(vmem_limit_bytes=VMEM_LIMIT)


def whole(shape):
    return pl.BlockSpec(shape, lambda step, place: (0,) * len(shape))


def body(sizes, blocks, pattern, occupied, ligand):
    n_aux, n_orb, n_ao = sizes
    aux_rows, _, nu_width = blocks.shape
    owners = n_aux * n_orb
    ni = NOCC // owners
    q_total = aux_rows * owners
    panel_width = occupied.shape[1]
    width = ligand.shape[1]
    orb = lax.axis_index("orb")
    ao = lax.axis_index("ao")
    place = jnp.stack([orb, ao]).astype(jnp.int32)

    panels = [occupied]
    for k in range(1, n_orb):
        panels.append(lax.ppermute(occupied, "orb", [((o + k) % n_orb, o) for o in range(n_orb)]))

    half = pl.pallas_call(
        half_kernel,
        grid_spec=pltpu.PrefetchScalarGridSpec(
            num_scalar_prefetch=1,
            grid=(1,),
            in_specs=[pl.BlockSpec(memory_space=pltpu.SMEM), whole(blocks.shape)] + [whole(occupied.shape)] * n_orb,
            out_specs=whole((owners, aux_rows, ni, nu_width)),
            scratch_shapes=[pltpu.VMEM((NB, aux_rows * nu_width), jnp.bfloat16)],
        ),
        out_shape=jax.ShapeDtypeStruct((owners, aux_rows, ni, nu_width), jnp.bfloat16),
        compiler_params=params(),
        name="half_transform",
    )(place, pattern, blocks, *panels)

    arrived = lax.all_to_all(half, ("aux", "orb"), split_axis=0, concat_axis=0, tiled=True)
    arrived = arrived.reshape(q_total, ni, nu_width)

    own_rows = pl.BlockSpec((nu_width, panel_width), lambda step, place: (place[1], 0))
    value = pl.pallas_call(
        density_kernel,
        grid_spec=pltpu.PrefetchScalarGridSpec(
            num_scalar_prefetch=1,
            grid=(1,),
            in_specs=[whole(half.shape)] + [own_rows] * n_orb,
            out_specs=whole((aux_rows, 8, 128)),
        ),
        out_shape=jax.ShapeDtypeStruct((aux_rows, 8, 128), jnp.float32),
        compiler_params=params(),
        name="density_terms",
    )(place, half, *panels)[:, 0, 0]
    swap = [(c, (c + 1) % n_ao) for c in range(n_ao)]
    density = (value + lax.ppermute(value, "ao", swap)) / math.sqrt(NOCC)

    own, sent = pl.pallas_call(
        pair_kernel,
        grid_spec=pltpu.PrefetchScalarGridSpec(
            num_scalar_prefetch=1,
            grid=(1,),
            in_specs=[
                whole(arrived.shape),
                pl.BlockSpec((nu_width, width), lambda step, place: (place[1], 0)),
            ],
            out_specs=[whole((q_total, ni, width))] * 2,
        ),
        out_shape=[
            jax.ShapeDtypeStruct((q_total, ni, width), jnp.float32),
            jax.ShapeDtypeStruct((q_total, ni, width), jnp.bfloat16),
        ],
        compiler_params=params(),
        name="pair_terms",
    )(place, arrived, ligand)
    other = lax.ppermute(sent, "ao", swap)

    cross_terms = pl.pallas_call(
        functools.partial(cross_kernel, 1.0 / math.sqrt(q_total)),
        grid=(ni // GROUP,),
        in_specs=[
            pl.BlockSpec((q_total, GROUP, nu_width), lambda g: (0, g, 0)),
            pl.BlockSpec((q_total, GROUP, width), lambda g: (0, g, 0)),
            pl.BlockSpec((q_total, GROUP, width), lambda g: (0, g, 0)),
        ],
        out_specs=pl.BlockSpec((GROUP, nu_width, width), lambda g: (g, 0, 0)),
        out_shape=jax.ShapeDtypeStruct((ni, nu_width, width), jnp.float32),
        compiler_params=params(),
        name="cross_terms",
    )(arrived, own, other)
    return (density, cross_terms)


def plain_body(blocks, pattern, occupied, ligand):
    panels = lax.all_gather(occupied, "orb", axis=1, tiled=True)
    aux_rows = blocks.shape[0]
    nu_width = blocks.shape[2]
    nu_blocks = pattern.shape[2]
    opened = pattern[0].astype(jnp.bfloat16)
    masked = blocks.reshape(aux_rows, NBLK, BLK, nu_blocks, BLK) * opened[None, :, None, :, None]
    masked = masked.reshape(aux_rows, NB, nu_width)
    transformed = jnp.einsum(
        "qmn,mi->qin", masked, panels, preferred_element_type=jnp.float32
    ).astype(jnp.bfloat16)
    nu_start = lax.axis_index("ao") * nu_width
    own_rows = lax.dynamic_slice_in_dim(panels, nu_start, nu_width, 0)
    partial_value = jnp.einsum(
        "qin,ni->q", transformed, own_rows, preferred_element_type=jnp.float32
    )
    density = lax.psum(partial_value, "ao") / math.sqrt(NOCC)
    arrived = lax.all_to_all(transformed, ("aux", "orb"), split_axis=1, concat_axis=0, tiled=True)
    own_ligand = lax.dynamic_slice_in_dim(ligand, nu_start, nu_width, 0)
    pair_part = jnp.einsum("qin,nj->qij", arrived, own_ligand, preferred_element_type=jnp.float32)
    mixed_pairs = lax.psum(pair_part, "ao").astype(jnp.bfloat16)
    crossed = jnp.einsum("qin,qij->inj", arrived, mixed_pairs, preferred_element_type=jnp.float32)
    cross_terms = crossed / math.sqrt(arrived.shape[0])
    return (density, cross_terms)


def solution(mesh):
    sizes = (mesh.shape["aux"], mesh.shape["orb"], mesh.shape["ao"])
    kernels = NOCC % (sizes[0] * sizes[1] * BLK) == 0 and sizes[2] == 2
    return jax.shard_map(
        functools.partial(body, sizes) if kernels else plain_body,
        mesh=mesh,
        in_specs=(
            P(("pose", "aux", "orb"), None, "ao"),
            P(("pose", "aux", "orb"), None, "ao"),
            P(None, "orb"),
            P(None, "pose"),
        ),
        out_specs=(P(("pose", "aux", "orb")), P(("pose", "aux", "orb"), "ao", None)),
        check_vma=False,
    )
```

```python
import functools
import math

import jax
import jax.numpy as jnp
from jax import lax
from jax.experimental import pallas as pl
from jax.experimental.pallas import tpu as pltpu
from jax.sharding import PartitionSpec as P

NOCC = 1024
BLK = 128
NBLK = 4
NB = 512
GROUP = 16
VMEM_LIMIT = 48 * 1024 * 1024


def own_half_kernel(place, pattern, blocks, occupied, *refs):
    outs, masked, (held, panel, turned, sems) = refs[:-5], refs[-5], refs[-4:]
    aux_rows, _, nu_width = blocks.shape
    ni = outs[0].shape[1]
    get_blocks = pltpu.make_async_copy(blocks, held, sems.at[0])
    get_panel = pltpu.make_async_copy(occupied, panel, sems.at[1])
    get_blocks.start()
    get_panel.start()
    get_blocks.wait()
    for q in range(aux_rows):
        for m in range(NBLK):
            for n in range(nu_width // BLK):
                rows, columns = pl.ds(m * BLK, BLK), pl.ds(n * BLK, BLK)
                tile = held[q, rows, columns]
                keep = pattern[0, m, n] != 0
                masked[rows, pl.ds(q * nu_width + n * BLK, BLK)] = jnp.where(keep, tile, jnp.zeros_like(tile))
    get_panel.wait()
    for s in range(len(outs)):
        turned[s] = panel[:, s * ni : (s + 1) * ni].T
    for k, out in enumerate(outs):
        result = jnp.dot(turned[place[0] ^ k], masked[...], preferred_element_type=jnp.float32).astype(jnp.bfloat16)
        for q in range(aux_rows):
            out[q] = result[:, q * nu_width : (q + 1) * nu_width]


def other_half_kernel(place, piece, mine, theirs, *refs):
    outs, turned = refs[:-1], refs[-1]
    aux_rows, ni, nu_width = outs[0].shape
    for t in range(piece.shape[1] // ni):
        turned[t] = piece[:, t * ni : (t + 1) * ni].T

    def emit(out, t, masked):
        result = jnp.dot(turned[t], masked[...], preferred_element_type=jnp.float32).astype(jnp.bfloat16)
        for q in range(aux_rows):
            out[q] = result[:, q * nu_width : (q + 1) * nu_width]

    for k, out in enumerate(outs):
        m = place[0] ^ k
        pl.when((m & 1) == place[2])(functools.partial(emit, out, m >> 1, mine))
        pl.when((m & 1) != place[2])(functools.partial(emit, out, m >> 1, theirs))


def density_kernel(place, occupied, piece, *refs):
    near, far, out = refs[: (len(refs) - 1) // 2], refs[(len(refs) - 1) // 2 : -1], refs[-1]
    aux_rows, ni, nu_width = near[0].shape
    eye = lax.broadcasted_iota(jnp.int32, (nu_width, nu_width), 0) == lax.broadcasted_iota(
        jnp.int32, (nu_width, nu_width), 1
    )
    for q in range(aux_rows):
        total = jnp.zeros((nu_width, nu_width), jnp.float32)
        for k, message in enumerate(near):
            s = pl.multiple_of((place[0] ^ k) * ni, ni)
            total += jnp.dot(occupied[:, pl.ds(s, ni)], message[q], preferred_element_type=jnp.float32)
        for k, message in enumerate(far):
            m = place[0] ^ k
            t, h = pl.multiple_of((m >> 1) * ni, ni), pl.multiple_of((m & 1) * nu_width, nu_width)
            total += jnp.dot(
                piece[pl.ds(h, nu_width), pl.ds(t, ni)], message[q], preferred_element_type=jnp.float32
            )
        value = jnp.sum(jnp.where(eye, total, 0.0))
        out[q] = jnp.full(out.shape[1:], value, jnp.float32)


def pair_kernel(flip, place, ligand, *refs):
    arrived, own, sent = refs[:-2], refs[-2], refs[-1]
    aux_rows, ni, nu_width = arrived[0].shape
    width = ligand.shape[1]
    for k, message in enumerate(arrived):
        part = jnp.dot(
            message[...].reshape(aux_rows * ni, nu_width), ligand[...], preferred_element_type=jnp.float32
        ).reshape(aux_rows, ni, width)
        own[k] = part
        sent[k ^ flip] = part.astype(jnp.bfloat16)


def cross_kernel(scale, *refs):
    messages, pairs, out = refs[:-5], refs[-5:-1], refs[-1]
    aux_rows, group, nu_width = messages[0].shape
    width = out.shape[2]
    depth = len(messages) * aux_rows * group
    turned = jnp.concatenate([x[...].reshape(aux_rows * group, nu_width) for x in messages], axis=0).T
    summed = [pairs[j][...] + pairs[j + 1][...].astype(jnp.float32) for j in (0, 2)]
    summed = jnp.concatenate([(x * scale).astype(jnp.bfloat16).reshape(-1, group, width) for x in summed], axis=0)
    row = lax.broadcasted_iota(jnp.int32, (1, group, width), 1)
    zero = jnp.zeros_like(summed)
    for i in range(0, group, 2):
        both = [jnp.where(row == i + e, summed, zero).reshape(depth, width) for e in (0, 1)]
        result = jnp.dot(turned, jnp.concatenate(both, axis=1), preferred_element_type=jnp.float32)
        out[i] = result[:, :width]
        out[i + 1] = result[:, width:]


def params():
    return pltpu.CompilerParams(vmem_limit_bytes=VMEM_LIMIT)


def cost(flops, bytes_accessed):
    return pl.CostEstimate(flops=flops, bytes_accessed=bytes_accessed, transcendentals=0)


def whole(shape):
    return pl.BlockSpec(shape, lambda step, place: (0,) * len(shape))


def body(sizes, blocks, pattern, occupied, ligand):
    n_aux, n_orb, n_ao = sizes
    aux_rows, _, nu_width = blocks.shape
    owners = n_aux * n_orb
    ni = NOCC // owners
    q_total = aux_rows * owners
    panel_width = occupied.shape[1]
    width = ligand.shape[1]
    aux, orb, ao = (lax.axis_index(name) for name in ("aux", "orb", "ao"))
    place = jnp.stack([aux, orb, ao]).astype(jnp.int32)
    axes = ("aux", "orb", "ao")

    def number(a, o, c):
        return (a * n_orb + o) * n_ao + c

    everyone = [(a, o, c) for a in range(n_aux) for o in range(n_orb) for c in range(n_ao)]
    swap = [(c, 1 - c) for c in range(n_ao)]
    half_panel = panel_width // n_ao
    message = jax.ShapeDtypeStruct((aux_rows, ni, nu_width), jnp.bfloat16)
    masked_shape = (NB, aux_rows * nu_width)

    piece = lax.ppermute(
        lax.dynamic_slice_in_dim(occupied, ao * half_panel, half_panel, 1), "orb", [(0, 1), (1, 0)]
    )

    *near, masked = pl.pallas_call(
        own_half_kernel,
        grid_spec=pltpu.PrefetchScalarGridSpec(
            num_scalar_prefetch=1,
            grid=(1,),
            in_specs=[pl.BlockSpec(memory_space=pltpu.SMEM)] + [pl.BlockSpec(memory_space=pltpu.HBM)] * 2,
            out_specs=[whole(message.shape)] * n_aux + [whole(masked_shape)],
            scratch_shapes=[
                pltpu.VMEM(blocks.shape, jnp.bfloat16),
                pltpu.VMEM(occupied.shape, jnp.bfloat16),
                pltpu.VMEM((n_aux, ni, NB), jnp.bfloat16),
                pltpu.SemaphoreType.DMA((2,)),
            ],
        ),
        out_shape=[message] * n_aux + [jax.ShapeDtypeStruct(masked_shape, jnp.bfloat16)],
        compiler_params=params(),
        cost_estimate=cost(2 * NB * panel_width * aux_rows * nu_width, 2 << 20),
        name="own_half",
    )(place, pattern, blocks, occupied)

    near_here = []
    for k in range(n_aux):
        moves = []
        for a, o, c in everyone:
            slot = o * n_aux + (a ^ k)
            moves.append((number(a, o, c), number(slot // n_orb, slot % n_orb, c)))
        near_here.append(lax.ppermute(near[k], axes, moves))
    theirs = lax.ppermute(masked, "ao", swap)

    far = pl.pallas_call(
        other_half_kernel,
        grid_spec=pltpu.PrefetchScalarGridSpec(
            num_scalar_prefetch=1,
            grid=(1,),
            in_specs=[whole((NB, half_panel)), whole(masked_shape), whole(masked_shape)],
            out_specs=[whole(message.shape)] * n_aux,
            scratch_shapes=[pltpu.VMEM((half_panel // ni, ni, NB), jnp.bfloat16)],
        ),
        out_shape=[message] * n_aux,
        compiler_params=params(),
        cost_estimate=cost(2 * NB * panel_width * aux_rows * nu_width, 2 << 20),
        name="other_half",
    )(place, piece, masked, theirs)

    far_here = []
    for k in range(n_aux):
        moves = []
        for a, o, c in everyone:
            m = a ^ k
            slot = (1 - o) * n_aux + c * (n_aux // n_ao) + (m >> 1)
            moves.append((number(a, o, c), number(slot // n_orb, slot % n_orb, m & 1)))
        far_here.append(lax.ppermute(far[k], axes, moves))

    def pairs_of(flip, arrived, name):
        shape = (n_aux, aux_rows, ni, width)
        own, sent = pl.pallas_call(
            functools.partial(pair_kernel, flip),
            grid_spec=pltpu.PrefetchScalarGridSpec(
                num_scalar_prefetch=1,
                grid=(1,),
                in_specs=[pl.BlockSpec((nu_width, width), lambda step, place: (place[2], 0))]
                + [whole(message.shape)] * n_aux,
                out_specs=[whole(shape)] * 2,
            ),
            out_shape=[jax.ShapeDtypeStruct(shape, jnp.float32), jax.ShapeDtypeStruct(shape, jnp.bfloat16)],
            compiler_params=params(),
            cost_estimate=cost(q_total * ni * nu_width * width, 2 << 20),
            name=name,
        )(place, ligand, *arrived)
        other = lax.ppermute(sent, "ao", swap)
        return [x.reshape(n_aux * aux_rows, ni, width) for x in (own, other)]

    near_pairs = pairs_of(0, near_here, "near_pairs")
    far_pairs = pairs_of(1, far_here, "far_pairs")

    value = pl.pallas_call(
        density_kernel,
        grid_spec=pltpu.PrefetchScalarGridSpec(
            num_scalar_prefetch=1,
            grid=(1,),
            in_specs=[
                pl.BlockSpec((nu_width, panel_width), lambda step, place: (place[2], 0)),
                whole((NB, half_panel)),
            ]
            + [whole(message.shape)] * (2 * n_aux),
            out_specs=whole((aux_rows, 8, 128)),
        ),
        out_shape=jax.ShapeDtypeStruct((aux_rows, 8, 128), jnp.float32),
        compiler_params=params(),
        cost_estimate=cost(4 * nu_width * nu_width * aux_rows * NOCC, 2 << 20),
        name="density_terms",
    )(place, occupied, piece, *near, *far)[:, 0, 0]
    density = (value + lax.ppermute(value, "ao", swap)) / math.sqrt(NOCC)

    cross_terms = pl.pallas_call(
        functools.partial(cross_kernel, 1.0 / math.sqrt(q_total)),
        grid=(ni // GROUP,),
        in_specs=[pl.BlockSpec((aux_rows, GROUP, nu_width), lambda g: (0, g, 0))] * owners
        + [pl.BlockSpec((n_aux * aux_rows, GROUP, width), lambda g: (0, g, 0))] * 4,
        out_specs=pl.BlockSpec((GROUP, nu_width, width), lambda g: (g, 0, 0)),
        out_shape=jax.ShapeDtypeStruct((ni, nu_width, width), jnp.float32),
        compiler_params=params(),
        cost_estimate=cost(32 * q_total * ni * nu_width * width, 18 << 20),
        name="cross_terms",
    )(*near_here, *far_here, *near_pairs, *far_pairs)
    return (density, cross_terms)


def plain_body(blocks, pattern, occupied, ligand):
    panels = lax.all_gather(occupied, "orb", axis=1, tiled=True)
    aux_rows = blocks.shape[0]
    nu_width = blocks.shape[2]
    nu_blocks = pattern.shape[2]
    opened = pattern[0].astype(jnp.bfloat16)
    masked = blocks.reshape(aux_rows, NBLK, BLK, nu_blocks, BLK) * opened[None, :, None, :, None]
    masked = masked.reshape(aux_rows, NB, nu_width)
    transformed = jnp.einsum(
        "qmn,mi->qin", masked, panels, preferred_element_type=jnp.float32
    ).astype(jnp.bfloat16)
    nu_start = lax.axis_index("ao") * nu_width
    own_rows = lax.dynamic_slice_in_dim(panels, nu_start, nu_width, 0)
    partial_value = jnp.einsum(
        "qin,ni->q", transformed, own_rows, preferred_element_type=jnp.float32
    )
    density = lax.psum(partial_value, "ao") / math.sqrt(NOCC)
    arrived = lax.all_to_all(transformed, ("aux", "orb"), split_axis=1, concat_axis=0, tiled=True)
    own_ligand = lax.dynamic_slice_in_dim(ligand, nu_start, nu_width, 0)
    pair_part = jnp.einsum("qin,nj->qij", arrived, own_ligand, preferred_element_type=jnp.float32)
    mixed_pairs = lax.psum(pair_part, "ao").astype(jnp.bfloat16)
    crossed = jnp.einsum("qin,qij->inj", arrived, mixed_pairs, preferred_element_type=jnp.float32)
    cross_terms = crossed / math.sqrt(arrived.shape[0])
    return (density, cross_terms)


def solution(mesh):
    sizes = (mesh.shape["aux"], mesh.shape["orb"], mesh.shape["ao"])
    kernels = sizes == (4, 2, 2)
    return jax.shard_map(
        functools.partial(body, sizes) if kernels else plain_body,
        mesh=mesh,
        in_specs=(
            P(("pose", "aux", "orb"), None, "ao"),
            P(("pose", "aux", "orb"), None, "ao"),
            P(None, "orb"),
            P(None, "pose"),
        ),
        out_specs=(P(("pose", "aux", "orb")), P(("pose", "aux", "orb"), "ao", None)),
        check_vma=False,
    )
```

```python
import functools
import math

import jax
import jax.numpy as jnp
from jax import lax
from jax.experimental import pallas as pl
from jax.experimental.pallas import tpu as pltpu
from jax.sharding import PartitionSpec as P

NOCC = 1024
BLK = 128
NBLK = 4
NB = 512
GROUP = 16
MIB = 1024 * 1024
SMEM = pl.BlockSpec(memory_space=pltpu.SMEM)
VMEM = pl.BlockSpec(memory_space=pltpu.VMEM)


def spread_kernel(pattern, blocks, occupied, ligand, *refs):
    parts, (panel, orbitals, held, opened, sems) = refs[:-5], refs[-5:]
    nu_width = blocks.shape[2]
    moves = ((blocks, held), (pattern, opened), (occupied, panel), (ligand, orbitals))
    copies = [pltpu.make_async_copy(source, target, sems.at[k]) for k, (source, target) in enumerate(moves)]
    for copy in copies:
        copy.start()
    copies[0].wait()
    copies[1].wait()
    for q, part in enumerate(parts):
        for m in range(NBLK):
            for n in range(nu_width // BLK):
                rows, columns = pl.ds(m * BLK, BLK), pl.ds(n * BLK, BLK)
                tile = held[q, rows, columns]
                part[0, rows, columns] = jnp.where(opened[0, n, m] != 0, tile, jnp.zeros_like(tile))
    for copy in copies[2:]:
        copy.wait()


def slot_of(place, d):
    return (2 * (place[0] & 1) + place[1]) ^ d


def half_into(outs, place, turned, parts):
    for d, out in enumerate(outs):
        rows = turned[slot_of(place, d)]
        for q, masked in enumerate(parts):
            out[q] = jnp.dot(rows, masked[0], preferred_element_type=jnp.float32).astype(jnp.bfloat16)


def own_kernel(place, occupied, other, *refs):
    parts, turned, outs = refs[:-5], refs[-5], refs[-4:]
    ni = turned.shape[1]
    near = place[1] == place[0] // 2

    def turn(panel):
        for s in range(turned.shape[0]):
            turned[s] = panel[:, s * ni : (s + 1) * ni].T

    pl.when(near)(functools.partial(turn, occupied))
    pl.when(jnp.logical_not(near))(functools.partial(turn, other))
    half_into(outs, place, turned, parts)


def part_kernel(place, masked, turned, *outs):
    half_into(outs, place, turned, [masked])


def density_kernel(place, turned, *refs):
    messages, out = refs[:-1], refs[-1]
    nu_width = messages[0].shape[2]
    first = pl.multiple_of(place[2] * nu_width, nu_width)
    row = 0
    for group in range(0, len(messages), 4):
        for q in range(messages[group].shape[0]):
            total = 0.0
            for d in range(4):
                rows = turned[slot_of(place, d), :, pl.ds(first, nu_width)].astype(jnp.float32)
                total += jnp.sum(rows * messages[group + d][q].astype(jnp.float32))
            out[row : row + 1, :] = jnp.full((1, out.shape[1]), total, jnp.float32)
            row += 1


def pair_kernel(place, ligand, *refs):
    arrived, own, sent = refs[:-2], refs[-2], refs[-1]
    aux_rows, ni, nu_width = arrived[0].shape
    width = ligand.shape[1]
    rows = ligand[pl.ds(pl.multiple_of(place[2] * nu_width, nu_width), nu_width), :]
    for k, message in enumerate(arrived):
        part = jnp.dot(
            message[...].reshape(aux_rows * ni, nu_width), rows, preferred_element_type=jnp.float32
        ).reshape(aux_rows, ni, width)
        own[k * aux_rows : (k + 1) * aux_rows] = part
        sent[k * aux_rows : (k + 1) * aux_rows] = part.astype(jnp.bfloat16)


def cross_kernel(scale, *refs):
    messages, pairs, (out, held, sem) = refs[:12], refs[12:18], refs[18:]
    nu_width = messages[0].shape[2]
    ni, _, width = out.shape

    def step(g, carry):
        here = pl.ds(pl.multiple_of(g * GROUP, GROUP), GROUP)
        rows = [x[:, here, :].reshape(-1, nu_width) for x in messages]
        turned = jnp.concatenate(rows, axis=0).T
        summed = [pairs[j][:, here, :] + pairs[j + 1][:, here, :].astype(jnp.float32) for j in (0, 2, 4)]
        summed = jnp.concatenate([(x * scale).astype(jnp.bfloat16) for x in summed], axis=0)
        row = lax.broadcasted_iota(jnp.int32, (1, GROUP, width), 1)
        zero = jnp.zeros_like(summed)
        for i in range(0, GROUP, 2):
            both = [jnp.where(row == i + e, summed, zero).reshape(-1, width) for e in (0, 1)]
            result = jnp.dot(turned, jnp.concatenate(both, axis=1), preferred_element_type=jnp.float32)
            held[g * GROUP + i] = result[:, :width]
            held[g * GROUP + i + 1] = result[:, width:]
            if i % 4 == 2:
                done = pl.ds(g * GROUP + i - 2, 4)
                pltpu.make_async_copy(held.at[done], out.at[done], sem).start()
        return carry

    lax.fori_loop(0, ni // GROUP, step, 0)
    pltpu.make_async_copy(held, out, sem).wait()


def call(kernel, name, inputs, outputs, scratch=(), limit=16, scalars=1, flops=0, moved=1 << 20, in_spec=VMEM, out_spec=VMEM):
    inputs = list(inputs)
    results = pl.pallas_call(
        kernel,
        in_specs=[SMEM] * scalars + [in_spec] * (len(inputs) - scalars),
        out_specs=[out_spec] * len(outputs),
        out_shape=outputs,
        scratch_shapes=list(scratch),
        compiler_params=pltpu.CompilerParams(vmem_limit_bytes=limit * MIB),
        cost_estimate=pl.CostEstimate(flops=flops, bytes_accessed=moved, transcendentals=0),
        name=name,
    )(*inputs)
    return list(results)


def body(sizes, blocks, pattern, occupied, ligand):
    n_aux, n_orb, n_ao = sizes
    aux_rows, _, nu_width = blocks.shape
    owners = n_aux * n_orb
    ni = NOCC // owners
    q_total = aux_rows * owners
    panel_width = occupied.shape[1]
    width = ligand.shape[1]
    place = jnp.stack([lax.axis_index(name) for name in ("aux", "orb", "ao")]).astype(jnp.int32)
    bf16 = functools.partial(jax.ShapeDtypeStruct, dtype=jnp.bfloat16)
    f32 = functools.partial(jax.ShapeDtypeStruct, dtype=jnp.float32)

    across = [(a, a ^ 2) for a in range(n_aux)]
    swap = [(c, 1 - c) for c in range(n_ao)]
    pattern = jnp.swapaxes(pattern, 1, 2)
    *parts, panel, orbitals = call(
        spread_kernel,
        "masked_blocks",
        (pltpu.with_memory_space_constraint(x, pltpu.HBM) for x in (pattern, blocks, occupied, ligand)),
        [bf16((1, NB, nu_width))] * aux_rows + [bf16(occupied.shape), bf16(ligand.shape)],
        [
            pltpu.VMEM(blocks.shape, jnp.bfloat16),
            pltpu.SMEM(pattern.shape, pattern.dtype),
            pltpu.SemaphoreType.DMA((4,)),
        ],
        scalars=0,
        in_spec=pl.BlockSpec(memory_space=pltpu.HBM),
    )
    far = [lax.ppermute(x, "aux", across) for x in parts]
    fetch = [(a * n_orb + a // 2, a * n_orb + 1 - a // 2) for a in range(n_aux)]
    other = lax.ppermute(panel, ("aux", "orb"), fetch)

    def square(messages):
        arrived = [messages[0]] + [None] * 3
        for d in (3, 2, 1):
            moves = [
                (a * n_orb + o, (a ^ (d >> 1)) * n_orb + (o ^ (d & 1))) for a in range(n_aux) for o in range(n_orb)
            ]
            arrived[d] = lax.ppermute(messages[d], ("aux", "orb"), moves)
        return arrived

    work = 2 * NB * panel_width * nu_width
    turned, *own = call(
        own_kernel,
        "own_half",
        (place, panel, other, *parts),
        [bf16((4, ni, NB))] + [bf16((aux_rows, ni, nu_width))] * 4,
        flops=work * aux_rows,
    )
    sent = [own]
    arrived = [square(own)]
    for q in range(aux_rows):
        messages = call(
            part_kernel,
            f"part_half_{q}",
            (place, far[q], turned),
            [bf16((1, ni, nu_width))] * 4,
            flops=work,
        )
        sent.append(messages)
        arrived.append(square(messages))

    value = call(
        density_kernel,
        "density_terms",
        (place, turned, *sum(sent, [])),
        [f32((2 * aux_rows, 128))],
        flops=8 * panel_width * nu_width * aux_rows,
    )[0]
    near = value[:aux_rows, 0] + lax.ppermute(value, "ao", swap)[:aux_rows, 0]
    crossing = [(a * n_ao + c, (a ^ 2) * n_ao + 1 - c) for a in range(n_aux) for c in range(n_ao)]
    back = lax.ppermute(value, "aux", across)[aux_rows:, 0] + lax.ppermute(value, ("aux", "ao"), crossing)[aux_rows:, 0]
    density = (near + back) / math.sqrt(NOCC)

    pairs = []
    for k, group in enumerate(arrived):
        shape = (4 * group[0].shape[0], ni, width)
        kept, given = call(
            pair_kernel,
            f"pair_terms_{k}",
            (place, orbitals, *group),
            [f32(shape), bf16(shape)],
            flops=2 * shape[0] * ni * nu_width * width,
        )
        pairs += [kept, lax.ppermute(given, "ao", swap)]

    result = (ni, nu_width, width)
    cross_terms = call(
        functools.partial(cross_kernel, 1.0 / math.sqrt(q_total)),
        "cross_terms",
        (*sum(arrived, []), *pairs),
        [f32(result)],
        [pltpu.VMEM(result, jnp.float32), pltpu.SemaphoreType.DMA],
        limit=32,
        scalars=0,
        flops=32 * q_total * ni * nu_width * width,
        moved=18 * MIB,
        out_spec=pl.BlockSpec(memory_space=pltpu.HBM),
    )[0]
    return (density, cross_terms)


def plain_body(blocks, pattern, occupied, ligand):
    panels = lax.all_gather(occupied, "orb", axis=1, tiled=True)
    aux_rows = blocks.shape[0]
    nu_width = blocks.shape[2]
    nu_blocks = pattern.shape[2]
    opened = pattern[0].astype(jnp.bfloat16)
    masked = blocks.reshape(aux_rows, NBLK, BLK, nu_blocks, BLK) * opened[None, :, None, :, None]
    masked = masked.reshape(aux_rows, NB, nu_width)
    transformed = jnp.einsum(
        "qmn,mi->qin", masked, panels, preferred_element_type=jnp.float32
    ).astype(jnp.bfloat16)
    nu_start = lax.axis_index("ao") * nu_width
    own_rows = lax.dynamic_slice_in_dim(panels, nu_start, nu_width, 0)
    partial_value = jnp.einsum(
        "qin,ni->q", transformed, own_rows, preferred_element_type=jnp.float32
    )
    density = lax.psum(partial_value, "ao") / math.sqrt(NOCC)
    arrived = lax.all_to_all(transformed, ("aux", "orb"), split_axis=1, concat_axis=0, tiled=True)
    own_ligand = lax.dynamic_slice_in_dim(ligand, nu_start, nu_width, 0)
    pair_part = jnp.einsum("qin,nj->qij", arrived, own_ligand, preferred_element_type=jnp.float32)
    mixed_pairs = lax.psum(pair_part, "ao").astype(jnp.bfloat16)
    crossed = jnp.einsum("qin,qij->inj", arrived, mixed_pairs, preferred_element_type=jnp.float32)
    cross_terms = crossed / math.sqrt(arrived.shape[0])
    return (density, cross_terms)


def solution(mesh):
    sizes = (mesh.shape["aux"], mesh.shape["orb"], mesh.shape["ao"])
    kernels = sizes == (4, 2, 2)
    return jax.shard_map(
        functools.partial(body, sizes) if kernels else plain_body,
        mesh=mesh,
        in_specs=(
            P(("pose", "aux", "orb"), None, "ao"),
            P(("pose", "aux", "orb"), None, "ao"),
            P(None, "orb"),
            P(None, "pose"),
        ),
        out_specs=(P(("pose", "aux", "orb")), P(("pose", "aux", "orb"), "ao", None)),
        check_vma=False,
    )
```

```python
import functools
import math

import jax
import jax.numpy as jnp
from jax import lax
from jax.experimental import pallas as pl
from jax.experimental.pallas import tpu as pltpu
from jax.sharding import PartitionSpec as P

NOCC = 1024
BLK = 128
NBLK = 4
NB = 512
GROUP = 16
MIB = 1024 * 1024
SMEM = pl.BlockSpec(memory_space=pltpu.SMEM)
VMEM = pl.BlockSpec(memory_space=pltpu.VMEM)


def masked_kernel(pattern, blocks, occupied, ligand, masked, panel, orbitals, held, opened, sems):
    aux_rows, _, nu_width = blocks.shape
    moves = ((blocks, held), (pattern, opened), (occupied, panel), (ligand, orbitals))
    copies = [pltpu.make_async_copy(source, target, sems.at[k]) for k, (source, target) in enumerate(moves)]
    for copy in copies:
        copy.start()
    copies[0].wait()
    copies[1].wait()
    for q in range(aux_rows):
        for m in range(NBLK):
            for n in range(nu_width // BLK):
                rows, columns = pl.ds(m * BLK, BLK), pl.ds(n * BLK, BLK)
                tile = held[q, rows, columns]
                masked[q, rows, columns] = jnp.where(opened[0, n, m] != 0, tile, jnp.zeros_like(tile))
    for copy in copies[2:]:
        copy.wait()


def slot_of(place, d):
    return (2 * (place[0] & 1) + place[1]) ^ d


def half_into(outs, place, turned, masked):
    for d, out in enumerate(outs):
        rows = turned[slot_of(place, d)]
        for q in range(out.shape[0]):
            out[q] = jnp.dot(rows, masked[q], preferred_element_type=jnp.float32).astype(jnp.bfloat16)


def own_kernel(place, occupied, other, masked, turned, *outs):
    ni = turned.shape[1]
    near = place[1] == place[0] // 2

    def turn(panel):
        for s in range(turned.shape[0]):
            turned[s] = panel[:, s * ni : (s + 1) * ni].T

    pl.when(near)(functools.partial(turn, occupied))
    pl.when(jnp.logical_not(near))(functools.partial(turn, other))
    half_into(outs, place, turned, masked)


def density_kernel(place, occupied, other, masked, turned, *refs):
    messages, out = refs[:-1], refs[-1]
    aux_rows, ni, nu_width = messages[0].shape
    own = pl.ds(pl.multiple_of(place[2] * nu_width, nu_width), nu_width)
    near = place[1] == place[0] // 2

    def near_terms(q):
        total = 0.0
        for d in range(4):
            rows = turned[slot_of(place, d), :, own].astype(jnp.float32)
            total += jnp.sum(rows * messages[d][q].astype(jnp.float32))
        return total

    def far_terms(panel):
        totals = [near_terms(q) for q in range(aux_rows)]
        for s in range(4):
            rows = panel[:, s * ni : (s + 1) * ni].T
            weights = panel[own, s * ni : (s + 1) * ni].T.astype(jnp.float32)
            for q in range(aux_rows):
                result = jnp.dot(rows, masked[q], preferred_element_type=jnp.float32).astype(jnp.bfloat16)
                totals[q] += jnp.sum(weights * result.astype(jnp.float32))
        for q in range(aux_rows):
            out[q : q + 1, :] = jnp.full((1, out.shape[1]), totals[q], jnp.float32)

    pl.when(near)(functools.partial(far_terms, other))
    pl.when(jnp.logical_not(near))(functools.partial(far_terms, occupied))


def far_kernel(place, value, value_there, masked, turned, density, *outs):
    density[...] = (value[...] + value_there[...]) / math.sqrt(NOCC)
    half_into(outs, place, turned, masked)


def pair_kernel(place, after, ligand, *refs):
    arrived, own, sent = refs[:-2], refs[-2], refs[-1]
    aux_rows, ni, nu_width = arrived[0].shape
    width = ligand.shape[1]
    rows = ligand[pl.ds(pl.multiple_of(place[2] * nu_width, nu_width), nu_width), :]
    for k, message in enumerate(arrived):
        part = jnp.dot(
            message[...].reshape(aux_rows * ni, nu_width), rows, preferred_element_type=jnp.float32
        ).reshape(aux_rows, ni, width)
        own[k * aux_rows : (k + 1) * aux_rows] = part
        sent[k * aux_rows : (k + 1) * aux_rows] = part.astype(jnp.bfloat16)


def turn_kernel(*refs):
    messages, out = refs[:-1], refs[-1]
    nu_width = messages[0].shape[2]
    for g in range(out.shape[0]):
        here = pl.ds(g * GROUP, GROUP)
        out[g] = jnp.concatenate([x[:, here, :].reshape(-1, nu_width) for x in messages], axis=0).T


def pair_and_turn_kernel(place, after, ligand, *refs):
    pair_kernel(place, after, ligand, *refs[:-1])
    turn_kernel(*refs[:-3], refs[-1])


def cross_kernel(scale, near, far, *refs):
    pairs, (out, held, sem) = refs[:4], refs[4:]
    ni, _, width = out.shape

    def step(g, carry):
        here = pl.ds(pl.multiple_of(g * GROUP, GROUP), GROUP)
        turned = jnp.concatenate([near[g], far[g]], axis=1)
        summed = [pairs[j][:, here, :] + pairs[j + 1][:, here, :].astype(jnp.float32) for j in (0, 2)]
        summed = jnp.concatenate([(x * scale).astype(jnp.bfloat16) for x in summed], axis=0)
        row = lax.broadcasted_iota(jnp.int32, (1, GROUP, width), 1)
        zero = jnp.zeros_like(summed)
        for i in range(0, GROUP, 2):
            both = [jnp.where(row == i + e, summed, zero).reshape(-1, width) for e in (0, 1)]
            result = jnp.dot(turned, jnp.concatenate(both, axis=1), preferred_element_type=jnp.float32)
            held[g * GROUP + i] = result[:, :width]
            held[g * GROUP + i + 1] = result[:, width:]
            if i % 4 == 2:
                done = pl.ds(g * GROUP + i - 2, 4)
                pltpu.make_async_copy(held.at[done], out.at[done], sem).start()
        return carry

    lax.fori_loop(0, ni // GROUP, step, 0)
    pltpu.make_async_copy(held, out, sem).wait()


def call(kernel, name, inputs, outputs, scratch=(), limit=16, scalars=1, flops=0, moved=1 << 20, in_spec=VMEM, out_spec=VMEM):
    inputs = list(inputs)
    results = pl.pallas_call(
        kernel,
        in_specs=[SMEM] * scalars + [in_spec] * (len(inputs) - scalars),
        out_specs=[out_spec] * len(outputs),
        out_shape=outputs,
        scratch_shapes=list(scratch),
        compiler_params=pltpu.CompilerParams(vmem_limit_bytes=limit * MIB),
        cost_estimate=pl.CostEstimate(flops=flops, bytes_accessed=moved, transcendentals=0),
        name=name,
    )(*inputs)
    return list(results)


def body(sizes, blocks, pattern, occupied, ligand):
    n_aux, n_orb, n_ao = sizes
    aux_rows, _, nu_width = blocks.shape
    owners = n_aux * n_orb
    ni = NOCC // owners
    q_total = aux_rows * owners
    panel_width = occupied.shape[1]
    width = ligand.shape[1]
    place = jnp.stack([lax.axis_index(name) for name in ("aux", "orb", "ao")]).astype(jnp.int32)
    bf16 = functools.partial(jax.ShapeDtypeStruct, dtype=jnp.bfloat16)
    f32 = functools.partial(jax.ShapeDtypeStruct, dtype=jnp.float32)

    across = [(a, a ^ 2) for a in range(n_aux)]
    swap = [(c, 1 - c) for c in range(n_ao)]
    pattern = jnp.swapaxes(pattern, 1, 2)
    masked, panel, orbitals = call(
        masked_kernel,
        "masked_blocks",
        (pltpu.with_memory_space_constraint(x, pltpu.HBM) for x in (pattern, blocks, occupied, ligand)),
        [bf16(blocks.shape), bf16(occupied.shape), bf16(ligand.shape)],
        [
            pltpu.VMEM(blocks.shape, jnp.bfloat16),
            pltpu.SMEM(pattern.shape, pattern.dtype),
            pltpu.SemaphoreType.DMA((4,)),
        ],
        scalars=0,
        in_spec=pl.BlockSpec(memory_space=pltpu.HBM),
    )
    far_masked = lax.ppermute(masked, "aux", across)
    other = lax.ppermute(panel, "orb", swap)

    def square(messages):
        arrived = [messages[0]] + [None] * 3
        for d in (3, 2, 1):
            moves = [
                (a * n_orb + o, (a ^ (d >> 1)) * n_orb + (o ^ (d & 1))) for a in range(n_aux) for o in range(n_orb)
            ]
            arrived[d] = lax.ppermute(messages[d], ("aux", "orb"), moves)
        return arrived

    work = 2 * NB * panel_width * nu_width * aux_rows
    messages = [bf16((aux_rows, ni, nu_width))] * 4
    turned, *own = call(
        own_kernel, "own_half", (place, panel, other, masked), [bf16((4, ni, NB))] + messages, flops=work
    )
    own_here = square(own)
    value = call(
        density_kernel,
        "density_terms",
        (place, panel, other, masked, turned, *own),
        [f32((aux_rows, 128))],
        flops=work,
    )[0]
    density, *far = call(
        far_kernel,
        "far_half",
        (place, value, lax.ppermute(value, "ao", swap), far_masked, turned),
        [f32((aux_rows, 128))] + messages,
        flops=work,
    )
    far_here = square(far)

    shape = (4 * aux_rows, ni, width)
    kept_and_given = [f32(shape), bf16(shape)]
    side = [bf16((ni // GROUP, nu_width, 4 * aux_rows * GROUP))]
    pair_work = 2 * shape[0] * ni * nu_width * width
    own_kept, own_given, own_rows = call(
        pair_and_turn_kernel,
        "own_pairs",
        (place, density, orbitals, *own_here),
        kept_and_given + side,
        flops=pair_work,
    )
    own_pairs = (own_kept, lax.ppermute(own_given, "ao", swap))
    far_kept, far_given = call(
        pair_kernel, "far_pairs", (place, density, orbitals, *far_here), kept_and_given, flops=pair_work
    )
    far_pairs = (far_kept, lax.ppermute(far_given, "ao", swap))
    far_rows = call(turn_kernel, "far_turned", far_here, side, scalars=0)[0]

    result = (ni, nu_width, width)
    cross_terms = call(
        functools.partial(cross_kernel, 1.0 / math.sqrt(q_total)),
        "cross_terms",
        (own_rows, far_rows, *own_pairs, *far_pairs),
        [f32(result)],
        [pltpu.VMEM(result, jnp.float32), pltpu.SemaphoreType.DMA],
        limit=32,
        scalars=0,
        flops=32 * q_total * ni * nu_width * width,
        moved=18 * MIB,
        out_spec=pl.BlockSpec(memory_space=pltpu.HBM),
    )[0]
    return (density[:, 0], cross_terms)


def plain_body(blocks, pattern, occupied, ligand):
    panels = lax.all_gather(occupied, "orb", axis=1, tiled=True)
    aux_rows = blocks.shape[0]
    nu_width = blocks.shape[2]
    nu_blocks = pattern.shape[2]
    opened = pattern[0].astype(jnp.bfloat16)
    masked = blocks.reshape(aux_rows, NBLK, BLK, nu_blocks, BLK) * opened[None, :, None, :, None]
    masked = masked.reshape(aux_rows, NB, nu_width)
    transformed = jnp.einsum(
        "qmn,mi->qin", masked, panels, preferred_element_type=jnp.float32
    ).astype(jnp.bfloat16)
    nu_start = lax.axis_index("ao") * nu_width
    own_rows = lax.dynamic_slice_in_dim(panels, nu_start, nu_width, 0)
    partial_value = jnp.einsum(
        "qin,ni->q", transformed, own_rows, preferred_element_type=jnp.float32
    )
    density = lax.psum(partial_value, "ao") / math.sqrt(NOCC)
    arrived = lax.all_to_all(transformed, ("aux", "orb"), split_axis=1, concat_axis=0, tiled=True)
    own_ligand = lax.dynamic_slice_in_dim(ligand, nu_start, nu_width, 0)
    pair_part = jnp.einsum("qin,nj->qij", arrived, own_ligand, preferred_element_type=jnp.float32)
    mixed_pairs = lax.psum(pair_part, "ao").astype(jnp.bfloat16)
    crossed = jnp.einsum("qin,qij->inj", arrived, mixed_pairs, preferred_element_type=jnp.float32)
    cross_terms = crossed / math.sqrt(arrived.shape[0])
    return (density, cross_terms)


def solution(mesh):
    sizes = (mesh.shape["aux"], mesh.shape["orb"], mesh.shape["ao"])
    kernels = sizes == (4, 2, 2)
    return jax.shard_map(
        functools.partial(body, sizes) if kernels else plain_body,
        mesh=mesh,
        in_specs=(
            P(("pose", "aux", "orb"), None, "ao"),
            P(("pose", "aux", "orb"), None, "ao"),
            P(None, "orb"),
            P(None, "pose"),
        ),
        out_specs=(P(("pose", "aux", "orb")), P(("pose", "aux", "orb"), "ao", None)),
        check_vma=False,
    )
```

```python
import functools
import math

import jax
import jax.numpy as jnp
from jax import lax
from jax.experimental import pallas as pl
from jax.experimental.pallas import tpu as pltpu
from jax.sharding import PartitionSpec as P

NOCC = 1024
BLK = 128
NBLK = 4
NB = 512
GROUP = 16
MIB = 1024 * 1024
SMEM = pl.BlockSpec(memory_space=pltpu.SMEM)
VMEM = pl.BlockSpec(memory_space=pltpu.VMEM)


def first_kernel(place, pattern, blocks, occupied, ligand, masked, panel, first, second, orbitals, held, opened, sems):
    aux_rows, _, nu_width = blocks.shape
    get = [(blocks, held), (pattern, opened), (occupied, panel), (ligand, orbitals)]
    get = [pltpu.make_async_copy(source, target, sems.at[k]) for k, (source, target) in enumerate(get)]
    for copy in get:
        copy.start()

    def fill(panel_slot, blocks_slot):
        again = pltpu.make_async_copy(occupied, panel_slot, sems.at[len(get)])
        again.start()
        get[0].wait()
        get[1].wait()
        for q in range(aux_rows):
            for m in range(NBLK):
                for n in range(nu_width // BLK):
                    rows, columns = pl.ds(m * BLK, BLK), pl.ds(n * BLK, BLK)
                    wide = pl.ds(q * nu_width + n * BLK, BLK)
                    tile = held[q, rows, columns]
                    tile = jnp.where(opened[0, n, m] != 0, tile, jnp.zeros_like(tile))
                    masked[rows, wide] = tile
                    blocks_slot[rows, wide] = tile
        again.wait()

    pl.when(place[2] == 0)(functools.partial(fill, first, second))
    pl.when(place[2] != 0)(functools.partial(fill, second, first))
    for copy in get[2:]:
        copy.wait()


def slot_of(place, d):
    return (2 * (place[0] & 1) + place[1]) ^ d


def rows_kernel(place, masked, panel, got_first, got_second, turned, *outs):
    ni = turned.shape[1]
    _, _, nu_width = outs[0].shape
    aux_rows = outs[0].shape[0] // 2
    near = place[1] == place[0] // 2
    first_core = place[2] == 0

    def turn(source):
        for s in range(turned.shape[0]):
            turned[s] = source[:, s * ni : (s + 1) * ni].T

    pl.when(near)(functools.partial(turn, panel))
    pl.when(jnp.logical_and(jnp.logical_not(near), first_core))(functools.partial(turn, got_first))
    pl.when(jnp.logical_not(jnp.logical_or(near, first_core)))(functools.partial(turn, got_second))

    def half(source, first):
        for k, out in enumerate(outs):
            d = k ^ (3 * place[2]) if k in (1, 2) else k
            result = jnp.dot(turned[slot_of(place, d)], source[...], preferred_element_type=jnp.float32)
            result = result.astype(jnp.bfloat16)
            for q in range(aux_rows):
                out[first + q] = result[:, q * nu_width : (q + 1) * nu_width]

    half(masked, 0)
    pl.when(first_core)(functools.partial(half, got_second, aux_rows))
    pl.when(jnp.logical_not(first_core))(functools.partial(half, got_first, aux_rows))


def density_kernel(place, panel, got_first, got_second, masked, turned, *refs):
    messages, out = refs[:-1], refs[-1]
    _, ni, nu_width = messages[0].shape
    aux_rows = messages[0].shape[0] // 2
    own = pl.ds(pl.multiple_of(place[2] * nu_width, nu_width), nu_width)
    near = place[1] == place[0] // 2
    first_core = place[2] == 0

    def terms(panel):
        totals = [0.0] * aux_rows
        for k, message in enumerate(messages):
            d = k ^ (3 * place[2]) if k in (1, 2) else k
            rows = turned[slot_of(place, d), :, own].astype(jnp.float32)
            for q in range(aux_rows):
                totals[q] += jnp.sum(rows * message[q].astype(jnp.float32))
        for s in range(4):
            rows = panel[:, s * ni : (s + 1) * ni].T
            weights = panel[own, s * ni : (s + 1) * ni].T.astype(jnp.float32)
            result = jnp.dot(rows, masked[...], preferred_element_type=jnp.float32).astype(jnp.bfloat16)
            for q in range(aux_rows):
                totals[q] += jnp.sum(weights * result[:, q * nu_width : (q + 1) * nu_width].astype(jnp.float32))
        for q in range(aux_rows):
            out[q : q + 1, :] = jnp.full((1, out.shape[1]), totals[q], jnp.float32)

    pl.when(jnp.logical_not(near))(functools.partial(terms, panel))
    pl.when(jnp.logical_and(near, first_core))(functools.partial(terms, got_first))
    pl.when(jnp.logical_and(near, jnp.logical_not(first_core)))(functools.partial(terms, got_second))


def pair_kernel(place, after, ligand, *refs):
    arrived, own, sent = refs[:-2], refs[-2], refs[-1]
    aux_rows, ni, nu_width = arrived[0].shape
    width = ligand.shape[1]
    rows = ligand[pl.ds(pl.multiple_of(place[2] * nu_width, nu_width), nu_width), :]
    for k, message in enumerate(arrived):
        part = jnp.dot(
            message[...].reshape(aux_rows * ni, nu_width), rows, preferred_element_type=jnp.float32
        ).reshape(aux_rows, ni, width)
        there = k ^ 3 if k in (1, 2) else k
        own[k * aux_rows : (k + 1) * aux_rows] = part
        sent[there * aux_rows : (there + 1) * aux_rows] = part.astype(jnp.bfloat16)


def turn_kernel(*refs):
    messages, out = refs[:-1], refs[-1]
    nu_width = messages[0].shape[2]
    for g in range(out.shape[0]):
        here = pl.ds(g * GROUP, GROUP)
        out[g] = jnp.concatenate([x[:, here, :].reshape(-1, nu_width) for x in messages], axis=0).T


def cross_kernel(scale, turned, own, other, out, held, sem):
    ni, _, width = out.shape

    def step(g, carry):
        here = pl.ds(pl.multiple_of(g * GROUP, GROUP), GROUP)
        summed = ((own[:, here, :] + other[:, here, :].astype(jnp.float32)) * scale).astype(jnp.bfloat16)
        row = lax.broadcasted_iota(jnp.int32, (1, GROUP, width), 1)
        zero = jnp.zeros_like(summed)
        for i in range(0, GROUP, 2):
            both = [jnp.where(row == i + e, summed, zero).reshape(-1, width) for e in (0, 1)]
            result = jnp.dot(turned[g], jnp.concatenate(both, axis=1), preferred_element_type=jnp.float32)
            held[g * GROUP + i] = result[:, :width]
            held[g * GROUP + i + 1] = result[:, width:]
            if i % 4 == 2:
                done = pl.ds(g * GROUP + i - 2, 4)
                pltpu.make_async_copy(held.at[done], out.at[done], sem).start()
        return carry

    lax.fori_loop(0, ni // GROUP, step, 0)
    pltpu.make_async_copy(held, out, sem).wait()


def call(kernel, name, inputs, outputs, scratch=(), limit=16, scalars=1, flops=0, moved=1 << 20, in_spec=VMEM, out_spec=VMEM):
    inputs = list(inputs)
    results = pl.pallas_call(
        kernel,
        in_specs=[SMEM] * scalars + [in_spec] * (len(inputs) - scalars),
        out_specs=[out_spec] * len(outputs),
        out_shape=outputs,
        scratch_shapes=list(scratch),
        compiler_params=pltpu.CompilerParams(vmem_limit_bytes=limit * MIB),
        cost_estimate=pl.CostEstimate(flops=flops, bytes_accessed=moved, transcendentals=0),
        name=name,
    )(*inputs)
    return list(results)


def body(sizes, blocks, pattern, occupied, ligand):
    n_aux, n_orb, n_ao = sizes
    aux_rows, _, nu_width = blocks.shape
    owners = n_aux * n_orb
    ni = NOCC // owners
    q_total = aux_rows * owners
    panel_width = occupied.shape[1]
    width = ligand.shape[1]
    place = jnp.stack([lax.axis_index(name) for name in ("aux", "orb", "ao")]).astype(jnp.int32)
    bf16 = functools.partial(jax.ShapeDtypeStruct, dtype=jnp.bfloat16)
    f32 = functools.partial(jax.ShapeDtypeStruct, dtype=jnp.float32)

    swap = [(c, 1 - c) for c in range(n_ao)]
    axes = ("aux", "orb", "ao")
    everyone = [(a, o, c) for a in range(n_aux) for o in range(n_orb) for c in range(n_ao)]

    def send(x, target):
        number = lambda a, o, c: (a * n_orb + o) * n_ao + c
        return lax.ppermute(x, axes, [(number(*here), number(*target(*here))) for here in everyone])

    pattern = jnp.swapaxes(pattern, 1, 2)
    square = bf16((NB, panel_width))
    hbm = pl.BlockSpec(memory_space=pltpu.HBM)
    masked, panel, first, second, orbitals = call(
        first_kernel,
        "masked_blocks",
        (place, *(pltpu.with_memory_space_constraint(x, pltpu.HBM) for x in (pattern, blocks, occupied, ligand))),
        [square] * 4 + [bf16(ligand.shape)],
        [
            pltpu.VMEM(blocks.shape, jnp.bfloat16),
            pltpu.SMEM(pattern.shape, pattern.dtype),
            pltpu.SemaphoreType.DMA((5,)),
        ],
        in_spec=hbm,
    )
    got_first = send(first, lambda a, o, c: (a ^ 2, o, c) if c else (a, 1 - o, c))
    got_second = send(second, lambda a, o, c: (a, 1 - o, c) if c else (a ^ 2, o, c))

    work = 2 * NB * panel_width * nu_width * aux_rows
    turned, *rows = call(
        rows_kernel,
        "half_rows",
        (place, masked, panel, got_first, got_second),
        [bf16((4, ni, NB))] + [bf16((2 * aux_rows, ni, nu_width))] * 4,
        flops=2 * work,
    )
    arrived = [rows[0]]
    arrived.append(send(rows[1], lambda a, o, c: (a ^ 1, o, c) if c else (a, 1 - o, c)))
    arrived.append(send(rows[2], lambda a, o, c: (a, 1 - o, c) if c else (a ^ 1, o, c)))
    arrived.append(send(rows[3], lambda a, o, c: (a ^ 1, 1 - o, c)))

    value = call(
        density_kernel,
        "density_terms",
        (place, panel, got_first, got_second, masked, turned, *rows),
        [f32((aux_rows, 128))],
        flops=work,
    )[0]
    density = (value[:, 0] + lax.ppermute(value, "ao", swap)[:, 0]) / math.sqrt(NOCC)

    shape = (q_total, ni, width)
    own, given = call(
        pair_kernel,
        "pair_terms",
        (place, value, orbitals, *arrived),
        [f32(shape), bf16(shape)],
        flops=2 * q_total * ni * nu_width * width,
    )
    other = lax.ppermute(given, "ao", swap)
    columns = call(turn_kernel, "turned", arrived, [bf16((ni // GROUP, nu_width, q_total * GROUP))], scalars=0)[0]

    result = (ni, nu_width, width)
    cross_terms = call(
        functools.partial(cross_kernel, 1.0 / math.sqrt(q_total)),
        "cross_terms",
        (columns, own, other),
        [f32(result)],
        [pltpu.VMEM(result, jnp.float32), pltpu.SemaphoreType.DMA],
        limit=32,
        scalars=0,
        flops=32 * q_total * ni * nu_width * width,
        moved=18 * MIB,
        out_spec=hbm,
    )[0]
    return (density, cross_terms)


def plain_body(blocks, pattern, occupied, ligand):
    panels = lax.all_gather(occupied, "orb", axis=1, tiled=True)
    aux_rows = blocks.shape[0]
    nu_width = blocks.shape[2]
    nu_blocks = pattern.shape[2]
    opened = pattern[0].astype(jnp.bfloat16)
    masked = blocks.reshape(aux_rows, NBLK, BLK, nu_blocks, BLK) * opened[None, :, None, :, None]
    masked = masked.reshape(aux_rows, NB, nu_width)
    transformed = jnp.einsum(
        "qmn,mi->qin", masked, panels, preferred_element_type=jnp.float32
    ).astype(jnp.bfloat16)
    nu_start = lax.axis_index("ao") * nu_width
    own_rows = lax.dynamic_slice_in_dim(panels, nu_start, nu_width, 0)
    partial_value = jnp.einsum(
        "qin,ni->q", transformed, own_rows, preferred_element_type=jnp.float32
    )
    density = lax.psum(partial_value, "ao") / math.sqrt(NOCC)
    arrived = lax.all_to_all(transformed, ("aux", "orb"), split_axis=1, concat_axis=0, tiled=True)
    own_ligand = lax.dynamic_slice_in_dim(ligand, nu_start, nu_width, 0)
    pair_part = jnp.einsum("qin,nj->qij", arrived, own_ligand, preferred_element_type=jnp.float32)
    mixed_pairs = lax.psum(pair_part, "ao").astype(jnp.bfloat16)
    crossed = jnp.einsum("qin,qij->inj", arrived, mixed_pairs, preferred_element_type=jnp.float32)
    cross_terms = crossed / math.sqrt(arrived.shape[0])
    return (density, cross_terms)


def solution(mesh):
    sizes = (mesh.shape["aux"], mesh.shape["orb"], mesh.shape["ao"])
    kernels = sizes == (4, 2, 2)
    return jax.shard_map(
        functools.partial(body, sizes) if kernels else plain_body,
        mesh=mesh,
        in_specs=(
            P(("pose", "aux", "orb"), None, "ao"),
            P(("pose", "aux", "orb"), None, "ao"),
            P(None, "orb"),
            P(None, "pose"),
        ),
        out_specs=(P(("pose", "aux", "orb")), P(("pose", "aux", "orb"), "ao", None)),
        check_vma=False,
    )
```

```python
import functools
import math

import jax
import jax.numpy as jnp
from jax import lax
from jax.experimental import pallas as pl
from jax.experimental.pallas import tpu as pltpu
from jax.sharding import PartitionSpec as P

NOCC = 1024
BLK = 128
NBLK = 4
NB = 512
GROUP = 16
MIB = 1024 * 1024
SMEM = pl.BlockSpec(memory_space=pltpu.SMEM)
VMEM = pl.BlockSpec(memory_space=pltpu.VMEM)


def masked_kernel(place, pattern, blocks, occupied, ligand, masked, panel, part, orbitals, held, opened, sems):
    aux_rows, _, nu_width = blocks.shape
    own = occupied.at[pl.ds(pl.multiple_of(place[2] * part.shape[0], part.shape[0]), part.shape[0])]
    moves = ((blocks, held), (pattern, opened), (own, part), (occupied, panel), (ligand, orbitals))
    copies = [pltpu.make_async_copy(source, target, sems.at[k]) for k, (source, target) in enumerate(moves)]
    for copy in copies:
        copy.start()
    copies[0].wait()
    copies[1].wait()
    for q in range(aux_rows):
        for m in range(NBLK):
            for n in range(nu_width // BLK):
                rows, columns = pl.ds(m * BLK, BLK), pl.ds(n * BLK, BLK)
                tile = held[q, rows, columns]
                masked[q, rows, columns] = jnp.where(opened[0, n, m] != 0, tile, jnp.zeros_like(tile))
    for copy in copies[2:]:
        copy.wait()


def slot_of(place, d):
    return (2 * (place[0] & 1) + place[1]) ^ d


def half_into(outs, place, turned, masked):
    for d, out in enumerate(outs):
        rows = turned[slot_of(place, d)]
        for q in range(out.shape[0]):
            out[q] = jnp.dot(rows, masked[q], preferred_element_type=jnp.float32).astype(jnp.bfloat16)


def own_kernel(place, occupied, mine, theirs, masked, turned, *outs):
    ni = turned.shape[1]
    near = place[1] == place[0] // 2

    @pl.when(near)
    def _():
        for s in range(turned.shape[0]):
            turned[s] = occupied[:, s * ni : (s + 1) * ni].T

    @pl.when(jnp.logical_not(near))
    def _():
        depth = mine.shape[0]
        for e, rows in enumerate((mine, theirs)):
            first = pl.multiple_of((place[2] ^ e) * depth, depth)
            for s in range(turned.shape[0]):
                turned[s, :, pl.ds(first, depth)] = rows[:, s * ni : (s + 1) * ni].T

    half_into(outs, place, turned, masked)


def density_kernel(place, occupied, mine, theirs, masked, turned, *refs):
    messages, out, panel = refs[:-2], refs[-2], refs[-1]
    aux_rows, ni, nu_width = messages[0].shape
    depth = mine.shape[0]
    own = pl.ds(pl.multiple_of(place[2] * nu_width, nu_width), nu_width)
    near = place[1] == place[0] // 2

    @pl.when(near)
    def _():
        for e, rows in enumerate((mine, theirs)):
            panel[pl.ds(pl.multiple_of((place[2] ^ e) * depth, depth), depth), :] = rows[...]

    @pl.when(jnp.logical_not(near))
    def _():
        panel[...] = occupied[...]

    totals = [0.0] * aux_rows
    for d, message in enumerate(messages):
        rows = turned[slot_of(place, d), :, own].astype(jnp.float32)
        for q in range(aux_rows):
            totals[q] += jnp.sum(rows * message[q].astype(jnp.float32))
    for s in range(4):
        rows = panel[:, s * ni : (s + 1) * ni].T
        weights = panel[own, s * ni : (s + 1) * ni].T.astype(jnp.float32)
        for q in range(aux_rows):
            result = jnp.dot(rows, masked[q], preferred_element_type=jnp.float32).astype(jnp.bfloat16)
            totals[q] += jnp.sum(weights * result.astype(jnp.float32))
    for q in range(aux_rows):
        out[q : q + 1, :] = jnp.full((1, out.shape[1]), totals[q], jnp.float32)


def far_kernel(place, masked, turned, *outs):
    half_into(outs, place, turned, masked)


def pair_kernel(place, before, earlier, ligand, *refs):
    arrived, own, sent = refs[:-2], refs[-2], refs[-1]
    aux_rows, ni, nu_width = arrived[0].shape
    width = ligand.shape[1]
    rows = ligand[pl.ds(pl.multiple_of(place[2] * nu_width, nu_width), nu_width), :]
    for k, message in enumerate(arrived):
        part = jnp.dot(
            message[...].reshape(aux_rows * ni, nu_width), rows, preferred_element_type=jnp.float32
        ).reshape(aux_rows, ni, width)
        own[k * aux_rows : (k + 1) * aux_rows] = part
        sent[k * aux_rows : (k + 1) * aux_rows] = part.astype(jnp.bfloat16)


def turn_kernel(*refs):
    messages, out = refs[:-1], refs[-1]
    nu_width = messages[0].shape[2]
    for g in range(out.shape[0]):
        here = pl.ds(g * GROUP, GROUP)
        out[g] = jnp.concatenate([x[:, here, :].reshape(-1, nu_width) for x in messages], axis=0).T


def pair_and_turn_kernel(place, before, earlier, ligand, *refs):
    pair_kernel(place, before, earlier, ligand, *refs[:-1])
    turn_kernel(*refs[:-3], refs[-1])


def cross_kernel(scale, near, far, *refs):
    pairs, (out, held, sem) = refs[:4], refs[4:]
    ni, _, width = out.shape

    def step(g, carry):
        here = pl.ds(pl.multiple_of(g * GROUP, GROUP), GROUP)
        turned = jnp.concatenate([near[g], far[g]], axis=1)
        summed = [pairs[j][:, here, :] + pairs[j + 1][:, here, :].astype(jnp.float32) for j in (0, 2)]
        summed = jnp.concatenate([(x * scale).astype(jnp.bfloat16) for x in summed], axis=0)
        row = lax.broadcasted_iota(jnp.int32, (1, GROUP, width), 1)
        zero = jnp.zeros_like(summed)
        for i in range(0, GROUP, 2):
            both = [jnp.where(row == i + e, summed, zero).reshape(-1, width) for e in (0, 1)]
            result = jnp.dot(turned, jnp.concatenate(both, axis=1), preferred_element_type=jnp.float32)
            held[g * GROUP + i] = result[:, :width]
            held[g * GROUP + i + 1] = result[:, width:]
            if i % 4 == 2:
                done = pl.ds(g * GROUP + i - 2, 4)
                pltpu.make_async_copy(held.at[done], out.at[done], sem).start()
        return carry

    lax.fori_loop(0, ni // GROUP, step, 0)
    pltpu.make_async_copy(held, out, sem).wait()


def call(kernel, name, inputs, outputs, scratch=(), limit=16, scalars=1, flops=0, moved=1 << 20, in_spec=VMEM, out_spec=VMEM):
    inputs = list(inputs)
    results = pl.pallas_call(
        kernel,
        in_specs=[SMEM] * scalars + [in_spec] * (len(inputs) - scalars),
        out_specs=[out_spec] * len(outputs),
        out_shape=outputs,
        scratch_shapes=list(scratch),
        compiler_params=pltpu.CompilerParams(vmem_limit_bytes=limit * MIB),
        cost_estimate=pl.CostEstimate(flops=flops, bytes_accessed=moved, transcendentals=0),
        name=name,
    )(*inputs)
    return list(results)


def body(sizes, blocks, pattern, occupied, ligand):
    n_aux, n_orb, n_ao = sizes
    aux_rows, _, nu_width = blocks.shape
    owners = n_aux * n_orb
    ni = NOCC // owners
    q_total = aux_rows * owners
    panel_width = occupied.shape[1]
    width = ligand.shape[1]
    place = jnp.stack([lax.axis_index(name) for name in ("aux", "orb", "ao")]).astype(jnp.int32)
    bf16 = functools.partial(jax.ShapeDtypeStruct, dtype=jnp.bfloat16)
    f32 = functools.partial(jax.ShapeDtypeStruct, dtype=jnp.float32)

    across = [(a, a ^ 2) for a in range(n_aux)]
    swap = [(c, 1 - c) for c in range(n_ao)]
    pattern = jnp.swapaxes(pattern, 1, 2)
    masked, panel, part, orbitals = call(
        masked_kernel,
        "masked_blocks",
        (place, *(pltpu.with_memory_space_constraint(x, pltpu.HBM) for x in (pattern, blocks, occupied, ligand))),
        [bf16(blocks.shape), bf16(occupied.shape), bf16((NB // n_ao, panel_width)), bf16(ligand.shape)],
        [
            pltpu.VMEM(blocks.shape, jnp.bfloat16),
            pltpu.SMEM(pattern.shape, pattern.dtype),
            pltpu.SemaphoreType.DMA((5,)),
        ],
        in_spec=pl.BlockSpec(memory_space=pltpu.HBM),
    )
    far_masked = lax.ppermute(masked, "aux", across)
    mine = lax.ppermute(part, "orb", swap)
    theirs = lax.ppermute(mine, "ao", swap)

    def square(messages):
        arrived = [messages[0]] + [None] * 3
        for d in (3, 2, 1):
            moves = [
                (a * n_orb + o, (a ^ (d >> 1)) * n_orb + (o ^ (d & 1))) for a in range(n_aux) for o in range(n_orb)
            ]
            arrived[d] = lax.ppermute(messages[d], ("aux", "orb"), moves)
        return arrived

    work = 2 * NB * panel_width * nu_width * aux_rows
    messages = [bf16((aux_rows, ni, nu_width))] * 4
    turned, *own = call(
        own_kernel, "own_half", (place, panel, mine, theirs, masked), [bf16((4, ni, NB))] + messages, flops=work
    )
    own_here = square(own)
    value = call(
        density_kernel,
        "density_terms",
        (place, panel, mine, theirs, masked, turned, *own),
        [f32((aux_rows, 128))],
        [pltpu.VMEM(occupied.shape, jnp.bfloat16)],
        flops=work,
    )[0]
    value_there = lax.ppermute(value, "ao", swap)
    density = (value[:, 0] + value_there[:, 0]) / math.sqrt(NOCC)
    far = call(far_kernel, "far_half", (place, far_masked, turned), messages, flops=work)
    far_here = square(far)

    shape = (4 * aux_rows, ni, width)
    kept_and_given = [f32(shape), bf16(shape)]
    side = [bf16((ni // GROUP, nu_width, 4 * aux_rows * GROUP))]
    pair_work = 2 * shape[0] * ni * nu_width * width
    own_kept, own_given, own_rows = call(
        pair_and_turn_kernel,
        "own_pairs",
        (place, value, far[0], orbitals, *own_here),
        kept_and_given + side,
        flops=pair_work,
    )
    own_pairs = (own_kept, lax.ppermute(own_given, "ao", swap))
    far_kept, far_given = call(
        pair_kernel, "far_pairs", (place, value_there, own_pairs[1], orbitals, *far_here), kept_and_given, flops=pair_work
    )
    far_pairs = (far_kept, lax.ppermute(far_given, "ao", swap))
    far_rows = call(turn_kernel, "far_turned", far_here, side, scalars=0)[0]

    result = (ni, nu_width, width)
    cross_terms = call(
        functools.partial(cross_kernel, 1.0 / math.sqrt(q_total)),
        "cross_terms",
        (own_rows, far_rows, *own_pairs, *far_pairs),
        [f32(result)],
        [pltpu.VMEM(result, jnp.float32), pltpu.SemaphoreType.DMA],
        limit=32,
        scalars=0,
        flops=32 * q_total * ni * nu_width * width,
        moved=18 * MIB,
        out_spec=pl.BlockSpec(memory_space=pltpu.HBM),
    )[0]
    return (density, cross_terms)


def plain_body(blocks, pattern, occupied, ligand):
    panels = lax.all_gather(occupied, "orb", axis=1, tiled=True)
    aux_rows = blocks.shape[0]
    nu_width = blocks.shape[2]
    nu_blocks = pattern.shape[2]
    opened = pattern[0].astype(jnp.bfloat16)
    masked = blocks.reshape(aux_rows, NBLK, BLK, nu_blocks, BLK) * opened[None, :, None, :, None]
    masked = masked.reshape(aux_rows, NB, nu_width)
    transformed = jnp.einsum(
        "qmn,mi->qin", masked, panels, preferred_element_type=jnp.float32
    ).astype(jnp.bfloat16)
    nu_start = lax.axis_index("ao") * nu_width
    own_rows = lax.dynamic_slice_in_dim(panels, nu_start, nu_width, 0)
    partial_value = jnp.einsum(
        "qin,ni->q", transformed, own_rows, preferred_element_type=jnp.float32
    )
    density = lax.psum(partial_value, "ao") / math.sqrt(NOCC)
    arrived = lax.all_to_all(transformed, ("aux", "orb"), split_axis=1, concat_axis=0, tiled=True)
    own_ligand = lax.dynamic_slice_in_dim(ligand, nu_start, nu_width, 0)
    pair_part = jnp.einsum("qin,nj->qij", arrived, own_ligand, preferred_element_type=jnp.float32)
    mixed_pairs = lax.psum(pair_part, "ao").astype(jnp.bfloat16)
    crossed = jnp.einsum("qin,qij->inj", arrived, mixed_pairs, preferred_element_type=jnp.float32)
    cross_terms = crossed / math.sqrt(arrived.shape[0])
    return (density, cross_terms)


def solution(mesh):
    sizes = (mesh.shape["aux"], mesh.shape["orb"], mesh.shape["ao"])
    kernels = sizes == (4, 2, 2)
    return jax.shard_map(
        functools.partial(body, sizes) if kernels else plain_body,
        mesh=mesh,
        in_specs=(
            P(("pose", "aux", "orb"), None, "ao"),
            P(("pose", "aux", "orb"), None, "ao"),
            P(None, "orb"),
            P(None, "pose"),
        ),
        out_specs=(P(("pose", "aux", "orb")), P(("pose", "aux", "orb"), "ao", None)),
        check_vma=False,
    )
```

```python
import functools
import math

import jax
import jax.numpy as jnp
from jax import lax
from jax.experimental import pallas as pl
from jax.experimental.pallas import tpu as pltpu
from jax.sharding import PartitionSpec as P

NOCC = 1024
BLK = 128
NBLK = 4
NB = 512
GROUP = 16
MIB = 1024 * 1024
SMEM = pl.BlockSpec(memory_space=pltpu.SMEM)
VMEM = pl.BlockSpec(memory_space=pltpu.VMEM)


def masked_kernel(place, pattern, blocks, occupied, ligand, masked, panel, part, orbitals, held, opened, sems):
    aux_rows, _, nu_width = blocks.shape
    own = occupied.at[pl.ds(pl.multiple_of(place[2] * part.shape[0], part.shape[0]), part.shape[0])]
    moves = ((blocks, held), (pattern, opened), (own, part), (occupied, panel), (ligand, orbitals))
    copies = [pltpu.make_async_copy(source, target, sems.at[k]) for k, (source, target) in enumerate(moves)]
    for copy in copies:
        copy.start()
    copies[0].wait()
    copies[1].wait()
    for q in range(aux_rows):
        for m in range(NBLK):
            for n in range(nu_width // BLK):
                rows, columns = pl.ds(m * BLK, BLK), pl.ds(n * BLK, BLK)
                tile = held[q, rows, columns]
                masked[q, rows, columns] = jnp.where(opened[0, n, m] != 0, tile, jnp.zeros_like(tile))
    for copy in copies[2:]:
        copy.wait()


def slot_of(place, d):
    return (2 * (place[0] & 1) + place[1]) ^ d


def half_into(outs, place, turned, masked):
    for d, out in enumerate(outs):
        rows = turned[slot_of(place, d)]
        for q in range(out.shape[0]):
            out[q] = jnp.dot(rows, masked[q], preferred_element_type=jnp.float32).astype(jnp.bfloat16)


def own_kernel(place, occupied, mine, theirs, masked, turned, *outs):
    ni = turned.shape[1]
    near = place[1] == place[0] // 2

    @pl.when(near)
    def _():
        for s in range(turned.shape[0]):
            turned[s] = occupied[:, s * ni : (s + 1) * ni].T

    @pl.when(jnp.logical_not(near))
    def _():
        depth = mine.shape[0]
        for e, rows in enumerate((mine, theirs)):
            first = pl.multiple_of((place[2] ^ e) * depth, depth)
            for s in range(turned.shape[0]):
                turned[s, :, pl.ds(first, depth)] = rows[:, s * ni : (s + 1) * ni].T

    half_into(outs, place, turned, masked)


def density_kernel(place, occupied, mine, theirs, masked, turned, *refs):
    messages, out, panel = refs[:-2], refs[-2], refs[-1]
    aux_rows, ni, nu_width = messages[0].shape
    depth = mine.shape[0]
    own = pl.ds(pl.multiple_of(place[2] * nu_width, nu_width), nu_width)
    near = place[1] == place[0] // 2

    @pl.when(near)
    def _():
        for e, rows in enumerate((mine, theirs)):
            panel[pl.ds(pl.multiple_of((place[2] ^ e) * depth, depth), depth), :] = rows[...]

    @pl.when(jnp.logical_not(near))
    def _():
        panel[...] = occupied[...]

    totals = [0.0] * aux_rows
    for d, message in enumerate(messages):
        rows = turned[slot_of(place, d), :, own].astype(jnp.float32)
        for q in range(aux_rows):
            totals[q] += jnp.sum(rows * message[q].astype(jnp.float32))
    for s in range(4):
        rows = panel[:, s * ni : (s + 1) * ni].T
        weights = panel[own, s * ni : (s + 1) * ni].T.astype(jnp.float32)
        for q in range(aux_rows):
            result = jnp.dot(rows, masked[q], preferred_element_type=jnp.float32).astype(jnp.bfloat16)
            totals[q] += jnp.sum(weights * result.astype(jnp.float32))
    for q in range(aux_rows):
        out[q : q + 1, :] = jnp.full((1, out.shape[1]), totals[q], jnp.float32)


def far_kernel(place, before, masked, turned, *outs):
    half_into(outs, place, turned, masked)


def pair_kernel(place, before, earlier, ligand, *refs):
    arrived, own, sent = refs[:-2], refs[-2], refs[-1]
    aux_rows, ni, nu_width = arrived[0].shape
    width = ligand.shape[1]
    rows = ligand[pl.ds(pl.multiple_of(place[2] * nu_width, nu_width), nu_width), :]
    for k, message in enumerate(arrived):
        part = jnp.dot(
            message[...].reshape(aux_rows * ni, nu_width), rows, preferred_element_type=jnp.float32
        ).reshape(aux_rows, ni, width)
        own[k * aux_rows : (k + 1) * aux_rows] = part
        sent[k * aux_rows : (k + 1) * aux_rows] = part.astype(jnp.bfloat16)


def turn_kernel(*refs):
    messages, out = refs[:-1], refs[-1]
    nu_width = messages[0].shape[2]
    for g in range(out.shape[0]):
        here = pl.ds(g * GROUP, GROUP)
        out[g] = jnp.concatenate([x[:, here, :].reshape(-1, nu_width) for x in messages], axis=0).T


def pair_and_turn_kernel(place, before, earlier, ligand, *refs):
    pair_kernel(place, before, earlier, ligand, *refs[:-1])
    turn_kernel(*refs[:-3], refs[-1])


def cross_kernel(scale, near, far, *refs):
    pairs, (out, held, sem) = refs[:4], refs[4:]
    ni, _, width = out.shape

    def step(g, carry):
        here = pl.ds(pl.multiple_of(g * GROUP, GROUP), GROUP)
        turned = jnp.concatenate([near[g], far[g]], axis=1)
        summed = [pairs[j][:, here, :] + pairs[j + 1][:, here, :].astype(jnp.float32) for j in (0, 2)]
        summed = jnp.concatenate([(x * scale).astype(jnp.bfloat16) for x in summed], axis=0)
        row = lax.broadcasted_iota(jnp.int32, (1, GROUP, width), 1)
        zero = jnp.zeros_like(summed)
        for i in range(0, GROUP, 2):
            both = [jnp.where(row == i + e, summed, zero).reshape(-1, width) for e in (0, 1)]
            result = jnp.dot(turned, jnp.concatenate(both, axis=1), preferred_element_type=jnp.float32)
            held[g * GROUP + i] = result[:, :width]
            held[g * GROUP + i + 1] = result[:, width:]
            if i % 4 == 2:
                done = pl.ds(g * GROUP + i - 2, 4)
                pltpu.make_async_copy(held.at[done], out.at[done], sem).start()
        return carry

    lax.fori_loop(0, ni // GROUP, step, 0)
    pltpu.make_async_copy(held, out, sem).wait()


def call(kernel, name, inputs, outputs, scratch=(), limit=16, scalars=1, flops=0, moved=1 << 20, in_spec=VMEM, out_spec=VMEM):
    inputs = list(inputs)
    results = pl.pallas_call(
        kernel,
        in_specs=[SMEM] * scalars + [in_spec] * (len(inputs) - scalars),
        out_specs=[out_spec] * len(outputs),
        out_shape=outputs,
        scratch_shapes=list(scratch),
        compiler_params=pltpu.CompilerParams(vmem_limit_bytes=limit * MIB),
        cost_estimate=pl.CostEstimate(flops=flops, bytes_accessed=moved, transcendentals=0),
        name=name,
    )(*inputs)
    return list(results)


def body(sizes, blocks, pattern, occupied, ligand):
    n_aux, n_orb, n_ao = sizes
    aux_rows, _, nu_width = blocks.shape
    owners = n_aux * n_orb
    ni = NOCC // owners
    q_total = aux_rows * owners
    panel_width = occupied.shape[1]
    width = ligand.shape[1]
    place = jnp.stack([lax.axis_index(name) for name in ("aux", "orb", "ao")]).astype(jnp.int32)
    bf16 = functools.partial(jax.ShapeDtypeStruct, dtype=jnp.bfloat16)
    f32 = functools.partial(jax.ShapeDtypeStruct, dtype=jnp.float32)

    across = [(a, a ^ 2) for a in range(n_aux)]
    swap = [(c, 1 - c) for c in range(n_ao)]
    pattern = jnp.swapaxes(pattern, 1, 2)
    masked, panel, part, orbitals = call(
        masked_kernel,
        "masked_blocks",
        (place, *(pltpu.with_memory_space_constraint(x, pltpu.HBM) for x in (pattern, blocks, occupied, ligand))),
        [bf16(blocks.shape), bf16(occupied.shape), bf16((NB // n_ao, panel_width)), bf16(ligand.shape)],
        [
            pltpu.VMEM(blocks.shape, jnp.bfloat16),
            pltpu.SMEM(pattern.shape, pattern.dtype),
            pltpu.SemaphoreType.DMA((5,)),
        ],
        in_spec=pl.BlockSpec(memory_space=pltpu.HBM),
    )
    far_masked = lax.ppermute(masked, "aux", across)
    mine = lax.ppermute(part, "orb", swap)
    theirs = lax.ppermute(mine, "ao", swap)

    def square(messages):
        arrived = [messages[0]] + [None] * 3
        for d in (3, 2, 1):
            moves = [
                (a * n_orb + o, (a ^ (d >> 1)) * n_orb + (o ^ (d & 1))) for a in range(n_aux) for o in range(n_orb)
            ]
            arrived[d] = lax.ppermute(messages[d], ("aux", "orb"), moves)
        return arrived

    work = 2 * NB * panel_width * nu_width * aux_rows
    messages = [bf16((aux_rows, ni, nu_width))] * 4
    turned, *own = call(
        own_kernel, "own_half", (place, panel, mine, theirs, masked), [bf16((4, ni, NB))] + messages, flops=work
    )
    own_here = square(own)
    value = call(
        density_kernel,
        "density_terms",
        (place, panel, mine, theirs, masked, turned, *own),
        [f32((aux_rows, 128))],
        [pltpu.VMEM(occupied.shape, jnp.bfloat16)],
        flops=work,
    )[0]
    value_there = lax.ppermute(value, "ao", swap)
    density = (value[:, 0] + value_there[:, 0]) / math.sqrt(NOCC)
    far = call(far_kernel, "far_half", (place, value, far_masked, turned), messages, flops=work)
    far_here = square(far)

    shape = (4 * aux_rows, ni, width)
    kept_and_given = [f32(shape), bf16(shape)]
    side = [bf16((ni // GROUP, nu_width, 4 * aux_rows * GROUP))]
    pair_work = 2 * shape[0] * ni * nu_width * width
    own_kept, own_given, own_rows = call(
        pair_and_turn_kernel,
        "own_pairs",
        (place, value_there, far[0], orbitals, *own_here),
        kept_and_given + side,
        flops=pair_work,
    )
    own_pairs = (own_kept, lax.ppermute(own_given, "ao", swap))
    far_kept, far_given = call(
        pair_kernel, "far_pairs", (place, value_there, own_rows, orbitals, *far_here), kept_and_given, flops=pair_work
    )
    far_pairs = (far_kept, lax.ppermute(far_given, "ao", swap))
    far_rows = call(turn_kernel, "far_turned", far_here, side, scalars=0)[0]

    result = (ni, nu_width, width)
    cross_terms = call(
        functools.partial(cross_kernel, 1.0 / math.sqrt(q_total)),
        "cross_terms",
        (own_rows, far_rows, *own_pairs, *far_pairs),
        [f32(result)],
        [pltpu.VMEM(result, jnp.float32), pltpu.SemaphoreType.DMA],
        limit=32,
        scalars=0,
        flops=32 * q_total * ni * nu_width * width,
        moved=18 * MIB,
        out_spec=pl.BlockSpec(memory_space=pltpu.HBM),
    )[0]
    return (density, cross_terms)


def plain_body(blocks, pattern, occupied, ligand):
    panels = lax.all_gather(occupied, "orb", axis=1, tiled=True)
    aux_rows = blocks.shape[0]
    nu_width = blocks.shape[2]
    nu_blocks = pattern.shape[2]
    opened = pattern[0].astype(jnp.bfloat16)
    masked = blocks.reshape(aux_rows, NBLK, BLK, nu_blocks, BLK) * opened[None, :, None, :, None]
    masked = masked.reshape(aux_rows, NB, nu_width)
    transformed = jnp.einsum(
        "qmn,mi->qin", masked, panels, preferred_element_type=jnp.float32
    ).astype(jnp.bfloat16)
    nu_start = lax.axis_index("ao") * nu_width
    own_rows = lax.dynamic_slice_in_dim(panels, nu_start, nu_width, 0)
    partial_value = jnp.einsum(
        "qin,ni->q", transformed, own_rows, preferred_element_type=jnp.float32
    )
    density = lax.psum(partial_value, "ao") / math.sqrt(NOCC)
    arrived = lax.all_to_all(transformed, ("aux", "orb"), split_axis=1, concat_axis=0, tiled=True)
    own_ligand = lax.dynamic_slice_in_dim(ligand, nu_start, nu_width, 0)
    pair_part = jnp.einsum("qin,nj->qij", arrived, own_ligand, preferred_element_type=jnp.float32)
    mixed_pairs = lax.psum(pair_part, "ao").astype(jnp.bfloat16)
    crossed = jnp.einsum("qin,qij->inj", arrived, mixed_pairs, preferred_element_type=jnp.float32)
    cross_terms = crossed / math.sqrt(arrived.shape[0])
    return (density, cross_terms)


def solution(mesh):
    sizes = (mesh.shape["aux"], mesh.shape["orb"], mesh.shape["ao"])
    kernels = sizes == (4, 2, 2)
    return jax.shard_map(
        functools.partial(body, sizes) if kernels else plain_body,
        mesh=mesh,
        in_specs=(
            P(("pose", "aux", "orb"), None, "ao"),
            P(("pose", "aux", "orb"), None, "ao"),
            P(None, "orb"),
            P(None, "pose"),
        ),
        out_specs=(P(("pose", "aux", "orb")), P(("pose", "aux", "orb"), "ao", None)),
        check_vma=False,
    )
```

```python
import functools
import math

import jax
import jax.numpy as jnp
from jax import lax
from jax.experimental import pallas as pl
from jax.experimental.pallas import tpu as pltpu
from jax.sharding import PartitionSpec as P

NOCC = 1024
BLK = 128
NBLK = 4
NB = 512
GROUP = 16
MIB = 1024 * 1024
SMEM = pl.BlockSpec(memory_space=pltpu.SMEM)
VMEM = pl.BlockSpec(memory_space=pltpu.VMEM)


def masked_kernel(pattern, blocks, occupied, ligand, masked, panel, orbitals, *refs):
    copies_out, (held, opened, sems) = refs[:-3], refs[-3:]
    aux_rows, _, nu_width = blocks.shape
    moves = ((blocks, held), (pattern, opened), (occupied, panel), (ligand, orbitals))
    copies = [pltpu.make_async_copy(source, target, sems.at[k]) for k, (source, target) in enumerate(moves)]
    for copy in copies:
        copy.start()
    copies[0].wait()
    copies[1].wait()
    for q in range(aux_rows):
        for m in range(NBLK):
            for n in range(nu_width // BLK):
                rows, columns = pl.ds(m * BLK, BLK), pl.ds(n * BLK, BLK)
                tile = held[q, rows, columns]
                tile = jnp.where(opened[0, n, m] != 0, tile, jnp.zeros_like(tile))
                masked[q, rows, columns] = tile
                copies_out[q][0, rows, columns] = tile
    for copy in copies[2:]:
        copy.wait()


def after_kernel(block, before, out):
    pass


def slot_of(place, d):
    return (2 * (place[0] & 1) + place[1]) ^ d


def half_into(outs, place, turned, parts):
    for d, out in enumerate(outs):
        rows = turned[slot_of(place, d)]
        for q, (source, index) in enumerate(parts):
            out[q] = jnp.dot(rows, source[index], preferred_element_type=jnp.float32).astype(jnp.bfloat16)


def near_kernel(place, occupied, other, masked, far, turned, *outs):
    ni = turned.shape[1]
    near = place[1] == place[0] // 2

    def turn(panel):
        for s in range(turned.shape[0]):
            turned[s] = panel[:, s * ni : (s + 1) * ni].T

    pl.when(near)(functools.partial(turn, occupied))
    pl.when(jnp.logical_not(near))(functools.partial(turn, other))
    half_into(outs, place, turned, [(masked, q) for q in range(masked.shape[0])] + [(far, 0)])


def density_kernel(place, occupied, other, masked, turned, *refs):
    messages, out = refs[:-1], refs[-1]
    aux_rows = masked.shape[0]
    _, ni, nu_width = messages[0].shape
    own = pl.ds(pl.multiple_of(place[2] * nu_width, nu_width), nu_width)
    near = place[1] == place[0] // 2

    def near_terms(q):
        total = 0.0
        for d in range(4):
            rows = turned[slot_of(place, d), :, own].astype(jnp.float32)
            total += jnp.sum(rows * messages[d][q].astype(jnp.float32))
        return total

    def far_terms(panel):
        totals = [near_terms(q) for q in range(aux_rows)]
        for s in range(4):
            rows = panel[:, s * ni : (s + 1) * ni].T
            weights = panel[own, s * ni : (s + 1) * ni].T.astype(jnp.float32)
            for q in range(aux_rows):
                result = jnp.dot(rows, masked[q], preferred_element_type=jnp.float32).astype(jnp.bfloat16)
                totals[q] += jnp.sum(weights * result.astype(jnp.float32))
        for q in range(aux_rows):
            out[q : q + 1, :] = jnp.full((1, out.shape[1]), totals[q], jnp.float32)

    pl.when(near)(functools.partial(far_terms, other))
    pl.when(jnp.logical_not(near))(functools.partial(far_terms, occupied))


def last_kernel(place, before, far, turned, *outs):
    half_into(outs, place, turned, [(far, 0)])


def pair_kernel(place, before, ligand, *refs):
    arrived, own, sent = refs[:-2], refs[-2], refs[-1]
    aux_rows, ni, nu_width = arrived[0].shape
    width = ligand.shape[1]
    rows = ligand[pl.ds(pl.multiple_of(place[2] * nu_width, nu_width), nu_width), :]
    for k, message in enumerate(arrived):
        part = jnp.dot(
            message[...].reshape(aux_rows * ni, nu_width), rows, preferred_element_type=jnp.float32
        ).reshape(aux_rows, ni, width)
        own[k * aux_rows : (k + 1) * aux_rows] = part
        sent[k * aux_rows : (k + 1) * aux_rows] = part.astype(jnp.bfloat16)


def last_pair_kernel(place, before, near_sent, ligand, *refs):
    sent = refs[-1]
    near = near_sent.shape[0]
    sent[:near] = near_sent[...]
    pair_kernel(place, before, ligand, *refs[:-1], sent.at[near:])


def turn_kernel(*refs):
    messages, out = refs[:-1], refs[-1]
    nu_width = messages[0].shape[2]
    for g in range(out.shape[0]):
        here = pl.ds(g * GROUP, GROUP)
        out[g] = jnp.concatenate([x[:, here, :].reshape(-1, nu_width) for x in messages], axis=0).T


def cross_kernel(scale, turned, *refs):
    own, other, (out, held, sem) = refs[:-4], refs[-4], refs[-3:]
    ni, _, width = out.shape

    def step(g, carry):
        here = pl.ds(pl.multiple_of(g * GROUP, GROUP), GROUP)
        summed = jnp.concatenate([x[:, here, :] for x in own], axis=0) + other[:, here, :].astype(jnp.float32)
        summed = (summed * scale).astype(jnp.bfloat16)
        row = lax.broadcasted_iota(jnp.int32, (1, GROUP, width), 1)
        zero = jnp.zeros_like(summed)
        for i in range(0, GROUP, 2):
            both = [jnp.where(row == i + e, summed, zero).reshape(-1, width) for e in (0, 1)]
            result = jnp.dot(turned[g], jnp.concatenate(both, axis=1), preferred_element_type=jnp.float32)
            held[g * GROUP + i] = result[:, :width]
            held[g * GROUP + i + 1] = result[:, width:]
            if i % 4 == 2:
                done = pl.ds(g * GROUP + i - 2, 4)
                pltpu.make_async_copy(held.at[done], out.at[done], sem).start()
        return carry

    lax.fori_loop(0, ni // GROUP, step, 0)
    pltpu.make_async_copy(held, out, sem).wait()


def call(kernel, name, inputs, outputs, scratch=(), limit=16, scalars=1, flops=0, moved=1 << 20, in_spec=VMEM, out_spec=VMEM, aliases=None):
    inputs = list(inputs)
    results = pl.pallas_call(
        kernel,
        in_specs=[SMEM] * scalars + [in_spec] * (len(inputs) - scalars),
        out_specs=[out_spec] * len(outputs),
        out_shape=outputs,
        scratch_shapes=list(scratch),
        compiler_params=pltpu.CompilerParams(vmem_limit_bytes=limit * MIB),
        cost_estimate=pl.CostEstimate(flops=flops, bytes_accessed=moved, transcendentals=0),
        input_output_aliases=aliases or {},
        name=name,
    )(*inputs)
    return list(results)


def body(sizes, blocks, pattern, occupied, ligand):
    n_aux, n_orb, n_ao = sizes
    aux_rows, _, nu_width = blocks.shape
    owners = n_aux * n_orb
    ni = NOCC // owners
    q_total = aux_rows * owners
    panel_width = occupied.shape[1]
    width = ligand.shape[1]
    place = jnp.stack([lax.axis_index(name) for name in ("aux", "orb", "ao")]).astype(jnp.int32)
    bf16 = functools.partial(jax.ShapeDtypeStruct, dtype=jnp.bfloat16)
    f32 = functools.partial(jax.ShapeDtypeStruct, dtype=jnp.float32)

    across = [(a, a ^ 2) for a in range(n_aux)]
    swap = [(c, 1 - c) for c in range(n_ao)]
    pattern = jnp.swapaxes(pattern, 1, 2)
    block = bf16((1, NB, nu_width))
    masked, panel, orbitals, *parts = call(
        masked_kernel,
        "masked_blocks",
        (pltpu.with_memory_space_constraint(x, pltpu.HBM) for x in (pattern, blocks, occupied, ligand)),
        [bf16(blocks.shape), bf16(occupied.shape), bf16(ligand.shape)] + [block] * aux_rows,
        [
            pltpu.VMEM(blocks.shape, jnp.bfloat16),
            pltpu.SMEM(pattern.shape, pattern.dtype),
            pltpu.SemaphoreType.DMA((4,)),
        ],
        scalars=0,
        in_spec=pl.BlockSpec(memory_space=pltpu.HBM),
    )
    other = lax.ppermute(panel, "orb", swap)
    far = [lax.ppermute(parts[0], "aux", across)]
    anywhere = pl.BlockSpec(memory_space=pl.ANY)
    follower = call(
        after_kernel,
        "second_block",
        (parts[1], far[0]),
        [block],
        scalars=0,
        in_spec=anywhere,
        out_spec=anywhere,
        aliases={0: 0},
    )[0]
    far.append(lax.ppermute(follower, "aux", across))

    def square(messages):
        arrived = [messages[0]] + [None] * 3
        for d in (3, 2, 1):
            moves = [
                (a * n_orb + o, (a ^ (d >> 1)) * n_orb + (o ^ (d & 1))) for a in range(n_aux) for o in range(n_orb)
            ]
            arrived[d] = lax.ppermute(messages[d], ("aux", "orb"), moves)
        return arrived

    work = 2 * NB * panel_width * nu_width
    turned, *near = call(
        near_kernel,
        "near_rows",
        (place, panel, other, masked, far[0]),
        [bf16((4, ni, NB))] + [bf16((aux_rows + 1, ni, nu_width))] * 4,
        flops=work * (aux_rows + 1),
    )
    near_here = square(near)
    value = call(
        density_kernel,
        "density_terms",
        (place, panel, other, masked, turned, *near),
        [f32((aux_rows, 128))],
        flops=work,
    )[0]
    value_there = lax.ppermute(value, "ao", swap)
    density = (value[:, 0] + value_there[:, 0]) / math.sqrt(NOCC)
    last = call(last_kernel, "last_rows", (place, value, far[1], turned), [bf16((1, ni, nu_width))] * 4, flops=work)
    last_here = square(last)

    n_near, n_last = (4 * group[0].shape[0] for group in (near_here, last_here))
    near_own, near_given = call(
        pair_kernel,
        "near_pairs",
        (place, last[0], orbitals, *near_here),
        [f32((n_near, ni, width)), bf16((n_near, ni, width))],
        flops=2 * n_near * ni * nu_width * width,
    )
    last_own, given = call(
        last_pair_kernel,
        "last_pairs",
        (place, value_there, near_given, orbitals, *last_here),
        [f32((n_last, ni, width)), bf16((q_total, ni, width))],
        flops=2 * n_last * ni * nu_width * width,
    )
    pairs = (near_own, last_own, lax.ppermute(given, "ao", swap))
    columns = call(
        turn_kernel, "turned", near_here + last_here, [bf16((ni // GROUP, nu_width, q_total * GROUP))], scalars=0
    )[0]

    result = (ni, nu_width, width)
    cross_terms = call(
        functools.partial(cross_kernel, 1.0 / math.sqrt(q_total)),
        "cross_terms",
        (columns, *pairs),
        [f32(result)],
        [pltpu.VMEM(result, jnp.float32), pltpu.SemaphoreType.DMA],
        limit=32,
        scalars=0,
        flops=32 * q_total * ni * nu_width * width,
        moved=18 * MIB,
        out_spec=pl.BlockSpec(memory_space=pltpu.HBM),
    )[0]
    return (density, cross_terms)


def plain_body(blocks, pattern, occupied, ligand):
    panels = lax.all_gather(occupied, "orb", axis=1, tiled=True)
    aux_rows = blocks.shape[0]
    nu_width = blocks.shape[2]
    nu_blocks = pattern.shape[2]
    opened = pattern[0].astype(jnp.bfloat16)
    masked = blocks.reshape(aux_rows, NBLK, BLK, nu_blocks, BLK) * opened[None, :, None, :, None]
    masked = masked.reshape(aux_rows, NB, nu_width)
    transformed = jnp.einsum(
        "qmn,mi->qin", masked, panels, preferred_element_type=jnp.float32
    ).astype(jnp.bfloat16)
    nu_start = lax.axis_index("ao") * nu_width
    own_rows = lax.dynamic_slice_in_dim(panels, nu_start, nu_width, 0)
    partial_value = jnp.einsum(
        "qin,ni->q", transformed, own_rows, preferred_element_type=jnp.float32
    )
    density = lax.psum(partial_value, "ao") / math.sqrt(NOCC)
    arrived = lax.all_to_all(transformed, ("aux", "orb"), split_axis=1, concat_axis=0, tiled=True)
    own_ligand = lax.dynamic_slice_in_dim(ligand, nu_start, nu_width, 0)
    pair_part = jnp.einsum("qin,nj->qij", arrived, own_ligand, preferred_element_type=jnp.float32)
    mixed_pairs = lax.psum(pair_part, "ao").astype(jnp.bfloat16)
    crossed = jnp.einsum("qin,qij->inj", arrived, mixed_pairs, preferred_element_type=jnp.float32)
    cross_terms = crossed / math.sqrt(arrived.shape[0])
    return (density, cross_terms)


def solution(mesh):
    sizes = (mesh.shape["aux"], mesh.shape["orb"], mesh.shape["ao"])
    kernels = sizes == (4, 2, 2)
    return jax.shard_map(
        functools.partial(body, sizes) if kernels else plain_body,
        mesh=mesh,
        in_specs=(
            P(("pose", "aux", "orb"), None, "ao"),
            P(("pose", "aux", "orb"), None, "ao"),
            P(None, "orb"),
            P(None, "pose"),
        ),
        out_specs=(P(("pose", "aux", "orb")), P(("pose", "aux", "orb"), "ao", None)),
        check_vma=False,
    )
```

```python
import functools
import math

import jax
import jax.numpy as jnp
from jax import lax
from jax.experimental import pallas as pl
from jax.experimental.pallas import tpu as pltpu
from jax.sharding import PartitionSpec as P

NOCC = 1024
BLK = 128
NBLK = 4
NB = 512
GROUP = 16
MIB = 1024 * 1024
VMEM = pl.BlockSpec(memory_space=pltpu.VMEM)


def masked_kernel(pattern, blocks, occupied, ligand, masked, panel, part, orbitals, held, opened, sems):
    aux_rows, _, nu_width = blocks.shape
    own = own_half_of(part.shape[0])
    moves = ((blocks, held), (pattern, opened), (occupied.at[own], part), (occupied, panel), (ligand.at[own], orbitals))
    copies = [pltpu.make_async_copy(source, target, sems.at[k]) for k, (source, target) in enumerate(moves)]
    for copy in copies:
        copy.start()
    copies[0].wait()
    copies[1].wait()
    for q in range(aux_rows):
        for m in range(NBLK):
            for n in range(nu_width // BLK):
                rows, columns = pl.ds(m * BLK, BLK), pl.ds(n * BLK, BLK)
                tile = held[q, rows, columns]
                masked[q, rows, columns] = jnp.where(opened[0, n, m] != 0, tile, jnp.zeros_like(tile))
    for copy in copies[2:]:
        copy.wait()


def own_half_of(length):
    return pl.ds(pl.multiple_of(lax.axis_index("ao") * length, length), length)


def half_into(outs, turned, masked):
    for d, out in enumerate(outs):
        for q in range(out.shape[0]):
            out[q] = jnp.dot(turned[d], masked[q], preferred_element_type=jnp.float32).astype(jnp.bfloat16)


def own_kernel(occupied, mine, theirs, masked, turned, *outs):
    aux, orb, ao = (lax.axis_index(name) for name in ("aux", "orb", "ao"))
    ni = turned.shape[1]
    here = 2 * (aux & 1) + orb
    near = orb == aux // 2

    @pl.when(near)
    def _():
        for s in range(turned.shape[0]):
            turned[here ^ s] = occupied[:, s * ni : (s + 1) * ni].T

    @pl.when(jnp.logical_not(near))
    def _():
        depth = mine.shape[0]
        for e, rows in enumerate((mine, theirs)):
            first = pl.multiple_of((ao ^ e) * depth, depth)
            for s in range(turned.shape[0]):
                turned[here ^ s, :, pl.ds(first, depth)] = rows[:, s * ni : (s + 1) * ni].T

    half_into(outs, turned, masked)


def density_kernel(occupied, mine, theirs, masked, turned, *refs):
    messages, out, panel = refs[:-2], refs[-2], refs[-1]
    aux_rows, ni, nu_width = messages[0].shape
    depth = mine.shape[0]
    own = own_half_of(nu_width)
    near = lax.axis_index("orb") == lax.axis_index("aux") // 2

    @pl.when(near)
    def _():
        for e, rows in enumerate((mine, theirs)):
            panel[pl.ds(pl.multiple_of((lax.axis_index("ao") ^ e) * depth, depth), depth), :] = rows[...]

    @pl.when(jnp.logical_not(near))
    def _():
        panel[...] = occupied[...]

    totals = [0.0] * aux_rows
    for d, message in enumerate(messages):
        rows = turned[d, :, own].astype(jnp.float32)
        for q in range(aux_rows):
            totals[q] += jnp.sum(rows * message[q].astype(jnp.float32))
    for s in range(4):
        rows = panel[:, s * ni : (s + 1) * ni].T
        weights = panel[own, s * ni : (s + 1) * ni].T.astype(jnp.float32)
        for q in range(aux_rows):
            result = jnp.dot(rows, masked[q], preferred_element_type=jnp.float32).astype(jnp.bfloat16)
            totals[q] += jnp.sum(weights * result.astype(jnp.float32))
    for q in range(aux_rows):
        out[q : q + 1, :] = jnp.full((1, out.shape[1]), totals[q], jnp.float32)


def far_kernel(before, masked, turned, *outs):
    half_into(outs, turned, masked)


def pair_kernel(before, earlier, ligand, *refs):
    arrived, own, sent = refs[:-2], refs[-2], refs[-1]
    aux_rows, ni, nu_width = arrived[0].shape
    width = ligand.shape[1]
    for k, message in enumerate(arrived):
        part = jnp.dot(
            message[...].reshape(aux_rows * ni, nu_width), ligand[...], preferred_element_type=jnp.float32
        ).reshape(aux_rows, ni, width)
        own[k * aux_rows : (k + 1) * aux_rows] = part
        sent[k * aux_rows : (k + 1) * aux_rows] = part.astype(jnp.bfloat16)


def turn_kernel(*refs):
    messages, out = refs[:-1], refs[-1]
    nu_width = messages[0].shape[2]
    for g in range(out.shape[0]):
        here = pl.ds(g * GROUP, GROUP)
        out[g] = jnp.concatenate([x[:, here, :].reshape(-1, nu_width) for x in messages], axis=0).T


def pair_and_turn_kernel(before, earlier, ligand, *refs):
    pair_kernel(before, earlier, ligand, *refs[:-1])
    turn_kernel(*refs[:-3], refs[-1])


def cross_kernel(scale, near, far, *refs):
    pairs, (out, held, sem) = refs[:4], refs[4:]
    ni, _, width = out.shape

    def step(g, carry):
        here = pl.ds(pl.multiple_of(g * GROUP, GROUP), GROUP)
        turned = jnp.concatenate([near[g], far[g]], axis=1)
        summed = [pairs[j][:, here, :] + pairs[j + 1][:, here, :].astype(jnp.float32) for j in (0, 2)]
        summed = jnp.concatenate([(x * scale).astype(jnp.bfloat16) for x in summed], axis=0)
        row = lax.broadcasted_iota(jnp.int32, (1, GROUP, width), 1)
        zero = jnp.zeros_like(summed)
        for i in range(0, GROUP, 2):
            both = [jnp.where(row == i + e, summed, zero).reshape(-1, width) for e in (0, 1)]
            result = jnp.dot(turned, jnp.concatenate(both, axis=1), preferred_element_type=jnp.float32)
            held[g * GROUP + i] = result[:, :width]
            held[g * GROUP + i + 1] = result[:, width:]
            if i % 4 == 2:
                done = pl.ds(g * GROUP + i - 2, 4)
                pltpu.make_async_copy(held.at[done], out.at[done], sem).start()
        return carry

    lax.fori_loop(0, ni // GROUP, step, 0)
    pltpu.make_async_copy(held, out, sem).wait()


def call(kernel, name, inputs, outputs, scratch=(), limit=16, flops=0, moved=1 << 20, in_spec=VMEM, out_spec=VMEM):
    inputs = list(inputs)
    results = pl.pallas_call(
        kernel,
        in_specs=[in_spec] * len(inputs),
        out_specs=[out_spec] * len(outputs),
        out_shape=outputs,
        scratch_shapes=list(scratch),
        compiler_params=pltpu.CompilerParams(vmem_limit_bytes=limit * MIB),
        cost_estimate=pl.CostEstimate(flops=flops, bytes_accessed=moved, transcendentals=0),
        name=name,
    )(*inputs)
    return list(results)


def body(sizes, blocks, pattern, occupied, ligand):
    n_aux, n_orb, n_ao = sizes
    aux_rows, _, nu_width = blocks.shape
    owners = n_aux * n_orb
    ni = NOCC // owners
    q_total = aux_rows * owners
    panel_width = occupied.shape[1]
    width = ligand.shape[1]
    bf16 = functools.partial(jax.ShapeDtypeStruct, dtype=jnp.bfloat16)
    f32 = functools.partial(jax.ShapeDtypeStruct, dtype=jnp.float32)

    across = [(a, a ^ 2) for a in range(n_aux)]
    swap = [(c, 1 - c) for c in range(n_ao)]
    pattern = jnp.swapaxes(pattern, 1, 2)
    masked, panel, part, orbitals = call(
        masked_kernel,
        "masked_blocks",
        (pltpu.with_memory_space_constraint(x, pltpu.HBM) for x in (pattern, blocks, occupied, ligand)),
        [bf16(blocks.shape), bf16(occupied.shape), bf16((NB // n_ao, panel_width)), bf16((NB // n_ao, width))],
        [
            pltpu.VMEM(blocks.shape, jnp.bfloat16),
            pltpu.SMEM(pattern.shape, pattern.dtype),
            pltpu.SemaphoreType.DMA((5,)),
        ],
        in_spec=pl.BlockSpec(memory_space=pltpu.HBM),
    )
    far_masked = lax.ppermute(masked, "aux", across)
    mine = lax.ppermute(part, "orb", swap)
    theirs = lax.ppermute(mine, "ao", swap)

    def square(messages):
        arrived = [messages[0]] + [None] * 3
        for d in (3, 2, 1):
            moves = [
                (a * n_orb + o, (a ^ (d >> 1)) * n_orb + (o ^ (d & 1))) for a in range(n_aux) for o in range(n_orb)
            ]
            arrived[d] = lax.ppermute(messages[d], ("aux", "orb"), moves)
        return arrived

    work = 2 * NB * panel_width * nu_width * aux_rows
    messages = [bf16((aux_rows, ni, nu_width))] * 4
    turned, *own = call(
        own_kernel, "own_half", (panel, mine, theirs, masked), [bf16((4, ni, NB))] + messages, flops=work
    )
    own_here = square(own)
    value = call(
        density_kernel,
        "density_terms",
        (panel, mine, theirs, masked, turned, *own),
        [f32((aux_rows, 128))],
        [pltpu.VMEM(occupied.shape, jnp.bfloat16)],
        flops=work,
    )[0]
    value_there = lax.ppermute(value, "ao", swap)
    density = (value[:, 0] + value_there[:, 0]) / math.sqrt(NOCC)
    far = call(far_kernel, "far_half", (value, far_masked, turned), messages, flops=work)
    far_here = square(far)

    shape = (4 * aux_rows, ni, width)
    kept_and_given = [f32(shape), bf16(shape)]
    side = [bf16((ni // GROUP, nu_width, 4 * aux_rows * GROUP))]
    pair_work = 2 * shape[0] * ni * nu_width * width
    own_kept, own_given, own_rows = call(
        pair_and_turn_kernel,
        "own_pairs",
        (value_there, far[0], orbitals, *own_here),
        kept_and_given + side,
        flops=pair_work,
    )
    own_pairs = (own_kept, lax.ppermute(own_given, "ao", swap))
    far_kept, far_given = call(
        pair_kernel, "far_pairs", (value_there, own_rows, orbitals, *far_here), kept_and_given, flops=pair_work
    )
    far_pairs = (far_kept, lax.ppermute(far_given, "ao", swap))
    far_rows = call(turn_kernel, "far_turned", far_here, side)[0]

    result = (ni, nu_width, width)
    cross_terms = call(
        functools.partial(cross_kernel, 1.0 / math.sqrt(q_total)),
        "cross_terms",
        (own_rows, far_rows, *own_pairs, *far_pairs),
        [f32(result)],
        [pltpu.VMEM(result, jnp.float32), pltpu.SemaphoreType.DMA],
        limit=32,
        flops=32 * q_total * ni * nu_width * width,
        moved=18 * MIB,
        out_spec=pl.BlockSpec(memory_space=pltpu.HBM),
    )[0]
    return (density, cross_terms)


def plain_body(blocks, pattern, occupied, ligand):
    panels = lax.all_gather(occupied, "orb", axis=1, tiled=True)
    aux_rows = blocks.shape[0]
    nu_width = blocks.shape[2]
    nu_blocks = pattern.shape[2]
    opened = pattern[0].astype(jnp.bfloat16)
    masked = blocks.reshape(aux_rows, NBLK, BLK, nu_blocks, BLK) * opened[None, :, None, :, None]
    masked = masked.reshape(aux_rows, NB, nu_width)
    transformed = jnp.einsum(
        "qmn,mi->qin", masked, panels, preferred_element_type=jnp.float32
    ).astype(jnp.bfloat16)
    nu_start = lax.axis_index("ao") * nu_width
    own_rows = lax.dynamic_slice_in_dim(panels, nu_start, nu_width, 0)
    partial_value = jnp.einsum(
        "qin,ni->q", transformed, own_rows, preferred_element_type=jnp.float32
    )
    density = lax.psum(partial_value, "ao") / math.sqrt(NOCC)
    arrived = lax.all_to_all(transformed, ("aux", "orb"), split_axis=1, concat_axis=0, tiled=True)
    own_ligand = lax.dynamic_slice_in_dim(ligand, nu_start, nu_width, 0)
    pair_part = jnp.einsum("qin,nj->qij", arrived, own_ligand, preferred_element_type=jnp.float32)
    mixed_pairs = lax.psum(pair_part, "ao").astype(jnp.bfloat16)
    crossed = jnp.einsum("qin,qij->inj", arrived, mixed_pairs, preferred_element_type=jnp.float32)
    cross_terms = crossed / math.sqrt(arrived.shape[0])
    return (density, cross_terms)


def solution(mesh):
    sizes = (mesh.shape["aux"], mesh.shape["orb"], mesh.shape["ao"])
    kernels = sizes == (4, 2, 2)
    return jax.shard_map(
        functools.partial(body, sizes) if kernels else plain_body,
        mesh=mesh,
        in_specs=(
            P(("pose", "aux", "orb"), None, "ao"),
            P(("pose", "aux", "orb"), None, "ao"),
            P(None, "orb"),
            P(None, "pose"),
        ),
        out_specs=(P(("pose", "aux", "orb")), P(("pose", "aux", "orb"), "ao", None)),
        check_vma=False,
    )
```

```python
import functools
import math

import jax
import jax.numpy as jnp
from jax import lax
from jax.experimental import pallas as pl
from jax.experimental.pallas import tpu as pltpu
from jax.sharding import PartitionSpec as P

NOCC = 1024
BLK = 128
NBLK = 4
NB = 512
GROUP = 16
MIB = 1024 * 1024
VMEM = pl.BlockSpec(memory_space=pltpu.VMEM)


def masked_kernel(pattern, blocks, occupied, ligand, masked, panel, part, orbitals, held, opened, sems):
    aux_rows, _, nu_width = blocks.shape
    own = own_half_of(part.shape[0])
    moves = ((blocks, held), (pattern, opened), (occupied.at[own], part), (occupied, panel), (ligand.at[own], orbitals))
    copies = [pltpu.make_async_copy(source, target, sems.at[k]) for k, (source, target) in enumerate(moves)]
    for copy in copies:
        copy.start()
    copies[0].wait()
    copies[1].wait()
    for q in range(aux_rows):
        for m in range(NBLK):
            for n in range(nu_width // BLK):
                rows, columns = pl.ds(m * BLK, BLK), pl.ds(n * BLK, BLK)
                tile = held[q, rows, columns]
                masked[q, rows, columns] = jnp.where(opened[0, n, m] != 0, tile, jnp.zeros_like(tile))
    for copy in copies[2:]:
        copy.wait()


def own_half_of(length):
    return pl.ds(pl.multiple_of(lax.axis_index("ao") * length, length), length)


def half_into(outs, turned, masked):
    for d, out in enumerate(outs):
        for q in range(out.shape[0]):
            out[q] = jnp.dot(turned[d], masked[q], preferred_element_type=jnp.float32).astype(jnp.bfloat16)


def own_kernel(occupied, mine, theirs, masked, turned, *outs):
    aux, orb, ao = (lax.axis_index(name) for name in ("aux", "orb", "ao"))
    ni = turned.shape[1]
    here = 2 * (aux & 1) + orb
    place = lambda s: (4 - (here ^ s)) & 3
    near = orb == aux // 2

    @pl.when(near)
    def _():
        for s in range(turned.shape[0]):
            turned[place(s)] = occupied[:, s * ni : (s + 1) * ni].T

    @pl.when(jnp.logical_not(near))
    def _():
        depth = mine.shape[0]
        for e, rows in enumerate((mine, theirs)):
            first = pl.multiple_of((ao ^ e) * depth, depth)
            for s in range(turned.shape[0]):
                turned[place(s), :, pl.ds(first, depth)] = rows[:, s * ni : (s + 1) * ni].T

    half_into(outs, turned, masked)


def density_kernel(occupied, mine, theirs, masked, turned, *refs):
    messages, out, panel = refs[:-2], refs[-2], refs[-1]
    aux_rows, ni, nu_width = messages[0].shape
    depth = mine.shape[0]
    own = own_half_of(nu_width)
    near = lax.axis_index("orb") == lax.axis_index("aux") // 2

    @pl.when(near)
    def _():
        for e, rows in enumerate((mine, theirs)):
            panel[pl.ds(pl.multiple_of((lax.axis_index("ao") ^ e) * depth, depth), depth), :] = rows[...]

    @pl.when(jnp.logical_not(near))
    def _():
        panel[...] = occupied[...]

    totals = [0.0] * aux_rows
    for d, message in enumerate(messages):
        rows = turned[d, :, own].astype(jnp.float32)
        for q in range(aux_rows):
            totals[q] += jnp.sum(rows * message[q].astype(jnp.float32))
    for s in range(4):
        rows = panel[:, s * ni : (s + 1) * ni].T
        weights = panel[own, s * ni : (s + 1) * ni].T.astype(jnp.float32)
        for q in range(aux_rows):
            result = jnp.dot(rows, masked[q], preferred_element_type=jnp.float32).astype(jnp.bfloat16)
            totals[q] += jnp.sum(weights * result.astype(jnp.float32))
    for q in range(aux_rows):
        out[q : q + 1, :] = jnp.full((1, out.shape[1]), totals[q], jnp.float32)


def far_kernel(before, masked, turned, *outs):
    half_into(outs, turned, masked)


def pair_kernel(before, earlier, ligand, *refs):
    arrived, own, sent = refs[:-2], refs[-2], refs[-1]
    aux_rows, ni, nu_width = arrived[0].shape
    width = ligand.shape[1]
    for k, message in enumerate(arrived):
        part = jnp.dot(
            message[...].reshape(aux_rows * ni, nu_width), ligand[...], preferred_element_type=jnp.float32
        ).reshape(aux_rows, ni, width)
        own[k * aux_rows : (k + 1) * aux_rows] = part
        sent[k * aux_rows : (k + 1) * aux_rows] = part.astype(jnp.bfloat16)


def turn_kernel(*refs):
    messages, out = refs[:-1], refs[-1]
    nu_width = messages[0].shape[2]
    for g in range(out.shape[0]):
        here = pl.ds(g * GROUP, GROUP)
        out[g] = jnp.concatenate([x[:, here, :].reshape(-1, nu_width) for x in messages], axis=0).T


def pair_and_turn_kernel(before, earlier, ligand, *refs):
    pair_kernel(before, earlier, ligand, *refs[:-1])
    turn_kernel(*refs[:-3], refs[-1])


def cross_kernel(scale, near, far, *refs):
    pairs, (out, held, sem) = refs[:4], refs[4:]
    ni, _, width = out.shape

    def step(g, carry):
        here = pl.ds(pl.multiple_of(g * GROUP, GROUP), GROUP)
        turned = jnp.concatenate([near[g], far[g]], axis=1)
        summed = [pairs[j][:, here, :] + pairs[j + 1][:, here, :].astype(jnp.float32) for j in (0, 2)]
        summed = jnp.concatenate([(x * scale).astype(jnp.bfloat16) for x in summed], axis=0)
        row = lax.broadcasted_iota(jnp.int32, (1, GROUP, width), 1)
        zero = jnp.zeros_like(summed)
        for i in range(0, GROUP, 2):
            both = [jnp.where(row == i + e, summed, zero).reshape(-1, width) for e in (0, 1)]
            result = jnp.dot(turned, jnp.concatenate(both, axis=1), preferred_element_type=jnp.float32)
            held[g * GROUP + i] = result[:, :width]
            held[g * GROUP + i + 1] = result[:, width:]
            if i % 4 == 2:
                done = pl.ds(g * GROUP + i - 2, 4)
                pltpu.make_async_copy(held.at[done], out.at[done], sem).start()
        return carry

    lax.fori_loop(0, ni // GROUP, step, 0)
    pltpu.make_async_copy(held, out, sem).wait()


def call(kernel, name, inputs, outputs, scratch=(), limit=16, flops=0, moved=1 << 20, in_spec=VMEM, out_spec=VMEM):
    inputs = list(inputs)
    results = pl.pallas_call(
        kernel,
        in_specs=[in_spec] * len(inputs),
        out_specs=[out_spec] * len(outputs),
        out_shape=outputs,
        scratch_shapes=list(scratch),
        compiler_params=pltpu.CompilerParams(vmem_limit_bytes=limit * MIB),
        cost_estimate=pl.CostEstimate(flops=flops, bytes_accessed=moved, transcendentals=0),
        name=name,
    )(*inputs)
    return list(results)


def body(sizes, blocks, pattern, occupied, ligand):
    n_aux, n_orb, n_ao = sizes
    aux_rows, _, nu_width = blocks.shape
    owners = n_aux * n_orb
    ni = NOCC // owners
    q_total = aux_rows * owners
    panel_width = occupied.shape[1]
    width = ligand.shape[1]
    bf16 = functools.partial(jax.ShapeDtypeStruct, dtype=jnp.bfloat16)
    f32 = functools.partial(jax.ShapeDtypeStruct, dtype=jnp.float32)

    across = [(a, a ^ 2) for a in range(n_aux)]
    swap = [(c, 1 - c) for c in range(n_ao)]
    pattern = jnp.swapaxes(pattern, 1, 2)
    masked, panel, part, orbitals = call(
        masked_kernel,
        "masked_blocks",
        (pltpu.with_memory_space_constraint(x, pltpu.HBM) for x in (pattern, blocks, occupied, ligand)),
        [bf16(blocks.shape), bf16(occupied.shape), bf16((NB // n_ao, panel_width)), bf16((NB // n_ao, width))],
        [
            pltpu.VMEM(blocks.shape, jnp.bfloat16),
            pltpu.SMEM(pattern.shape, pattern.dtype),
            pltpu.SemaphoreType.DMA((5,)),
        ],
        in_spec=pl.BlockSpec(memory_space=pltpu.HBM),
    )
    far_masked = lax.ppermute(masked, "aux", across)
    mine = lax.ppermute(part, "orb", swap)
    theirs = lax.ppermute(mine, "ao", swap)

    def square(messages):
        arrived = [messages[0]]
        for message, d in zip(messages[1:], (3, 2, 1)):
            moves = [
                (a * n_orb + o, (a ^ (d >> 1)) * n_orb + (o ^ (d & 1))) for a in range(n_aux) for o in range(n_orb)
            ]
            arrived.append(lax.ppermute(message, ("aux", "orb"), moves))
        return arrived

    work = 2 * NB * panel_width * nu_width * aux_rows
    messages = [bf16((aux_rows, ni, nu_width))] * 4
    turned, *own = call(
        own_kernel, "own_half", (panel, mine, theirs, masked), [bf16((4, ni, NB))] + messages, flops=work
    )
    own_here = square(own)
    value = call(
        density_kernel,
        "density_terms",
        (panel, mine, theirs, masked, turned, *own),
        [f32((aux_rows, 128))],
        [pltpu.VMEM(occupied.shape, jnp.bfloat16)],
        flops=work,
    )[0]
    value_there = lax.ppermute(value, "ao", swap)
    density = (value[:, 0] + value_there[:, 0]) / math.sqrt(NOCC)
    far = call(far_kernel, "far_half", (value, far_masked, turned), messages, flops=work)
    far_here = square(far)

    shape = (4 * aux_rows, ni, width)
    kept_and_given = [f32(shape), bf16(shape)]
    side = [bf16((ni // GROUP, nu_width, 4 * aux_rows * GROUP))]
    pair_work = 2 * shape[0] * ni * nu_width * width
    own_kept, own_given, own_rows = call(
        pair_and_turn_kernel,
        "own_pairs",
        (value_there, far[0], orbitals, *own_here),
        kept_and_given + side,
        flops=pair_work,
    )
    own_pairs = (own_kept, lax.ppermute(own_given, "ao", swap))
    far_kept, far_given = call(
        pair_kernel, "far_pairs", (value_there, own_rows, orbitals, *far_here), kept_and_given, flops=pair_work
    )
    far_pairs = (far_kept, lax.ppermute(far_given, "ao", swap))
    far_rows = call(turn_kernel, "far_turned", far_here, side)[0]

    result = (ni, nu_width, width)
    cross_terms = call(
        functools.partial(cross_kernel, 1.0 / math.sqrt(q_total)),
        "cross_terms",
        (own_rows, far_rows, *own_pairs, *far_pairs),
        [f32(result)],
        [pltpu.VMEM(result, jnp.float32), pltpu.SemaphoreType.DMA],
        limit=32,
        flops=32 * q_total * ni * nu_width * width,
        moved=18 * MIB,
        out_spec=pl.BlockSpec(memory_space=pltpu.HBM),
    )[0]
    return (density, cross_terms)


def plain_body(blocks, pattern, occupied, ligand):
    panels = lax.all_gather(occupied, "orb", axis=1, tiled=True)
    aux_rows = blocks.shape[0]
    nu_width = blocks.shape[2]
    nu_blocks = pattern.shape[2]
    opened = pattern[0].astype(jnp.bfloat16)
    masked = blocks.reshape(aux_rows, NBLK, BLK, nu_blocks, BLK) * opened[None, :, None, :, None]
    masked = masked.reshape(aux_rows, NB, nu_width)
    transformed = jnp.einsum(
        "qmn,mi->qin", masked, panels, preferred_element_type=jnp.float32
    ).astype(jnp.bfloat16)
    nu_start = lax.axis_index("ao") * nu_width
    own_rows = lax.dynamic_slice_in_dim(panels, nu_start, nu_width, 0)
    partial_value = jnp.einsum(
        "qin,ni->q", transformed, own_rows, preferred_element_type=jnp.float32
    )
    density = lax.psum(partial_value, "ao") / math.sqrt(NOCC)
    arrived = lax.all_to_all(transformed, ("aux", "orb"), split_axis=1, concat_axis=0, tiled=True)
    own_ligand = lax.dynamic_slice_in_dim(ligand, nu_start, nu_width, 0)
    pair_part = jnp.einsum("qin,nj->qij", arrived, own_ligand, preferred_element_type=jnp.float32)
    mixed_pairs = lax.psum(pair_part, "ao").astype(jnp.bfloat16)
    crossed = jnp.einsum("qin,qij->inj", arrived, mixed_pairs, preferred_element_type=jnp.float32)
    cross_terms = crossed / math.sqrt(arrived.shape[0])
    return (density, cross_terms)


def solution(mesh):
    sizes = (mesh.shape["aux"], mesh.shape["orb"], mesh.shape["ao"])
    kernels = sizes == (4, 2, 2)
    return jax.shard_map(
        functools.partial(body, sizes) if kernels else plain_body,
        mesh=mesh,
        in_specs=(
            P(("pose", "aux", "orb"), None, "ao"),
            P(("pose", "aux", "orb"), None, "ao"),
            P(None, "orb"),
            P(None, "pose"),
        ),
        out_specs=(P(("pose", "aux", "orb")), P(("pose", "aux", "orb"), "ao", None)),
        check_vma=False,
    )
```

```python
import functools
import math

import jax
import jax.numpy as jnp
from jax import lax
from jax.experimental import pallas as pl
from jax.experimental.pallas import tpu as pltpu
from jax.sharding import PartitionSpec as P

NOCC = 1024
BLK = 128
NBLK = 4
NB = 512
GROUP = 16
MIB = 1024 * 1024
VMEM = pl.BlockSpec(memory_space=pltpu.VMEM)


def masked_kernel(pattern, blocks, occupied, ligand, masked, panel, orbitals, held, opened, sems):
    aux_rows, _, nu_width = blocks.shape
    own = own_half_of(orbitals.shape[0])
    moves = ((blocks, held), (pattern, opened), (occupied, panel), (ligand.at[own], orbitals))
    copies = [pltpu.make_async_copy(source, target, sems.at[k]) for k, (source, target) in enumerate(moves)]
    for copy in copies:
        copy.start()
    copies[0].wait()
    copies[1].wait()
    for q in range(aux_rows):
        for m in range(NBLK):
            for n in range(nu_width // BLK):
                rows, columns = pl.ds(m * BLK, BLK), pl.ds(n * BLK, BLK)
                tile = held[q, rows, columns]
                masked[q, rows, columns] = jnp.where(opened[0, n, m] != 0, tile, jnp.zeros_like(tile))
    for copy in copies[2:]:
        copy.wait()


def own_half_of(length):
    return pl.ds(pl.multiple_of(lax.axis_index("ao") * length, length), length)


def half_into(outs, turned, masked):
    for d, out in enumerate(outs):
        for q in range(out.shape[0]):
            out[q] = jnp.dot(turned[d], masked[q], preferred_element_type=jnp.float32).astype(jnp.bfloat16)


def own_kernel(occupied, other, masked, turned, *outs):
    aux, orb = lax.axis_index("aux"), lax.axis_index("orb")
    ni = turned.shape[1]
    here = 2 * (aux & 1) + orb
    place = lambda s: (4 - (here ^ s)) & 3
    near = orb == aux // 2

    @pl.when(near)
    def _():
        for s in range(turned.shape[0]):
            turned[place(s)] = occupied[:, s * ni : (s + 1) * ni].T

    @pl.when(jnp.logical_not(near))
    def _():
        for s in range(turned.shape[0]):
            turned[place(s)] = other[:, s * ni : (s + 1) * ni].T

    half_into(outs, turned, masked)


def density_kernel(occupied, other, masked, turned, *refs):
    messages, out, panel = refs[:-2], refs[-2], refs[-1]
    aux_rows, ni, nu_width = messages[0].shape
    own = own_half_of(nu_width)
    near = lax.axis_index("orb") == lax.axis_index("aux") // 2

    @pl.when(near)
    def _():
        panel[...] = other[...]

    @pl.when(jnp.logical_not(near))
    def _():
        panel[...] = occupied[...]

    totals = [0.0] * aux_rows
    for d, message in enumerate(messages):
        rows = turned[d, :, own].astype(jnp.float32)
        for q in range(aux_rows):
            totals[q] += jnp.sum(rows * message[q].astype(jnp.float32))
    for s in range(4):
        rows = panel[:, s * ni : (s + 1) * ni].T
        weights = panel[own, s * ni : (s + 1) * ni].T.astype(jnp.float32)
        for q in range(aux_rows):
            result = jnp.dot(rows, masked[q], preferred_element_type=jnp.float32).astype(jnp.bfloat16)
            totals[q] += jnp.sum(weights * result.astype(jnp.float32))
    for q in range(aux_rows):
        out[q : q + 1, :] = jnp.full((1, out.shape[1]), totals[q], jnp.float32)


def open_kernel(pattern, opened):
    for m in range(NBLK):
        for n in range(opened.shape[1] // BLK):
            value = jnp.where(pattern[0, n, m] != 0, 1.0, 0.0)
            opened[pl.ds(m * BLK, BLK), pl.ds(n * BLK, BLK)] = jnp.full((BLK, BLK), value, jnp.float32)


def far_kernel(before, opened, blocks, turned, *refs):
    outs, masked = refs[:-1], refs[-1]
    keep = opened[...] != 0
    for q in range(blocks.shape[0]):
        tile = blocks[q]
        masked[q] = jnp.where(keep, tile, jnp.zeros_like(tile))
    half_into(outs, turned, masked)


def pair_kernel(before, earlier, ligand, *refs):
    arrived, own, sent = refs[:-2], refs[-2], refs[-1]
    aux_rows, ni, nu_width = arrived[0].shape
    width = ligand.shape[1]
    for k, message in enumerate(arrived):
        part = jnp.dot(
            message[...].reshape(aux_rows * ni, nu_width), ligand[...], preferred_element_type=jnp.float32
        ).reshape(aux_rows, ni, width)
        own[k * aux_rows : (k + 1) * aux_rows] = part
        sent[k * aux_rows : (k + 1) * aux_rows] = part.astype(jnp.bfloat16)


def turn_kernel(*refs):
    messages, out = refs[:-1], refs[-1]
    nu_width = messages[0].shape[2]
    for g in range(out.shape[0]):
        here = pl.ds(g * GROUP, GROUP)
        out[g] = jnp.concatenate([x[:, here, :].reshape(-1, nu_width) for x in messages], axis=0).T


def pair_and_turn_kernel(before, earlier, ligand, *refs):
    pair_kernel(before, earlier, ligand, *refs[:-1])
    turn_kernel(*refs[:-3], refs[-1])


def cross_kernel(scale, near, far, *refs):
    pairs, (out, held, sem) = refs[:4], refs[4:]
    ni, _, width = out.shape

    def step(g, carry):
        here = pl.ds(pl.multiple_of(g * GROUP, GROUP), GROUP)
        turned = jnp.concatenate([near[g], far[g]], axis=1)
        summed = [pairs[j][:, here, :] + pairs[j + 1][:, here, :].astype(jnp.float32) for j in (0, 2)]
        summed = jnp.concatenate([(x * scale).astype(jnp.bfloat16) for x in summed], axis=0)
        row = lax.broadcasted_iota(jnp.int32, (1, GROUP, width), 1)
        zero = jnp.zeros_like(summed)
        for i in range(0, GROUP, 2):
            both = [jnp.where(row == i + e, summed, zero).reshape(-1, width) for e in (0, 1)]
            result = jnp.dot(turned, jnp.concatenate(both, axis=1), preferred_element_type=jnp.float32)
            held[g * GROUP + i] = result[:, :width]
            held[g * GROUP + i + 1] = result[:, width:]
            if i % 4 == 2:
                done = pl.ds(g * GROUP + i - 2, 4)
                pltpu.make_async_copy(held.at[done], out.at[done], sem).start()
        return carry

    lax.fori_loop(0, ni // GROUP, step, 0)
    pltpu.make_async_copy(held, out, sem).wait()


def call(kernel, name, inputs, outputs, scratch=(), limit=16, flops=0, moved=1 << 20, in_spec=VMEM, out_spec=VMEM):
    inputs = list(inputs)
    results = pl.pallas_call(
        kernel,
        in_specs=[in_spec] * len(inputs),
        out_specs=[out_spec] * len(outputs),
        out_shape=outputs,
        scratch_shapes=list(scratch),
        compiler_params=pltpu.CompilerParams(vmem_limit_bytes=limit * MIB),
        cost_estimate=pl.CostEstimate(flops=flops, bytes_accessed=moved, transcendentals=0),
        name=name,
    )(*inputs)
    return list(results)


def body(sizes, blocks, pattern, occupied, ligand):
    n_aux, n_orb, n_ao = sizes
    aux_rows, _, nu_width = blocks.shape
    owners = n_aux * n_orb
    ni = NOCC // owners
    q_total = aux_rows * owners
    panel_width = occupied.shape[1]
    width = ligand.shape[1]
    bf16 = functools.partial(jax.ShapeDtypeStruct, dtype=jnp.bfloat16)
    f32 = functools.partial(jax.ShapeDtypeStruct, dtype=jnp.float32)

    across = [(a, a ^ 2) for a in range(n_aux)]
    swap = [(c, 1 - c) for c in range(n_ao)]
    pattern = jnp.swapaxes(pattern, 1, 2)
    masked, panel, orbitals = call(
        masked_kernel,
        "masked_blocks",
        (pltpu.with_memory_space_constraint(x, pltpu.HBM) for x in (pattern, blocks, occupied, ligand)),
        [bf16(blocks.shape), bf16(occupied.shape), bf16((NB // n_ao, width))],
        [
            pltpu.VMEM(blocks.shape, jnp.bfloat16),
            pltpu.SMEM(pattern.shape, pattern.dtype),
            pltpu.SemaphoreType.DMA((4,)),
        ],
        in_spec=pl.BlockSpec(memory_space=pltpu.HBM),
    )
    far_blocks = lax.ppermute(blocks, "aux", across)
    opened = call(
        open_kernel,
        "open_blocks",
        (lax.ppermute(pattern, "aux", across),),
        [f32((NB, nu_width))],
        in_spec=pl.BlockSpec(memory_space=pltpu.SMEM),
    )[0]
    other = lax.ppermute(occupied, "orb", swap)

    def square(messages):
        arrived = [messages[0]]
        for message, d in zip(messages[1:], (3, 2, 1)):
            moves = [
                (a * n_orb + o, (a ^ (d >> 1)) * n_orb + (o ^ (d & 1))) for a in range(n_aux) for o in range(n_orb)
            ]
            arrived.append(lax.ppermute(message, ("aux", "orb"), moves))
        return arrived

    work = 2 * NB * panel_width * nu_width * aux_rows
    messages = [bf16((aux_rows, ni, nu_width))] * 4
    turned, *own = call(
        own_kernel, "own_half", (panel, other, masked), [bf16((4, ni, NB))] + messages, flops=work
    )
    own_here = square(own)
    value = call(
        density_kernel,
        "density_terms",
        (panel, other, masked, turned, *own),
        [f32((aux_rows, 128))],
        [pltpu.VMEM(occupied.shape, jnp.bfloat16)],
        flops=work,
    )[0]
    value_there = lax.ppermute(value, "ao", swap)
    density = (value[:, 0] + value_there[:, 0]) / math.sqrt(NOCC)
    far = call(
        far_kernel,
        "far_half",
        (value, opened, far_blocks, turned),
        messages,
        [pltpu.VMEM(blocks.shape, jnp.bfloat16)],
        flops=work,
    )
    far_here = square(far)

    shape = (4 * aux_rows, ni, width)
    kept_and_given = [f32(shape), bf16(shape)]
    side = [bf16((ni // GROUP, nu_width, 4 * aux_rows * GROUP))]
    pair_work = 2 * shape[0] * ni * nu_width * width
    own_kept, own_given, own_rows = call(
        pair_and_turn_kernel,
        "own_pairs",
        (value_there, far[0], orbitals, *own_here),
        kept_and_given + side,
        flops=pair_work,
    )
    own_pairs = (own_kept, lax.ppermute(own_given, "ao", swap))
    far_kept, far_given = call(
        pair_kernel, "far_pairs", (value_there, own_rows, orbitals, *far_here), kept_and_given, flops=pair_work
    )
    far_pairs = (far_kept, lax.ppermute(far_given, "ao", swap))
    far_rows = call(turn_kernel, "far_turned", far_here, side)[0]

    result = (ni, nu_width, width)
    cross_terms = call(
        functools.partial(cross_kernel, 1.0 / math.sqrt(q_total)),
        "cross_terms",
        (own_rows, far_rows, *own_pairs, *far_pairs),
        [f32(result)],
        [pltpu.VMEM(result, jnp.float32), pltpu.SemaphoreType.DMA],
        limit=32,
        flops=32 * q_total * ni * nu_width * width,
        moved=18 * MIB,
        out_spec=pl.BlockSpec(memory_space=pltpu.HBM),
    )[0]
    return (density, cross_terms)


def plain_body(blocks, pattern, occupied, ligand):
    panels = lax.all_gather(occupied, "orb", axis=1, tiled=True)
    aux_rows = blocks.shape[0]
    nu_width = blocks.shape[2]
    nu_blocks = pattern.shape[2]
    opened = pattern[0].astype(jnp.bfloat16)
    masked = blocks.reshape(aux_rows, NBLK, BLK, nu_blocks, BLK) * opened[None, :, None, :, None]
    masked = masked.reshape(aux_rows, NB, nu_width)
    transformed = jnp.einsum(
        "qmn,mi->qin", masked, panels, preferred_element_type=jnp.float32
    ).astype(jnp.bfloat16)
    nu_start = lax.axis_index("ao") * nu_width
    own_rows = lax.dynamic_slice_in_dim(panels, nu_start, nu_width, 0)
    partial_value = jnp.einsum(
        "qin,ni->q", transformed, own_rows, preferred_element_type=jnp.float32
    )
    density = lax.psum(partial_value, "ao") / math.sqrt(NOCC)
    arrived = lax.all_to_all(transformed, ("aux", "orb"), split_axis=1, concat_axis=0, tiled=True)
    own_ligand = lax.dynamic_slice_in_dim(ligand, nu_start, nu_width, 0)
    pair_part = jnp.einsum("qin,nj->qij", arrived, own_ligand, preferred_element_type=jnp.float32)
    mixed_pairs = lax.psum(pair_part, "ao").astype(jnp.bfloat16)
    crossed = jnp.einsum("qin,qij->inj", arrived, mixed_pairs, preferred_element_type=jnp.float32)
    cross_terms = crossed / math.sqrt(arrived.shape[0])
    return (density, cross_terms)


def solution(mesh):
    sizes = (mesh.shape["aux"], mesh.shape["orb"], mesh.shape["ao"])
    kernels = sizes == (4, 2, 2)
    return jax.shard_map(
        functools.partial(body, sizes) if kernels else plain_body,
        mesh=mesh,
        in_specs=(
            P(("pose", "aux", "orb"), None, "ao"),
            P(("pose", "aux", "orb"), None, "ao"),
            P(None, "orb"),
            P(None, "pose"),
        ),
        out_specs=(P(("pose", "aux", "orb")), P(("pose", "aux", "orb"), "ao", None)),
        check_vma=False,
    )
```

```python
import functools
import math

import jax
import jax.numpy as jnp
from jax import lax
from jax.experimental import pallas as pl
from jax.experimental.pallas import tpu as pltpu
from jax.sharding import PartitionSpec as P

NOCC = 1024
BLK = 128
NBLK = 4
NB = 512
GROUP = 16
MIB = 1024 * 1024
VMEM = pl.BlockSpec(memory_space=pltpu.VMEM)


def masked_kernel(pattern, blocks, occupied, ligand, masked, again, panel, part, orbitals, held, opened, sems):
    aux_rows, _, nu_width = blocks.shape
    own = own_half_of(part.shape[0])
    moves = ((blocks, held), (pattern, opened), (occupied.at[own], part), (occupied, panel), (ligand.at[own], orbitals))
    copies = [pltpu.make_async_copy(source, target, sems.at[k]) for k, (source, target) in enumerate(moves)]
    for copy in copies:
        copy.start()
    copies[0].wait()
    copies[1].wait()
    for q in range(aux_rows):
        for m in range(NBLK):
            for n in range(nu_width // BLK):
                rows, columns = pl.ds(m * BLK, BLK), pl.ds(n * BLK, BLK)
                tile = held[q, rows, columns]
                tile = jnp.where(opened[0, n, m] != 0, tile, jnp.zeros_like(tile))
                masked[q, rows, columns] = tile
                again[q, rows, columns] = tile
    for copy in copies[2:]:
        copy.wait()


def own_half_of(length):
    return pl.ds(pl.multiple_of(lax.axis_index("ao") * length, length), length)


def after_kernel(block, before, out):
    pass


def half_into(outs, turned, masked):
    for d, out in enumerate(outs):
        for q in range(out.shape[0]):
            out[q] = jnp.dot(turned[d], masked[q], preferred_element_type=jnp.float32).astype(jnp.bfloat16)


def own_kernel(occupied, mine, theirs, masked, turned, *outs):
    aux, orb, ao = (lax.axis_index(name) for name in ("aux", "orb", "ao"))
    ni = turned.shape[1]
    here = 2 * (aux & 1) + orb
    place = lambda s: (4 - (here ^ s)) & 3
    near = orb == aux // 2

    @pl.when(near)
    def _():
        for s in range(turned.shape[0]):
            turned[place(s)] = occupied[:, s * ni : (s + 1) * ni].T

    @pl.when(jnp.logical_not(near))
    def _():
        depth = mine.shape[0]
        for e, rows in enumerate((mine, theirs)):
            first = pl.multiple_of((ao ^ e) * depth, depth)
            for s in range(turned.shape[0]):
                turned[place(s), :, pl.ds(first, depth)] = rows[:, s * ni : (s + 1) * ni].T

    half_into(outs, turned, masked)


def density_kernel(occupied, mine, theirs, masked, turned, *refs):
    messages, out, panel = refs[:-2], refs[-2], refs[-1]
    aux_rows, ni, nu_width = messages[0].shape
    depth = mine.shape[0]
    own = own_half_of(nu_width)
    near = lax.axis_index("orb") == lax.axis_index("aux") // 2

    @pl.when(near)
    def _():
        for e, rows in enumerate((mine, theirs)):
            panel[pl.ds(pl.multiple_of((lax.axis_index("ao") ^ e) * depth, depth), depth), :] = rows[...]

    @pl.when(jnp.logical_not(near))
    def _():
        panel[...] = occupied[...]

    totals = [0.0] * aux_rows
    for d, message in enumerate(messages):
        rows = turned[d, :, own].astype(jnp.float32)
        for q in range(aux_rows):
            totals[q] += jnp.sum(rows * message[q].astype(jnp.float32))
    for s in range(4):
        rows = panel[:, s * ni : (s + 1) * ni].T
        weights = panel[own, s * ni : (s + 1) * ni].T.astype(jnp.float32)
        for q in range(aux_rows):
            result = jnp.dot(rows, masked[q], preferred_element_type=jnp.float32).astype(jnp.bfloat16)
            totals[q] += jnp.sum(weights * result.astype(jnp.float32))
    for q in range(aux_rows):
        out[q : q + 1, :] = jnp.full((1, out.shape[1]), totals[q], jnp.float32)


def far_kernel(before, inward, outward, turned, *outs):
    aux = lax.axis_index("aux")
    inner = jnp.logical_or(aux == 1, aux == 2)
    pl.when(inner)(functools.partial(half_into, outs, turned, inward))
    pl.when(jnp.logical_not(inner))(functools.partial(half_into, outs, turned, outward))


def pair_kernel(before, earlier, ligand, *refs):
    arrived, own, sent = refs[:-2], refs[-2], refs[-1]
    aux_rows, ni, nu_width = arrived[0].shape
    width = ligand.shape[1]
    for k, message in enumerate(arrived):
        part = jnp.dot(
            message[...].reshape(aux_rows * ni, nu_width), ligand[...], preferred_element_type=jnp.float32
        ).reshape(aux_rows, ni, width)
        own[k * aux_rows : (k + 1) * aux_rows] = part
        sent[k * aux_rows : (k + 1) * aux_rows] = part.astype(jnp.bfloat16)


def turn_kernel(*refs):
    messages, out = refs[:-1], refs[-1]
    nu_width = messages[0].shape[2]
    for g in range(out.shape[0]):
        here = pl.ds(g * GROUP, GROUP)
        out[g] = jnp.concatenate([x[:, here, :].reshape(-1, nu_width) for x in messages], axis=0).T


def pair_and_turn_kernel(before, earlier, ligand, *refs):
    pair_kernel(before, earlier, ligand, *refs[:-1])
    turn_kernel(*refs[:-3], refs[-1])


def cross_kernel(scale, near, far, *refs):
    pairs, (out, held, sem) = refs[:4], refs[4:]
    ni, _, width = out.shape

    def step(g, carry):
        here = pl.ds(pl.multiple_of(g * GROUP, GROUP), GROUP)
        turned = jnp.concatenate([near[g], far[g]], axis=1)
        summed = [pairs[j][:, here, :] + pairs[j + 1][:, here, :].astype(jnp.float32) for j in (0, 2)]
        summed = jnp.concatenate([(x * scale).astype(jnp.bfloat16) for x in summed], axis=0)
        row = lax.broadcasted_iota(jnp.int32, (1, GROUP, width), 1)
        zero = jnp.zeros_like(summed)
        for i in range(0, GROUP, 2):
            both = [jnp.where(row == i + e, summed, zero).reshape(-1, width) for e in (0, 1)]
            result = jnp.dot(turned, jnp.concatenate(both, axis=1), preferred_element_type=jnp.float32)
            held[g * GROUP + i] = result[:, :width]
            held[g * GROUP + i + 1] = result[:, width:]
            if i % 4 == 2:
                done = pl.ds(g * GROUP + i - 2, 4)
                pltpu.make_async_copy(held.at[done], out.at[done], sem).start()
        return carry

    lax.fori_loop(0, ni // GROUP, step, 0)
    pltpu.make_async_copy(held, out, sem).wait()


def call(kernel, name, inputs, outputs, scratch=(), limit=16, flops=0, moved=1 << 20, in_spec=VMEM, out_spec=VMEM, aliases=None):
    inputs = list(inputs)
    results = pl.pallas_call(
        kernel,
        in_specs=[in_spec] * len(inputs),
        out_specs=[out_spec] * len(outputs),
        out_shape=outputs,
        scratch_shapes=list(scratch),
        compiler_params=pltpu.CompilerParams(vmem_limit_bytes=limit * MIB),
        cost_estimate=pl.CostEstimate(flops=flops, bytes_accessed=moved, transcendentals=0),
        input_output_aliases=aliases or {},
        name=name,
    )(*inputs)
    return list(results)


def body(sizes, blocks, pattern, occupied, ligand):
    n_aux, n_orb, n_ao = sizes
    aux_rows, _, nu_width = blocks.shape
    owners = n_aux * n_orb
    ni = NOCC // owners
    q_total = aux_rows * owners
    panel_width = occupied.shape[1]
    width = ligand.shape[1]
    bf16 = functools.partial(jax.ShapeDtypeStruct, dtype=jnp.bfloat16)
    f32 = functools.partial(jax.ShapeDtypeStruct, dtype=jnp.float32)

    swap = [(c, 1 - c) for c in range(n_ao)]
    pattern = jnp.swapaxes(pattern, 1, 2)
    masked, again, panel, part, orbitals = call(
        masked_kernel,
        "masked_blocks",
        (pltpu.with_memory_space_constraint(x, pltpu.HBM) for x in (pattern, blocks, occupied, ligand)),
        [bf16(blocks.shape)] * 2
        + [bf16(occupied.shape), bf16((NB // n_ao, panel_width)), bf16((NB // n_ao, width))],
        [
            pltpu.VMEM(blocks.shape, jnp.bfloat16),
            pltpu.SMEM(pattern.shape, pattern.dtype),
            pltpu.SemaphoreType.DMA((5,)),
        ],
        in_spec=pl.BlockSpec(memory_space=pltpu.HBM),
    )
    inward = lax.ppermute(masked, "aux", [(0, 2), (3, 1)])
    anywhere = pl.BlockSpec(memory_space=pl.ANY)
    follower = call(
        after_kernel,
        "inner_blocks",
        (again, inward),
        [bf16(blocks.shape)],
        in_spec=anywhere,
        out_spec=anywhere,
        aliases={0: 0},
    )[0]
    outward = lax.ppermute(follower, "aux", [(1, 3), (2, 0)])
    mine = lax.ppermute(part, "orb", swap)
    theirs = lax.ppermute(mine, "ao", swap)

    def square(messages):
        arrived = [messages[0]]
        for message, d in zip(messages[1:], (3, 2, 1)):
            moves = [
                (a * n_orb + o, (a ^ (d >> 1)) * n_orb + (o ^ (d & 1))) for a in range(n_aux) for o in range(n_orb)
            ]
            arrived.append(lax.ppermute(message, ("aux", "orb"), moves))
        return arrived

    work = 2 * NB * panel_width * nu_width * aux_rows
    messages = [bf16((aux_rows, ni, nu_width))] * 4
    turned, *own = call(
        own_kernel, "own_half", (panel, mine, theirs, masked), [bf16((4, ni, NB))] + messages, flops=work
    )
    own_here = square(own)
    value = call(
        density_kernel,
        "density_terms",
        (panel, mine, theirs, masked, turned, *own),
        [f32((aux_rows, 128))],
        [pltpu.VMEM(occupied.shape, jnp.bfloat16)],
        flops=work,
    )[0]
    value_there = lax.ppermute(value, "ao", swap)
    density = (value[:, 0] + value_there[:, 0]) / math.sqrt(NOCC)
    far = call(far_kernel, "far_half", (value, inward, outward, turned), messages, flops=work)
    far_here = square(far)

    shape = (4 * aux_rows, ni, width)
    kept_and_given = [f32(shape), bf16(shape)]
    side = [bf16((ni // GROUP, nu_width, 4 * aux_rows * GROUP))]
    pair_work = 2 * shape[0] * ni * nu_width * width
    own_kept, own_given, own_rows = call(
        pair_and_turn_kernel,
        "own_pairs",
        (value_there, far[0], orbitals, *own_here),
        kept_and_given + side,
        flops=pair_work,
    )
    own_pairs = (own_kept, lax.ppermute(own_given, "ao", swap))
    far_kept, far_given = call(
        pair_kernel, "far_pairs", (value_there, own_rows, orbitals, *far_here), kept_and_given, flops=pair_work
    )
    far_pairs = (far_kept, lax.ppermute(far_given, "ao", swap))
    far_rows = call(turn_kernel, "far_turned", far_here, side)[0]

    result = (ni, nu_width, width)
    cross_terms = call(
        functools.partial(cross_kernel, 1.0 / math.sqrt(q_total)),
        "cross_terms",
        (own_rows, far_rows, *own_pairs, *far_pairs),
        [f32(result)],
        [pltpu.VMEM(result, jnp.float32), pltpu.SemaphoreType.DMA],
        limit=32,
        flops=32 * q_total * ni * nu_width * width,
        moved=18 * MIB,
        out_spec=pl.BlockSpec(memory_space=pltpu.HBM),
    )[0]
    return (density, cross_terms)


def plain_body(blocks, pattern, occupied, ligand):
    panels = lax.all_gather(occupied, "orb", axis=1, tiled=True)
    aux_rows = blocks.shape[0]
    nu_width = blocks.shape[2]
    nu_blocks = pattern.shape[2]
    opened = pattern[0].astype(jnp.bfloat16)
    masked = blocks.reshape(aux_rows, NBLK, BLK, nu_blocks, BLK) * opened[None, :, None, :, None]
    masked = masked.reshape(aux_rows, NB, nu_width)
    transformed = jnp.einsum(
        "qmn,mi->qin", masked, panels, preferred_element_type=jnp.float32
    ).astype(jnp.bfloat16)
    nu_start = lax.axis_index("ao") * nu_width
    own_rows = lax.dynamic_slice_in_dim(panels, nu_start, nu_width, 0)
    partial_value = jnp.einsum(
        "qin,ni->q", transformed, own_rows, preferred_element_type=jnp.float32
    )
    density = lax.psum(partial_value, "ao") / math.sqrt(NOCC)
    arrived = lax.all_to_all(transformed, ("aux", "orb"), split_axis=1, concat_axis=0, tiled=True)
    own_ligand = lax.dynamic_slice_in_dim(ligand, nu_start, nu_width, 0)
    pair_part = jnp.einsum("qin,nj->qij", arrived, own_ligand, preferred_element_type=jnp.float32)
    mixed_pairs = lax.psum(pair_part, "ao").astype(jnp.bfloat16)
    crossed = jnp.einsum("qin,qij->inj", arrived, mixed_pairs, preferred_element_type=jnp.float32)
    cross_terms = crossed / math.sqrt(arrived.shape[0])
    return (density, cross_terms)


def solution(mesh):
    sizes = (mesh.shape["aux"], mesh.shape["orb"], mesh.shape["ao"])
    kernels = sizes == (4, 2, 2)
    return jax.shard_map(
        functools.partial(body, sizes) if kernels else plain_body,
        mesh=mesh,
        in_specs=(
            P(("pose", "aux", "orb"), None, "ao"),
            P(("pose", "aux", "orb"), None, "ao"),
            P(None, "orb"),
            P(None, "pose"),
        ),
        out_specs=(P(("pose", "aux", "orb")), P(("pose", "aux", "orb"), "ao", None)),
        check_vma=False,
    )
```

```python
import functools
import math

import jax
import jax.numpy as jnp
from jax import lax
from jax.experimental import pallas as pl
from jax.experimental.pallas import tpu as pltpu
from jax.sharding import PartitionSpec as P

NOCC = 1024
BLK = 128
NBLK = 4
NB = 512
GROUP = 16
MIB = 1024 * 1024
VMEM = pl.BlockSpec(memory_space=pltpu.VMEM)


def masked_kernel(pattern, blocks, occupied, ligand, masked, panel, part, orbitals, held, opened, sems):
    aux_rows, _, nu_width = blocks.shape
    own = own_half_of(part.shape[0])
    moves = ((blocks, held), (pattern, opened), (occupied.at[own], part), (occupied, panel), (ligand.at[own], orbitals))
    copies = [pltpu.make_async_copy(source, target, sems.at[k]) for k, (source, target) in enumerate(moves)]
    for copy in copies:
        copy.start()
    copies[0].wait()
    copies[1].wait()
    for q in range(aux_rows):
        for m in range(NBLK):
            for n in range(nu_width // BLK):
                rows, columns = pl.ds(m * BLK, BLK), pl.ds(n * BLK, BLK)
                tile = held[q, rows, columns]
                masked[q, rows, columns] = jnp.where(opened[0, n, m] != 0, tile, jnp.zeros_like(tile))
    for copy in copies[2:]:
        copy.wait()


def own_half_of(length):
    return pl.ds(pl.multiple_of(lax.axis_index("ao") * length, length), length)


def half_into(outs, turned, masked):
    for d, out in enumerate(outs):
        for q in range(out.shape[0]):
            out[q] = jnp.dot(turned[d], masked[q], preferred_element_type=jnp.float32).astype(jnp.bfloat16)


def own_kernel(occupied, mine, theirs, masked, turned, *outs):
    aux, orb, ao = (lax.axis_index(name) for name in ("aux", "orb", "ao"))
    ni = turned.shape[1]
    here = 2 * (aux & 1) + orb
    place = lambda s: (4 - (here ^ s)) & 3
    near = orb == aux // 2

    @pl.when(near)
    def _():
        for s in range(turned.shape[0]):
            turned[place(s)] = occupied[:, s * ni : (s + 1) * ni].T

    @pl.when(jnp.logical_not(near))
    def _():
        depth = mine.shape[0]
        for e, rows in enumerate((mine, theirs)):
            first = pl.multiple_of((ao ^ e) * depth, depth)
            for s in range(turned.shape[0]):
                turned[place(s), :, pl.ds(first, depth)] = rows[:, s * ni : (s + 1) * ni].T

    half_into(outs, turned, masked)


def density_kernel(occupied, mine, theirs, masked, turned, *refs):
    messages, out, panel = refs[:-2], refs[-2], refs[-1]
    aux_rows, ni, nu_width = messages[0].shape
    depth = mine.shape[0]
    own = own_half_of(nu_width)
    near = lax.axis_index("orb") == lax.axis_index("aux") // 2

    @pl.when(near)
    def _():
        for e, rows in enumerate((mine, theirs)):
            panel[pl.ds(pl.multiple_of((lax.axis_index("ao") ^ e) * depth, depth), depth), :] = rows[...]

    @pl.when(jnp.logical_not(near))
    def _():
        panel[...] = occupied[...]

    totals = [0.0] * aux_rows
    for d, message in enumerate(messages):
        rows = turned[d, :, own].astype(jnp.float32)
        for q in range(aux_rows):
            totals[q] += jnp.sum(rows * message[q].astype(jnp.float32))
    for s in range(4):
        rows = panel[:, s * ni : (s + 1) * ni].T
        weights = panel[own, s * ni : (s + 1) * ni].T.astype(jnp.float32)
        for q in range(aux_rows):
            result = jnp.dot(rows, masked[q], preferred_element_type=jnp.float32).astype(jnp.bfloat16)
            totals[q] += jnp.sum(weights * result.astype(jnp.float32))
    for q in range(aux_rows):
        out[q : q + 1, :] = jnp.full((1, out.shape[1]), totals[q], jnp.float32)


def far_kernel(before, masked, turned, *outs):
    half_into(outs, turned, masked)


def pair_kernel(before, earlier, ligand, *refs):
    arrived, own, sent = refs[:-2], refs[-2], refs[-1]
    aux_rows, ni, nu_width = arrived[0].shape
    width = ligand.shape[1]
    for k, message in enumerate(arrived):
        part = jnp.dot(
            message[...].reshape(aux_rows * ni, nu_width), ligand[...], preferred_element_type=jnp.float32
        ).reshape(aux_rows, ni, width)
        own[k * aux_rows : (k + 1) * aux_rows] = part
        sent[k * aux_rows : (k + 1) * aux_rows] = part.astype(jnp.bfloat16)


def turn_kernel(*refs):
    messages, out = refs[:-1], refs[-1]
    nu_width = messages[0].shape[2]
    for g in range(out.shape[0]):
        here = pl.ds(g * GROUP, GROUP)
        out[g] = jnp.concatenate([x[:, here, :].reshape(-1, nu_width) for x in messages], axis=0).T


def pair_and_turn_kernel(before, earlier, ligand, *refs):
    pair_kernel(before, earlier, ligand, *refs[:-1])
    turn_kernel(*refs[:-3], refs[-1])


def cross_kernel(scale, near, far, *refs):
    pairs, (out, held, sem) = refs[:4], refs[4:]
    ni, _, width = out.shape

    def step(g, carry):
        here = pl.ds(pl.multiple_of(g * GROUP, GROUP), GROUP)
        turned = jnp.concatenate([near[g], far[g]], axis=1)
        summed = [pairs[j][:, here, :] + pairs[j + 1][:, here, :].astype(jnp.float32) for j in (0, 2)]
        summed = jnp.concatenate([(x * scale).astype(jnp.bfloat16) for x in summed], axis=0)
        row = lax.broadcasted_iota(jnp.int32, (1, GROUP, width), 1)
        zero = jnp.zeros_like(summed)
        for i in range(0, GROUP, 2):
            both = [jnp.where(row == i + e, summed, zero).reshape(-1, width) for e in (0, 1)]
            result = jnp.dot(turned, jnp.concatenate(both, axis=1), preferred_element_type=jnp.float32)
            held[g * GROUP + i] = result[:, :width]
            held[g * GROUP + i + 1] = result[:, width:]
            if i % 4 == 2:
                done = pl.ds(g * GROUP + i - 2, 4)
                pltpu.make_async_copy(held.at[done], out.at[done], sem).start()
        return carry

    lax.fori_loop(0, ni // GROUP, step, 0, unroll=4)
    pltpu.make_async_copy(held, out, sem).wait()


def call(kernel, name, inputs, outputs, scratch=(), limit=16, flops=0, moved=1 << 20, in_spec=VMEM, out_spec=VMEM):
    inputs = list(inputs)
    results = pl.pallas_call(
        kernel,
        in_specs=[in_spec] * len(inputs),
        out_specs=[out_spec] * len(outputs),
        out_shape=outputs,
        scratch_shapes=list(scratch),
        compiler_params=pltpu.CompilerParams(vmem_limit_bytes=limit * MIB),
        cost_estimate=pl.CostEstimate(flops=flops, bytes_accessed=moved, transcendentals=0),
        name=name,
    )(*inputs)
    return list(results)


def body(sizes, blocks, pattern, occupied, ligand):
    n_aux, n_orb, n_ao = sizes
    aux_rows, _, nu_width = blocks.shape
    owners = n_aux * n_orb
    ni = NOCC // owners
    q_total = aux_rows * owners
    panel_width = occupied.shape[1]
    width = ligand.shape[1]
    bf16 = functools.partial(jax.ShapeDtypeStruct, dtype=jnp.bfloat16)
    f32 = functools.partial(jax.ShapeDtypeStruct, dtype=jnp.float32)

    across = [(a, a ^ 2) for a in range(n_aux)]
    swap = [(c, 1 - c) for c in range(n_ao)]
    pattern = jnp.swapaxes(pattern, 1, 2)
    masked, panel, part, orbitals = call(
        masked_kernel,
        "masked_blocks",
        (pltpu.with_memory_space_constraint(x, pltpu.HBM) for x in (pattern, blocks, occupied, ligand)),
        [bf16(blocks.shape), bf16(occupied.shape), bf16((NB // n_ao, panel_width)), bf16((NB // n_ao, width))],
        [
            pltpu.VMEM(blocks.shape, jnp.bfloat16),
            pltpu.SMEM(pattern.shape, pattern.dtype),
            pltpu.SemaphoreType.DMA((5,)),
        ],
        in_spec=pl.BlockSpec(memory_space=pltpu.HBM),
    )
    far_masked = lax.ppermute(masked, "aux", across)
    mine = lax.ppermute(part, "orb", swap)
    theirs = lax.ppermute(mine, "ao", swap)

    def square(messages):
        arrived = [messages[0]]
        for message, d in zip(messages[1:], (3, 2, 1)):
            moves = [
                (a * n_orb + o, (a ^ (d >> 1)) * n_orb + (o ^ (d & 1))) for a in range(n_aux) for o in range(n_orb)
            ]
            arrived.append(lax.ppermute(message, ("aux", "orb"), moves))
        return arrived

    work = 2 * NB * panel_width * nu_width * aux_rows
    messages = [bf16((aux_rows, ni, nu_width))] * 4
    turned, *own = call(
        own_kernel, "own_half", (panel, mine, theirs, masked), [bf16((4, ni, NB))] + messages, flops=work
    )
    own_here = square(own)
    value = call(
        density_kernel,
        "density_terms",
        (panel, mine, theirs, masked, turned, *own),
        [f32((aux_rows, 128))],
        [pltpu.VMEM(occupied.shape, jnp.bfloat16)],
        flops=work,
    )[0]
    value_there = lax.ppermute(value, "ao", swap)
    density = (value[:, 0] + value_there[:, 0]) / math.sqrt(NOCC)
    far = call(far_kernel, "far_half", (value, far_masked, turned), messages, flops=work)
    far_here = square(far)

    shape = (4 * aux_rows, ni, width)
    kept_and_given = [f32(shape), bf16(shape)]
    side = [bf16((ni // GROUP, nu_width, 4 * aux_rows * GROUP))]
    pair_work = 2 * shape[0] * ni * nu_width * width
    own_kept, own_given, own_rows = call(
        pair_and_turn_kernel,
        "own_pairs",
        (value_there, far[0], orbitals, *own_here),
        kept_and_given + side,
        flops=pair_work,
    )
    own_pairs = (own_kept, lax.ppermute(own_given, "ao", swap))
    far_kept, far_given = call(
        pair_kernel, "far_pairs", (value_there, own_rows, orbitals, *far_here), kept_and_given, flops=pair_work
    )
    far_pairs = (far_kept, lax.ppermute(far_given, "ao", swap))
    far_rows = call(turn_kernel, "far_turned", far_here, side)[0]

    result = (ni, nu_width, width)
    cross_terms = call(
        functools.partial(cross_kernel, 1.0 / math.sqrt(q_total)),
        "cross_terms",
        (own_rows, far_rows, *own_pairs, *far_pairs),
        [f32(result)],
        [pltpu.VMEM(result, jnp.float32), pltpu.SemaphoreType.DMA],
        limit=32,
        flops=32 * q_total * ni * nu_width * width,
        moved=18 * MIB,
        out_spec=pl.BlockSpec(memory_space=pltpu.HBM),
    )[0]
    return (density, cross_terms)


def plain_body(blocks, pattern, occupied, ligand):
    panels = lax.all_gather(occupied, "orb", axis=1, tiled=True)
    aux_rows = blocks.shape[0]
    nu_width = blocks.shape[2]
    nu_blocks = pattern.shape[2]
    opened = pattern[0].astype(jnp.bfloat16)
    masked = blocks.reshape(aux_rows, NBLK, BLK, nu_blocks, BLK) * opened[None, :, None, :, None]
    masked = masked.reshape(aux_rows, NB, nu_width)
    transformed = jnp.einsum(
        "qmn,mi->qin", masked, panels, preferred_element_type=jnp.float32
    ).astype(jnp.bfloat16)
    nu_start = lax.axis_index("ao") * nu_width
    own_rows = lax.dynamic_slice_in_dim(panels, nu_start, nu_width, 0)
    partial_value = jnp.einsum(
        "qin,ni->q", transformed, own_rows, preferred_element_type=jnp.float32
    )
    density = lax.psum(partial_value, "ao") / math.sqrt(NOCC)
    arrived = lax.all_to_all(transformed, ("aux", "orb"), split_axis=1, concat_axis=0, tiled=True)
    own_ligand = lax.dynamic_slice_in_dim(ligand, nu_start, nu_width, 0)
    pair_part = jnp.einsum("qin,nj->qij", arrived, own_ligand, preferred_element_type=jnp.float32)
    mixed_pairs = lax.psum(pair_part, "ao").astype(jnp.bfloat16)
    crossed = jnp.einsum("qin,qij->inj", arrived, mixed_pairs, preferred_element_type=jnp.float32)
    cross_terms = crossed / math.sqrt(arrived.shape[0])
    return (density, cross_terms)


def solution(mesh):
    sizes = (mesh.shape["aux"], mesh.shape["orb"], mesh.shape["ao"])
    kernels = sizes == (4, 2, 2)
    return jax.shard_map(
        functools.partial(body, sizes) if kernels else plain_body,
        mesh=mesh,
        in_specs=(
            P(("pose", "aux", "orb"), None, "ao"),
            P(("pose", "aux", "orb"), None, "ao"),
            P(None, "orb"),
            P(None, "pose"),
        ),
        out_specs=(P(("pose", "aux", "orb")), P(("pose", "aux", "orb"), "ao", None)),
        check_vma=False,
    )
```

```python
import functools
import math

import jax
import jax.numpy as jnp
from jax import lax
from jax.experimental import pallas as pl
from jax.experimental.pallas import tpu as pltpu
from jax.sharding import PartitionSpec as P

NOCC = 1024
BLK = 128
NBLK = 4
NB = 512
GROUP = 16
MIB = 1024 * 1024
VMEM = pl.BlockSpec(memory_space=pltpu.VMEM)


def masked_kernel(pattern, blocks, occupied, ligand, masked, panel, part, orbitals, held, opened, sems):
    aux_rows, _, nu_width = blocks.shape
    own = own_half_of(part.shape[0])
    moves = ((blocks, held), (pattern, opened), (occupied.at[own], part), (occupied, panel), (ligand.at[own], orbitals))
    copies = [pltpu.make_async_copy(source, target, sems.at[k]) for k, (source, target) in enumerate(moves)]
    for copy in copies:
        copy.start()
    copies[0].wait()
    copies[1].wait()
    for q in range(aux_rows):
        for m in range(NBLK):
            for n in range(nu_width // BLK):
                rows, columns = pl.ds(m * BLK, BLK), pl.ds(n * BLK, BLK)
                tile = held[q, rows, columns]
                masked[q, rows, columns] = jnp.where(opened[0, n, m] != 0, tile, jnp.zeros_like(tile))
    for copy in copies[2:]:
        copy.wait()


def own_half_of(length):
    return pl.ds(pl.multiple_of(lax.axis_index("ao") * length, length), length)


def half_into(outs, turned, masked):
    for d, out in enumerate(outs):
        for q in range(out.shape[0]):
            out[q] = jnp.dot(turned[d], masked[q], preferred_element_type=jnp.float32).astype(jnp.bfloat16)


def own_kernel(occupied, mine, theirs, masked, turned, *outs):
    aux, orb, ao = (lax.axis_index(name) for name in ("aux", "orb", "ao"))
    ni = turned.shape[1]
    here = 2 * (aux & 1) + orb
    place = lambda s: (4 - (here ^ s)) & 3
    near = orb == aux // 2

    @pl.when(near)
    def _():
        for s in range(turned.shape[0]):
            turned[place(s)] = occupied[:, s * ni : (s + 1) * ni].T

    @pl.when(jnp.logical_not(near))
    def _():
        depth = mine.shape[0]
        for e, rows in enumerate((mine, theirs)):
            first = pl.multiple_of((ao ^ e) * depth, depth)
            for s in range(turned.shape[0]):
                turned[place(s), :, pl.ds(first, depth)] = rows[:, s * ni : (s + 1) * ni].T

    half_into(outs, turned, masked)


def density_kernel(occupied, mine, theirs, masked, turned, *refs):
    messages, out, panel = refs[:-2], refs[-2], refs[-1]
    aux_rows, ni, nu_width = messages[0].shape
    depth = mine.shape[0]
    own = own_half_of(nu_width)
    near = lax.axis_index("orb") == lax.axis_index("aux") // 2

    @pl.when(near)
    def _():
        for e, rows in enumerate((mine, theirs)):
            panel[pl.ds(pl.multiple_of((lax.axis_index("ao") ^ e) * depth, depth), depth), :] = rows[...]

    @pl.when(jnp.logical_not(near))
    def _():
        panel[...] = occupied[...]

    totals = [0.0] * aux_rows
    for d, message in enumerate(messages):
        rows = turned[d, :, own].astype(jnp.float32)
        for q in range(aux_rows):
            totals[q] += jnp.sum(rows * message[q].astype(jnp.float32))
    for s in range(4):
        rows = panel[:, s * ni : (s + 1) * ni].T
        weights = panel[own, s * ni : (s + 1) * ni].T.astype(jnp.float32)
        for q in range(aux_rows):
            result = jnp.dot(rows, masked[q], preferred_element_type=jnp.float32).astype(jnp.bfloat16)
            totals[q] += jnp.sum(weights * result.astype(jnp.float32))
    for q in range(aux_rows):
        out[q : q + 1, :] = jnp.full((1, out.shape[1]), totals[q], jnp.float32)


def far_kernel(before, masked, turned, *outs):
    half_into(outs, turned, masked)


def pair_kernel(before, earlier, ligand, *refs):
    arrived, own, sent = refs[:-2], refs[-2], refs[-1]
    aux_rows, ni, nu_width = arrived[0].shape
    width = ligand.shape[1]
    for k, message in enumerate(arrived):
        part = jnp.dot(
            message[...].reshape(aux_rows * ni, nu_width), ligand[...], preferred_element_type=jnp.float32
        ).reshape(aux_rows, ni, width)
        own[k * aux_rows : (k + 1) * aux_rows] = part
        sent[k * aux_rows : (k + 1) * aux_rows] = part.astype(jnp.bfloat16)


def mark_kernel(*refs):
    refs[-1][...] = jnp.zeros_like(refs[-1])


def turn_kernel(*refs):
    messages, out = refs[:-1], refs[-1]
    nu_width = messages[0].shape[2]
    for g in range(out.shape[0]):
        here = pl.ds(g * GROUP, GROUP)
        out[g] = jnp.concatenate([x[:, here, :].reshape(-1, nu_width) for x in messages], axis=0).T


def pair_and_turn_kernel(before, earlier, ligand, *refs):
    pair_kernel(before, earlier, ligand, *refs[:-1])
    turn_kernel(*refs[:-3], refs[-1])


def cross_kernel(scale, near, far, *refs):
    pairs, (out, held, sem) = refs[:4], refs[4:]
    ni, _, width = out.shape

    def step(g, carry):
        here = pl.ds(pl.multiple_of(g * GROUP, GROUP), GROUP)
        turned = jnp.concatenate([near[g], far[g]], axis=1)
        summed = [pairs[j][:, here, :] + pairs[j + 1][:, here, :].astype(jnp.float32) for j in (0, 2)]
        summed = jnp.concatenate([(x * scale).astype(jnp.bfloat16) for x in summed], axis=0)
        row = lax.broadcasted_iota(jnp.int32, (1, GROUP, width), 1)
        zero = jnp.zeros_like(summed)
        for i in range(0, GROUP, 2):
            both = [jnp.where(row == i + e, summed, zero).reshape(-1, width) for e in (0, 1)]
            result = jnp.dot(turned, jnp.concatenate(both, axis=1), preferred_element_type=jnp.float32)
            held[g * GROUP + i] = result[:, :width]
            held[g * GROUP + i + 1] = result[:, width:]
            if i % 4 == 2:
                done = pl.ds(g * GROUP + i - 2, 4)
                pltpu.make_async_copy(held.at[done], out.at[done], sem).start()
        return carry

    lax.fori_loop(0, ni // GROUP, step, 0, unroll=4)
    pltpu.make_async_copy(held, out, sem).wait()


def call(kernel, name, inputs, outputs, scratch=(), limit=16, flops=0, moved=1 << 20, in_spec=VMEM, out_spec=VMEM):
    inputs = list(inputs)
    results = pl.pallas_call(
        kernel,
        in_specs=[in_spec] * len(inputs),
        out_specs=[out_spec] * len(outputs),
        out_shape=outputs,
        scratch_shapes=list(scratch),
        compiler_params=pltpu.CompilerParams(vmem_limit_bytes=limit * MIB),
        cost_estimate=pl.CostEstimate(flops=flops, bytes_accessed=moved, transcendentals=0),
        name=name,
    )(*inputs)
    return list(results)


def body(sizes, blocks, pattern, occupied, ligand):
    n_aux, n_orb, n_ao = sizes
    aux_rows, _, nu_width = blocks.shape
    owners = n_aux * n_orb
    ni = NOCC // owners
    q_total = aux_rows * owners
    panel_width = occupied.shape[1]
    width = ligand.shape[1]
    bf16 = functools.partial(jax.ShapeDtypeStruct, dtype=jnp.bfloat16)
    f32 = functools.partial(jax.ShapeDtypeStruct, dtype=jnp.float32)

    across = [(a, a ^ 2) for a in range(n_aux)]
    swap = [(c, 1 - c) for c in range(n_ao)]
    pattern = jnp.swapaxes(pattern, 1, 2)
    masked, panel, part, orbitals = call(
        masked_kernel,
        "masked_blocks",
        (pltpu.with_memory_space_constraint(x, pltpu.HBM) for x in (pattern, blocks, occupied, ligand)),
        [bf16(blocks.shape), bf16(occupied.shape), bf16((NB // n_ao, panel_width)), bf16((NB // n_ao, width))],
        [
            pltpu.VMEM(blocks.shape, jnp.bfloat16),
            pltpu.SMEM(pattern.shape, pattern.dtype),
            pltpu.SemaphoreType.DMA((5,)),
        ],
        in_spec=pl.BlockSpec(memory_space=pltpu.HBM),
    )
    far_masked = lax.ppermute(masked, "aux", across)
    mine = lax.ppermute(part, "orb", swap)
    theirs = lax.ppermute(mine, "ao", swap)

    def square(messages):
        arrived = [messages[0]]
        for message, d in zip(messages[1:], (3, 2, 1)):
            moves = [
                (a * n_orb + o, (a ^ (d >> 1)) * n_orb + (o ^ (d & 1))) for a in range(n_aux) for o in range(n_orb)
            ]
            arrived.append(lax.ppermute(message, ("aux", "orb"), moves))
        return arrived

    work = 2 * NB * panel_width * nu_width * aux_rows
    messages = [bf16((aux_rows, ni, nu_width))] * 4
    turned, *own = call(
        own_kernel, "own_half", (panel, mine, theirs, masked), [bf16((4, ni, NB))] + messages, flops=work
    )
    own_here = square(own)
    value = call(
        density_kernel,
        "density_terms",
        (panel, mine, theirs, masked, turned, *own),
        [f32((aux_rows, 128))],
        [pltpu.VMEM(occupied.shape, jnp.bfloat16)],
        flops=work,
    )[0]
    value_there = lax.ppermute(value, "ao", swap)
    density = (value[:, 0] + value_there[:, 0]) / math.sqrt(NOCC)
    far = call(far_kernel, "far_half", (value, far_masked, turned), messages, flops=work)
    far_here = square(far)

    shape = (4 * aux_rows, ni, width)
    kept_and_given = [f32(shape), bf16(shape)]
    side = [bf16((ni // GROUP, nu_width, 4 * aux_rows * GROUP))]
    pair_work = 2 * shape[0] * ni * nu_width * width
    own_kept, own_given, own_rows = call(
        pair_and_turn_kernel,
        "own_pairs",
        (value_there, far[0], orbitals, *own_here),
        kept_and_given + side,
        flops=pair_work,
    )
    own_pairs = (own_kept, lax.ppermute(own_given, "ao", swap))
    all_here = call(
        mark_kernel, "far_rows_here", far_here, [f32((8, 128))], flops=1 << 34, in_spec=pl.BlockSpec(memory_space=pl.ANY)
    )[0]
    far_kept, far_given = call(
        pair_kernel, "far_pairs", (all_here, own_pairs[1], orbitals, *far_here), kept_and_given, flops=pair_work
    )
    far_pairs = (far_kept, lax.ppermute(far_given, "ao", swap))
    far_rows = call(turn_kernel, "far_turned", far_here, side)[0]

    result = (ni, nu_width, width)
    cross_terms = call(
        functools.partial(cross_kernel, 1.0 / math.sqrt(q_total)),
        "cross_terms",
        (own_rows, far_rows, *own_pairs, *far_pairs),
        [f32(result)],
        [pltpu.VMEM(result, jnp.float32), pltpu.SemaphoreType.DMA],
        limit=32,
        flops=32 * q_total * ni * nu_width * width,
        moved=18 * MIB,
        out_spec=pl.BlockSpec(memory_space=pltpu.HBM),
    )[0]
    return (density, cross_terms)


def plain_body(blocks, pattern, occupied, ligand):
    panels = lax.all_gather(occupied, "orb", axis=1, tiled=True)
    aux_rows = blocks.shape[0]
    nu_width = blocks.shape[2]
    nu_blocks = pattern.shape[2]
    opened = pattern[0].astype(jnp.bfloat16)
    masked = blocks.reshape(aux_rows, NBLK, BLK, nu_blocks, BLK) * opened[None, :, None, :, None]
    masked = masked.reshape(aux_rows, NB, nu_width)
    transformed = jnp.einsum(
        "qmn,mi->qin", masked, panels, preferred_element_type=jnp.float32
    ).astype(jnp.bfloat16)
    nu_start = lax.axis_index("ao") * nu_width
    own_rows = lax.dynamic_slice_in_dim(panels, nu_start, nu_width, 0)
    partial_value = jnp.einsum(
        "qin,ni->q", transformed, own_rows, preferred_element_type=jnp.float32
    )
    density = lax.psum(partial_value, "ao") / math.sqrt(NOCC)
    arrived = lax.all_to_all(transformed, ("aux", "orb"), split_axis=1, concat_axis=0, tiled=True)
    own_ligand = lax.dynamic_slice_in_dim(ligand, nu_start, nu_width, 0)
    pair_part = jnp.einsum("qin,nj->qij", arrived, own_ligand, preferred_element_type=jnp.float32)
    mixed_pairs = lax.psum(pair_part, "ao").astype(jnp.bfloat16)
    crossed = jnp.einsum("qin,qij->inj", arrived, mixed_pairs, preferred_element_type=jnp.float32)
    cross_terms = crossed / math.sqrt(arrived.shape[0])
    return (density, cross_terms)


def solution(mesh):
    sizes = (mesh.shape["aux"], mesh.shape["orb"], mesh.shape["ao"])
    kernels = sizes == (4, 2, 2)
    return jax.shard_map(
        functools.partial(body, sizes) if kernels else plain_body,
        mesh=mesh,
        in_specs=(
            P(("pose", "aux", "orb"), None, "ao"),
            P(("pose", "aux", "orb"), None, "ao"),
            P(None, "orb"),
            P(None, "pose"),
        ),
        out_specs=(P(("pose", "aux", "orb")), P(("pose", "aux", "orb"), "ao", None)),
        check_vma=False,
    )
```

```python
import functools
import math

import jax
import jax.numpy as jnp
from jax import lax
from jax.experimental import pallas as pl
from jax.experimental.pallas import tpu as pltpu
from jax.sharding import PartitionSpec as P

NOCC = 1024
BLK = 128
NBLK = 4
NB = 512
GROUP = 16
MIB = 1024 * 1024
VMEM = pl.BlockSpec(memory_space=pltpu.VMEM)


def masked_kernel(pattern, blocks, occupied, masked, part, held, opened, sems):
    aux_rows, _, nu_width = blocks.shape
    moves = ((blocks, held), (pattern, opened), (occupied.at[own_half_of(part.shape[0])], part))
    copies = [pltpu.make_async_copy(source, target, sems.at[k]) for k, (source, target) in enumerate(moves)]
    for copy in copies:
        copy.start()
    copies[0].wait()
    copies[1].wait()
    for q in range(aux_rows):
        for m in range(NBLK):
            for n in range(nu_width // BLK):
                rows, columns = pl.ds(m * BLK, BLK), pl.ds(n * BLK, BLK)
                tile = held[q, rows, columns]
                masked[q, rows, columns] = jnp.where(opened[0, n, m] != 0, tile, jnp.zeros_like(tile))
    for copy in copies[2:]:
        copy.wait()


def own_half_of(length):
    return pl.ds(pl.multiple_of(lax.axis_index("ao") * length, length), length)


def panel_kernel(occupied, ligand, panel, orbitals, sems):
    moves = ((occupied, panel), (ligand.at[own_half_of(orbitals.shape[0])], orbitals))
    copies = [pltpu.make_async_copy(source, target, sems.at[k]) for k, (source, target) in enumerate(moves)]
    for copy in copies:
        copy.start()
    for copy in copies:
        copy.wait()


def half_into(outs, turned, masked):
    for d, out in enumerate(outs):
        for q in range(out.shape[0]):
            out[q] = jnp.dot(turned[d], masked[q], preferred_element_type=jnp.float32).astype(jnp.bfloat16)


def own_kernel(occupied, mine, theirs, masked, turned, *outs):
    aux, orb, ao = (lax.axis_index(name) for name in ("aux", "orb", "ao"))
    ni = turned.shape[1]
    here = 2 * (aux & 1) + orb
    place = lambda s: (4 - (here ^ s)) & 3
    near = orb == aux // 2

    @pl.when(near)
    def _():
        for s in range(turned.shape[0]):
            turned[place(s)] = occupied[:, s * ni : (s + 1) * ni].T

    @pl.when(jnp.logical_not(near))
    def _():
        depth = mine.shape[0]
        for e, rows in enumerate((mine, theirs)):
            first = pl.multiple_of((ao ^ e) * depth, depth)
            for s in range(turned.shape[0]):
                turned[place(s), :, pl.ds(first, depth)] = rows[:, s * ni : (s + 1) * ni].T

    half_into(outs, turned, masked)


def density_kernel(occupied, mine, theirs, masked, turned, *refs):
    messages, out, panel = refs[:-2], refs[-2], refs[-1]
    aux_rows, ni, nu_width = messages[0].shape
    depth = mine.shape[0]
    own = own_half_of(nu_width)
    near = lax.axis_index("orb") == lax.axis_index("aux") // 2

    @pl.when(near)
    def _():
        for e, rows in enumerate((mine, theirs)):
            panel[pl.ds(pl.multiple_of((lax.axis_index("ao") ^ e) * depth, depth), depth), :] = rows[...]

    @pl.when(jnp.logical_not(near))
    def _():
        panel[...] = occupied[...]

    totals = [0.0] * aux_rows
    for d, message in enumerate(messages):
        rows = turned[d, :, own].astype(jnp.float32)
        for q in range(aux_rows):
            totals[q] += jnp.sum(rows * message[q].astype(jnp.float32))
    for s in range(4):
        rows = panel[:, s * ni : (s + 1) * ni].T
        weights = panel[own, s * ni : (s + 1) * ni].T.astype(jnp.float32)
        for q in range(aux_rows):
            result = jnp.dot(rows, masked[q], preferred_element_type=jnp.float32).astype(jnp.bfloat16)
            totals[q] += jnp.sum(weights * result.astype(jnp.float32))
    for q in range(aux_rows):
        out[q : q + 1, :] = jnp.full((1, out.shape[1]), totals[q], jnp.float32)


def far_kernel(before, masked, turned, *outs):
    half_into(outs, turned, masked)


def pair_kernel(before, earlier, ligand, *refs):
    arrived, own, sent = refs[:-2], refs[-2], refs[-1]
    aux_rows, ni, nu_width = arrived[0].shape
    width = ligand.shape[1]
    for k, message in enumerate(arrived):
        part = jnp.dot(
            message[...].reshape(aux_rows * ni, nu_width), ligand[...], preferred_element_type=jnp.float32
        ).reshape(aux_rows, ni, width)
        own[k * aux_rows : (k + 1) * aux_rows] = part
        sent[k * aux_rows : (k + 1) * aux_rows] = part.astype(jnp.bfloat16)


def mark_kernel(*refs):
    refs[-1][...] = jnp.zeros_like(refs[-1])


def turn_kernel(*refs):
    messages, out = refs[:-1], refs[-1]
    nu_width = messages[0].shape[2]
    for g in range(out.shape[0]):
        here = pl.ds(g * GROUP, GROUP)
        out[g] = jnp.concatenate([x[:, here, :].reshape(-1, nu_width) for x in messages], axis=0).T


def pair_and_turn_kernel(before, earlier, ligand, *refs):
    pair_kernel(before, earlier, ligand, *refs[:-1])
    turn_kernel(*refs[:-3], refs[-1])


def cross_kernel(scale, near, far, *refs):
    pairs, (out, held, sem) = refs[:4], refs[4:]
    ni, _, width = out.shape

    def step(g, carry):
        here = pl.ds(pl.multiple_of(g * GROUP, GROUP), GROUP)
        turned = jnp.concatenate([near[g], far[g]], axis=1)
        summed = [pairs[j][:, here, :] + pairs[j + 1][:, here, :].astype(jnp.float32) for j in (0, 2)]
        summed = jnp.concatenate([(x * scale).astype(jnp.bfloat16) for x in summed], axis=0)
        row = lax.broadcasted_iota(jnp.int32, (1, GROUP, width), 1)
        zero = jnp.zeros_like(summed)
        for i in range(0, GROUP, 2):
            both = [jnp.where(row == i + e, summed, zero).reshape(-1, width) for e in (0, 1)]
            result = jnp.dot(turned, jnp.concatenate(both, axis=1), preferred_element_type=jnp.float32)
            held[g * GROUP + i] = result[:, :width]
            held[g * GROUP + i + 1] = result[:, width:]
            if i % 4 == 2:
                done = pl.ds(g * GROUP + i - 2, 4)
                pltpu.make_async_copy(held.at[done], out.at[done], sem).start()
        return carry

    lax.fori_loop(0, ni // GROUP, step, 0, unroll=4)
    pltpu.make_async_copy(held, out, sem).wait()


def call(kernel, name, inputs, outputs, scratch=(), limit=16, flops=0, moved=1 << 20, in_spec=VMEM, out_spec=VMEM):
    inputs = list(inputs)
    results = pl.pallas_call(
        kernel,
        in_specs=[in_spec] * len(inputs),
        out_specs=[out_spec] * len(outputs),
        out_shape=outputs,
        scratch_shapes=list(scratch),
        compiler_params=pltpu.CompilerParams(vmem_limit_bytes=limit * MIB),
        cost_estimate=pl.CostEstimate(flops=flops, bytes_accessed=moved, transcendentals=0),
        name=name,
    )(*inputs)
    return list(results)


def body(sizes, blocks, pattern, occupied, ligand):
    n_aux, n_orb, n_ao = sizes
    aux_rows, _, nu_width = blocks.shape
    owners = n_aux * n_orb
    ni = NOCC // owners
    q_total = aux_rows * owners
    panel_width = occupied.shape[1]
    width = ligand.shape[1]
    bf16 = functools.partial(jax.ShapeDtypeStruct, dtype=jnp.bfloat16)
    f32 = functools.partial(jax.ShapeDtypeStruct, dtype=jnp.float32)

    across = [(a, a ^ 2) for a in range(n_aux)]
    swap = [(c, 1 - c) for c in range(n_ao)]
    pattern = jnp.swapaxes(pattern, 1, 2)
    in_hbm = functools.partial(pltpu.with_memory_space_constraint, memory_space=pltpu.HBM)
    hbm = pl.BlockSpec(memory_space=pltpu.HBM)
    masked, part = call(
        masked_kernel,
        "masked_blocks",
        (in_hbm(pattern), in_hbm(blocks), in_hbm(occupied)),
        [bf16(blocks.shape), bf16((NB // n_ao, panel_width))],
        [
            pltpu.VMEM(blocks.shape, jnp.bfloat16),
            pltpu.SMEM(pattern.shape, pattern.dtype),
            pltpu.SemaphoreType.DMA((3,)),
        ],
        in_spec=hbm,
    )
    far_masked = lax.ppermute(masked, "aux", across)
    mine = lax.ppermute(part, "orb", swap)
    theirs = lax.ppermute(mine, "ao", swap)
    panel, orbitals = call(
        panel_kernel,
        "own_panel",
        (in_hbm(occupied), in_hbm(ligand)),
        [bf16(occupied.shape), bf16((NB // n_ao, width))],
        [pltpu.SemaphoreType.DMA((2,))],
        in_spec=hbm,
    )

    def square(messages):
        arrived = [messages[0]]
        for message, d in zip(messages[1:], (3, 2, 1)):
            moves = [
                (a * n_orb + o, (a ^ (d >> 1)) * n_orb + (o ^ (d & 1))) for a in range(n_aux) for o in range(n_orb)
            ]
            arrived.append(lax.ppermute(message, ("aux", "orb"), moves))
        return arrived

    work = 2 * NB * panel_width * nu_width * aux_rows
    messages = [bf16((aux_rows, ni, nu_width))] * 4
    turned, *own = call(
        own_kernel, "own_half", (panel, mine, theirs, masked), [bf16((4, ni, NB))] + messages, flops=work
    )
    own_here = square(own)
    value = call(
        density_kernel,
        "density_terms",
        (panel, mine, theirs, masked, turned, *own),
        [f32((aux_rows, 128))],
        [pltpu.VMEM(occupied.shape, jnp.bfloat16)],
        flops=work,
    )[0]
    value_there = lax.ppermute(value, "ao", swap)
    density = (value[:, 0] + value_there[:, 0]) / math.sqrt(NOCC)
    far = call(far_kernel, "far_half", (value, far_masked, turned), messages, flops=work)
    far_here = square(far)

    shape = (4 * aux_rows, ni, width)
    kept_and_given = [f32(shape), bf16(shape)]
    side = [bf16((ni // GROUP, nu_width, 4 * aux_rows * GROUP))]
    pair_work = 2 * shape[0] * ni * nu_width * width
    own_kept, own_given, own_rows = call(
        pair_and_turn_kernel,
        "own_pairs",
        (value_there, far[0], orbitals, *own_here),
        kept_and_given + side,
        flops=pair_work,
    )
    own_pairs = (own_kept, lax.ppermute(own_given, "ao", swap))
    all_here = call(
        mark_kernel, "far_rows_here", far_here, [f32((8, 128))], flops=1 << 34, in_spec=pl.BlockSpec(memory_space=pl.ANY)
    )[0]
    far_kept, far_given = call(
        pair_kernel, "far_pairs", (all_here, own_pairs[1], orbitals, *far_here), kept_and_given, flops=pair_work
    )
    far_pairs = (far_kept, lax.ppermute(far_given, "ao", swap))
    far_rows = call(turn_kernel, "far_turned", far_here, side)[0]

    result = (ni, nu_width, width)
    cross_terms = call(
        functools.partial(cross_kernel, 1.0 / math.sqrt(q_total)),
        "cross_terms",
        (own_rows, far_rows, *own_pairs, *far_pairs),
        [f32(result)],
        [pltpu.VMEM(result, jnp.float32), pltpu.SemaphoreType.DMA],
        limit=32,
        flops=32 * q_total * ni * nu_width * width,
        moved=18 * MIB,
        out_spec=pl.BlockSpec(memory_space=pltpu.HBM),
    )[0]
    return (density, cross_terms)


def plain_body(blocks, pattern, occupied, ligand):
    panels = lax.all_gather(occupied, "orb", axis=1, tiled=True)
    aux_rows = blocks.shape[0]
    nu_width = blocks.shape[2]
    nu_blocks = pattern.shape[2]
    opened = pattern[0].astype(jnp.bfloat16)
    masked = blocks.reshape(aux_rows, NBLK, BLK, nu_blocks, BLK) * opened[None, :, None, :, None]
    masked = masked.reshape(aux_rows, NB, nu_width)
    transformed = jnp.einsum(
        "qmn,mi->qin", masked, panels, preferred_element_type=jnp.float32
    ).astype(jnp.bfloat16)
    nu_start = lax.axis_index("ao") * nu_width
    own_rows = lax.dynamic_slice_in_dim(panels, nu_start, nu_width, 0)
    partial_value = jnp.einsum(
        "qin,ni->q", transformed, own_rows, preferred_element_type=jnp.float32
    )
    density = lax.psum(partial_value, "ao") / math.sqrt(NOCC)
    arrived = lax.all_to_all(transformed, ("aux", "orb"), split_axis=1, concat_axis=0, tiled=True)
    own_ligand = lax.dynamic_slice_in_dim(ligand, nu_start, nu_width, 0)
    pair_part = jnp.einsum("qin,nj->qij", arrived, own_ligand, preferred_element_type=jnp.float32)
    mixed_pairs = lax.psum(pair_part, "ao").astype(jnp.bfloat16)
    crossed = jnp.einsum("qin,qij->inj", arrived, mixed_pairs, preferred_element_type=jnp.float32)
    cross_terms = crossed / math.sqrt(arrived.shape[0])
    return (density, cross_terms)


def solution(mesh):
    sizes = (mesh.shape["aux"], mesh.shape["orb"], mesh.shape["ao"])
    kernels = sizes == (4, 2, 2)
    return jax.shard_map(
        functools.partial(body, sizes) if kernels else plain_body,
        mesh=mesh,
        in_specs=(
            P(("pose", "aux", "orb"), None, "ao"),
            P(("pose", "aux", "orb"), None, "ao"),
            P(None, "orb"),
            P(None, "pose"),
        ),
        out_specs=(P(("pose", "aux", "orb")), P(("pose", "aux", "orb"), "ao", None)),
        check_vma=False,
    )
```

```python
import functools
import math

import jax
import jax.numpy as jnp
from jax import lax
from jax.experimental import pallas as pl
from jax.experimental.pallas import tpu as pltpu
from jax.sharding import PartitionSpec as P

NOCC = 1024
BLK = 128
NBLK = 4
NB = 512
GROUP = 16
MIB = 1024 * 1024
VMEM = pl.BlockSpec(memory_space=pltpu.VMEM)


def masked_kernel(pattern, blocks, occupied, masked, part, held, opened, sems):
    aux_rows, _, nu_width = blocks.shape
    moves = ((blocks, held), (pattern, opened), (occupied.at[own_half_of(part.shape[0])], part))
    copies = [pltpu.make_async_copy(source, target, sems.at[k]) for k, (source, target) in enumerate(moves)]
    for copy in copies:
        copy.start()
    copies[0].wait()
    copies[1].wait()
    for q in range(aux_rows):
        for m in range(NBLK):
            for n in range(nu_width // BLK):
                rows, columns = pl.ds(m * BLK, BLK), pl.ds(n * BLK, BLK)
                tile = held[q, rows, columns]
                masked[q, rows, columns] = jnp.where(opened[0, n, m] != 0, tile, jnp.zeros_like(tile))
    for copy in copies[2:]:
        copy.wait()


def own_half_of(length):
    return pl.ds(pl.multiple_of(lax.axis_index("ao") * length, length), length)


def panel_kernel(occupied, ligand, panel, orbitals, sems):
    moves = ((occupied, panel), (ligand.at[own_half_of(orbitals.shape[0])], orbitals))
    copies = [pltpu.make_async_copy(source, target, sems.at[k]) for k, (source, target) in enumerate(moves)]
    for copy in copies:
        copy.start()
    for copy in copies:
        copy.wait()


def half_into(outs, turned, masked):
    for d, out in enumerate(outs):
        for q in range(out.shape[0]):
            out[q] = jnp.dot(turned[d], masked[q], preferred_element_type=jnp.float32).astype(jnp.bfloat16)


def own_kernel(occupied, mine, theirs, masked, turned, *outs):
    aux, orb, ao = (lax.axis_index(name) for name in ("aux", "orb", "ao"))
    ni = turned.shape[1]
    here = 2 * (aux & 1) + orb
    place = lambda s: (4 - (here ^ s)) & 3
    near = orb == aux // 2

    @pl.when(near)
    def _():
        for s in range(turned.shape[0]):
            turned[place(s)] = occupied[:, s * ni : (s + 1) * ni].T

    @pl.when(jnp.logical_not(near))
    def _():
        depth = mine.shape[0]
        for e, rows in enumerate((mine, theirs)):
            first = pl.multiple_of((ao ^ e) * depth, depth)
            for s in range(turned.shape[0]):
                turned[place(s), :, pl.ds(first, depth)] = rows[:, s * ni : (s + 1) * ni].T

    half_into(outs, turned, masked)


def density_kernel(occupied, mine, theirs, masked, turned, *refs):
    messages, out, panel = refs[:-2], refs[-2], refs[-1]
    aux_rows, ni, nu_width = messages[0].shape
    depth = mine.shape[0]
    own = own_half_of(nu_width)
    near = lax.axis_index("orb") == lax.axis_index("aux") // 2

    @pl.when(near)
    def _():
        for e, rows in enumerate((mine, theirs)):
            panel[pl.ds(pl.multiple_of((lax.axis_index("ao") ^ e) * depth, depth), depth), :] = rows[...]

    @pl.when(jnp.logical_not(near))
    def _():
        panel[...] = occupied[...]

    totals = [0.0] * aux_rows
    for d, message in enumerate(messages):
        rows = turned[d, :, own].astype(jnp.float32)
        for q in range(aux_rows):
            totals[q] += jnp.sum(rows * message[q].astype(jnp.float32))
    for s in range(4):
        rows = panel[:, s * ni : (s + 1) * ni].T
        weights = panel[own, s * ni : (s + 1) * ni].T.astype(jnp.float32)
        for q in range(aux_rows):
            result = jnp.dot(rows, masked[q], preferred_element_type=jnp.float32).astype(jnp.bfloat16)
            totals[q] += jnp.sum(weights * result.astype(jnp.float32))
    for q in range(aux_rows):
        out[q : q + 1, :] = jnp.full((1, out.shape[1]), totals[q], jnp.float32)


def far_kernel(before, masked, turned, *outs):
    half_into(outs, turned, masked)


def pair_kernel(before, earlier, ligand, *refs):
    arrived, own, sent = refs[:-2], refs[-2], refs[-1]
    aux_rows, ni, nu_width = arrived[0].shape
    width = ligand.shape[1]
    for k, message in enumerate(arrived):
        part = jnp.dot(
            message[...].reshape(aux_rows * ni, nu_width), ligand[...], preferred_element_type=jnp.float32
        ).reshape(aux_rows, ni, width)
        own[k * aux_rows : (k + 1) * aux_rows] = part
        sent[k * aux_rows : (k + 1) * aux_rows] = part.astype(jnp.bfloat16)


def mark_kernel(*refs):
    refs[-1][...] = jnp.zeros_like(refs[-1])


def turn_kernel(*refs):
    messages, out = refs[:-1], refs[-1]
    nu_width = messages[0].shape[2]
    for g in range(out.shape[0]):
        here = pl.ds(g * GROUP, GROUP)
        out[g] = jnp.concatenate([x[:, here, :].reshape(-1, nu_width) for x in messages], axis=0).T


def pair_and_turn_kernel(before, earlier, ligand, *refs):
    pair_kernel(before, earlier, ligand, *refs[:-1])
    turn_kernel(*refs[:-3], refs[-1])


def cross_kernel(scale, near, far, *refs):
    pairs, (out, held, sem) = refs[:4], refs[4:]
    ni, _, width = out.shape

    def step(g, carry):
        here = pl.ds(pl.multiple_of(g * GROUP, GROUP), GROUP)
        turned = jnp.concatenate([near[g], far[g]], axis=1)
        summed = [pairs[j][:, here, :] + pairs[j + 1][:, here, :].astype(jnp.float32) for j in (0, 2)]
        summed = jnp.concatenate([(x * scale).astype(jnp.bfloat16) for x in summed], axis=0)
        row = lax.broadcasted_iota(jnp.int32, (1, GROUP, width), 1)
        zero = jnp.zeros_like(summed)
        for i in range(0, GROUP, 2):
            both = [jnp.where(row == i + e, summed, zero).reshape(-1, width) for e in (0, 1)]
            result = jnp.dot(turned, jnp.concatenate(both, axis=1), preferred_element_type=jnp.float32)
            held[g * GROUP + i] = result[:, :width]
            held[g * GROUP + i + 1] = result[:, width:]
            if i % 4 == 2:
                done = pl.ds(g * GROUP + i - 2, 4)
                pltpu.make_async_copy(held.at[done], out.at[done], sem).start()
        return carry

    lax.fori_loop(0, ni // GROUP, step, 0, unroll=4)
    pltpu.make_async_copy(held, out, sem).wait()


def call(kernel, name, inputs, outputs, scratch=(), limit=16, flops=0, moved=1 << 20, in_spec=VMEM, out_spec=VMEM):
    inputs = list(inputs)
    results = pl.pallas_call(
        kernel,
        in_specs=[in_spec] * len(inputs),
        out_specs=[out_spec] * len(outputs),
        out_shape=outputs,
        scratch_shapes=list(scratch),
        compiler_params=pltpu.CompilerParams(vmem_limit_bytes=limit * MIB),
        cost_estimate=pl.CostEstimate(flops=flops, bytes_accessed=moved, transcendentals=0),
        name=name,
    )(*inputs)
    return list(results)


def body(sizes, blocks, pattern, occupied, ligand):
    n_aux, n_orb, n_ao = sizes
    aux_rows, _, nu_width = blocks.shape
    owners = n_aux * n_orb
    ni = NOCC // owners
    q_total = aux_rows * owners
    panel_width = occupied.shape[1]
    width = ligand.shape[1]
    bf16 = functools.partial(jax.ShapeDtypeStruct, dtype=jnp.bfloat16)
    f32 = functools.partial(jax.ShapeDtypeStruct, dtype=jnp.float32)

    across = [(a, n_aux - 1 - a) for a in range(n_aux)]
    swap = [(c, 1 - c) for c in range(n_ao)]
    pattern = jnp.swapaxes(pattern, 1, 2)
    in_hbm = functools.partial(pltpu.with_memory_space_constraint, memory_space=pltpu.HBM)
    hbm = pl.BlockSpec(memory_space=pltpu.HBM)
    masked, part = call(
        masked_kernel,
        "masked_blocks",
        (in_hbm(pattern), in_hbm(blocks), in_hbm(occupied)),
        [bf16(blocks.shape), bf16((NB // n_ao, panel_width))],
        [
            pltpu.VMEM(blocks.shape, jnp.bfloat16),
            pltpu.SMEM(pattern.shape, pattern.dtype),
            pltpu.SemaphoreType.DMA((3,)),
        ],
        in_spec=hbm,
    )
    far_masked = lax.ppermute(masked, "aux", across)
    mine = lax.ppermute(part, "orb", swap)
    theirs = lax.ppermute(mine, "ao", swap)
    panel, orbitals = call(
        panel_kernel,
        "own_panel",
        (in_hbm(occupied), in_hbm(ligand)),
        [bf16(occupied.shape), bf16((NB // n_ao, width))],
        [pltpu.SemaphoreType.DMA((2,))],
        in_spec=hbm,
    )

    def square(messages):
        arrived = [messages[0]]
        for message, d in zip(messages[1:], (3, 2, 1)):
            moves = [
                (a * n_orb + o, (a ^ (d >> 1)) * n_orb + (o ^ (d & 1))) for a in range(n_aux) for o in range(n_orb)
            ]
            arrived.append(lax.ppermute(message, ("aux", "orb"), moves))
        return arrived

    work = 2 * NB * panel_width * nu_width * aux_rows
    messages = [bf16((aux_rows, ni, nu_width))] * 4
    turned, *own = call(
        own_kernel, "own_half", (panel, mine, theirs, masked), [bf16((4, ni, NB))] + messages, flops=work
    )
    own_here = square(own)
    value = call(
        density_kernel,
        "density_terms",
        (panel, mine, theirs, masked, turned, *own),
        [f32((aux_rows, 128))],
        [pltpu.VMEM(occupied.shape, jnp.bfloat16)],
        flops=work,
    )[0]
    value_there = lax.ppermute(value, "ao", swap)
    density = (value[:, 0] + value_there[:, 0]) / math.sqrt(NOCC)
    far = call(far_kernel, "far_half", (value, far_masked, turned), messages, flops=work)
    far_here = square(far)

    shape = (4 * aux_rows, ni, width)
    kept_and_given = [f32(shape), bf16(shape)]
    side = [bf16((ni // GROUP, nu_width, 4 * aux_rows * GROUP))]
    pair_work = 2 * shape[0] * ni * nu_width * width
    own_kept, own_given, own_rows = call(
        pair_and_turn_kernel,
        "own_pairs",
        (value_there, far[0], orbitals, *own_here),
        kept_and_given + side,
        flops=pair_work,
    )
    own_pairs = (own_kept, lax.ppermute(own_given, "ao", swap))
    all_here = call(
        mark_kernel, "far_rows_here", far_here, [f32((8, 128))], flops=1 << 34, in_spec=pl.BlockSpec(memory_space=pl.ANY)
    )[0]
    far_kept, far_given = call(
        pair_kernel, "far_pairs", (all_here, own_pairs[1], orbitals, *far_here), kept_and_given, flops=pair_work
    )
    far_pairs = (far_kept, lax.ppermute(far_given, "ao", swap))
    far_rows = call(turn_kernel, "far_turned", far_here, side)[0]

    result = (ni, nu_width, width)
    cross_terms = call(
        functools.partial(cross_kernel, 1.0 / math.sqrt(q_total)),
        "cross_terms",
        (own_rows, far_rows, *own_pairs, *far_pairs),
        [f32(result)],
        [pltpu.VMEM(result, jnp.float32), pltpu.SemaphoreType.DMA],
        limit=32,
        flops=32 * q_total * ni * nu_width * width,
        moved=18 * MIB,
        out_spec=pl.BlockSpec(memory_space=pltpu.HBM),
    )[0]
    return (density, cross_terms)


def plain_body(blocks, pattern, occupied, ligand):
    panels = lax.all_gather(occupied, "orb", axis=1, tiled=True)
    aux_rows = blocks.shape[0]
    nu_width = blocks.shape[2]
    nu_blocks = pattern.shape[2]
    opened = pattern[0].astype(jnp.bfloat16)
    masked = blocks.reshape(aux_rows, NBLK, BLK, nu_blocks, BLK) * opened[None, :, None, :, None]
    masked = masked.reshape(aux_rows, NB, nu_width)
    transformed = jnp.einsum(
        "qmn,mi->qin", masked, panels, preferred_element_type=jnp.float32
    ).astype(jnp.bfloat16)
    nu_start = lax.axis_index("ao") * nu_width
    own_rows = lax.dynamic_slice_in_dim(panels, nu_start, nu_width, 0)
    partial_value = jnp.einsum(
        "qin,ni->q", transformed, own_rows, preferred_element_type=jnp.float32
    )
    density = lax.psum(partial_value, "ao") / math.sqrt(NOCC)
    arrived = lax.all_to_all(transformed, ("aux", "orb"), split_axis=1, concat_axis=0, tiled=True)
    own_ligand = lax.dynamic_slice_in_dim(ligand, nu_start, nu_width, 0)
    pair_part = jnp.einsum("qin,nj->qij", arrived, own_ligand, preferred_element_type=jnp.float32)
    mixed_pairs = lax.psum(pair_part, "ao").astype(jnp.bfloat16)
    crossed = jnp.einsum("qin,qij->inj", arrived, mixed_pairs, preferred_element_type=jnp.float32)
    cross_terms = crossed / math.sqrt(arrived.shape[0])
    return (density, cross_terms)


def solution(mesh):
    sizes = (mesh.shape["aux"], mesh.shape["orb"], mesh.shape["ao"])
    kernels = sizes == (4, 2, 2)
    return jax.shard_map(
        functools.partial(body, sizes) if kernels else plain_body,
        mesh=mesh,
        in_specs=(
            P(("pose", "aux", "orb"), None, "ao"),
            P(("pose", "aux", "orb"), None, "ao"),
            P(None, "orb"),
            P(None, "pose"),
        ),
        out_specs=(P(("pose", "aux", "orb")), P(("pose", "aux", "orb"), "ao", None)),
        check_vma=False,
    )
```

```python
import functools
import math

import jax
import jax.numpy as jnp
from jax import lax
from jax.experimental import pallas as pl
from jax.experimental.pallas import tpu as pltpu
from jax.sharding import PartitionSpec as P

NOCC = 1024
BLK = 128
NBLK = 4
NB = 512
GROUP = 16
MIB = 1024 * 1024
VMEM = pl.BlockSpec(memory_space=pltpu.VMEM)


def masked_kernel(pattern, blocks, occupied, masked, part, held, opened, sems):
    aux_rows, _, nu_width = blocks.shape
    moves = ((blocks, held), (pattern, opened), (occupied.at[own_half_of(part.shape[0])], part))
    copies = [pltpu.make_async_copy(source, target, sems.at[k]) for k, (source, target) in enumerate(moves)]
    for copy in copies:
        copy.start()
    copies[0].wait()
    copies[1].wait()
    for q in range(aux_rows):
        for m in range(NBLK):
            for n in range(nu_width // BLK):
                rows, columns = pl.ds(m * BLK, BLK), pl.ds(n * BLK, BLK)
                tile = held[q, rows, columns]
                masked[q, rows, columns] = jnp.where(opened[0, n, m] != 0, tile, jnp.zeros_like(tile))
    for copy in copies[2:]:
        copy.wait()


def own_half_of(length):
    return pl.ds(pl.multiple_of(lax.axis_index("ao") * length, length), length)


def panel_kernel(occupied, ligand, panel, orbitals, sems):
    moves = ((occupied, panel), (ligand.at[own_half_of(orbitals.shape[0])], orbitals))
    copies = [pltpu.make_async_copy(source, target, sems.at[k]) for k, (source, target) in enumerate(moves)]
    for copy in copies:
        copy.start()
    for copy in copies:
        copy.wait()


def half_into(outs, turned, masked):
    for d, out in enumerate(outs):
        for q in range(out.shape[0]):
            out[q] = jnp.dot(turned[d], masked[q], preferred_element_type=jnp.float32).astype(jnp.bfloat16)


def own_kernel(occupied, mine, theirs, masked, turned, *outs):
    aux, orb, ao = (lax.axis_index(name) for name in ("aux", "orb", "ao"))
    ni = turned.shape[1]
    here = 2 * (aux & 1) + orb
    place = lambda s: (here ^ s) ^ ((here ^ s) >> 1)
    near = orb == aux // 2

    @pl.when(near)
    def _():
        for s in range(turned.shape[0]):
            turned[place(s)] = occupied[:, s * ni : (s + 1) * ni].T

    @pl.when(jnp.logical_not(near))
    def _():
        depth = mine.shape[0]
        for e, rows in enumerate((mine, theirs)):
            first = pl.multiple_of((ao ^ e) * depth, depth)
            for s in range(turned.shape[0]):
                turned[place(s), :, pl.ds(first, depth)] = rows[:, s * ni : (s + 1) * ni].T

    half_into(outs, turned, masked)


def density_kernel(occupied, mine, theirs, masked, turned, *refs):
    messages, out, panel = refs[:-2], refs[-2], refs[-1]
    aux_rows, ni, nu_width = messages[0].shape
    depth = mine.shape[0]
    own = own_half_of(nu_width)
    near = lax.axis_index("orb") == lax.axis_index("aux") // 2

    @pl.when(near)
    def _():
        for e, rows in enumerate((mine, theirs)):
            panel[pl.ds(pl.multiple_of((lax.axis_index("ao") ^ e) * depth, depth), depth), :] = rows[...]

    @pl.when(jnp.logical_not(near))
    def _():
        panel[...] = occupied[...]

    totals = [0.0] * aux_rows
    for d, message in enumerate(messages):
        rows = turned[d, :, own].astype(jnp.float32)
        for q in range(aux_rows):
            totals[q] += jnp.sum(rows * message[q].astype(jnp.float32))
    for s in range(4):
        rows = panel[:, s * ni : (s + 1) * ni].T
        weights = panel[own, s * ni : (s + 1) * ni].T.astype(jnp.float32)
        for q in range(aux_rows):
            result = jnp.dot(rows, masked[q], preferred_element_type=jnp.float32).astype(jnp.bfloat16)
            totals[q] += jnp.sum(weights * result.astype(jnp.float32))
    for q in range(aux_rows):
        out[q : q + 1, :] = jnp.full((1, out.shape[1]), totals[q], jnp.float32)


def far_kernel(before, masked, turned, *outs):
    half_into(outs, turned, masked)


def pair_kernel(before, earlier, ligand, *refs):
    arrived, own, sent = refs[:-2], refs[-2], refs[-1]
    aux_rows, ni, nu_width = arrived[0].shape
    width = ligand.shape[1]
    for k, message in enumerate(arrived):
        part = jnp.dot(
            message[...].reshape(aux_rows * ni, nu_width), ligand[...], preferred_element_type=jnp.float32
        ).reshape(aux_rows, ni, width)
        own[k * aux_rows : (k + 1) * aux_rows] = part
        sent[k * aux_rows : (k + 1) * aux_rows] = part.astype(jnp.bfloat16)


def mark_kernel(*refs):
    refs[-1][...] = jnp.zeros_like(refs[-1])


def turn_kernel(*refs):
    messages, out = refs[:-1], refs[-1]
    nu_width = messages[0].shape[2]
    for g in range(out.shape[0]):
        here = pl.ds(g * GROUP, GROUP)
        out[g] = jnp.concatenate([x[:, here, :].reshape(-1, nu_width) for x in messages], axis=0).T


def pair_and_turn_kernel(before, earlier, ligand, *refs):
    pair_kernel(before, earlier, ligand, *refs[:-1])
    turn_kernel(*refs[:-3], refs[-1])


def cross_kernel(scale, near, far, *refs):
    pairs, (out, held, sem) = refs[:4], refs[4:]
    ni, _, width = out.shape

    def step(g, carry):
        here = pl.ds(pl.multiple_of(g * GROUP, GROUP), GROUP)
        turned = jnp.concatenate([near[g], far[g]], axis=1)
        summed = [pairs[j][:, here, :] + pairs[j + 1][:, here, :].astype(jnp.float32) for j in (0, 2)]
        summed = jnp.concatenate([(x * scale).astype(jnp.bfloat16) for x in summed], axis=0)
        row = lax.broadcasted_iota(jnp.int32, (1, GROUP, width), 1)
        zero = jnp.zeros_like(summed)
        for i in range(0, GROUP, 2):
            both = [jnp.where(row == i + e, summed, zero).reshape(-1, width) for e in (0, 1)]
            result = jnp.dot(turned, jnp.concatenate(both, axis=1), preferred_element_type=jnp.float32)
            held[g * GROUP + i] = result[:, :width]
            held[g * GROUP + i + 1] = result[:, width:]
            if i % 4 == 2:
                done = pl.ds(g * GROUP + i - 2, 4)
                pltpu.make_async_copy(held.at[done], out.at[done], sem).start()
        return carry

    lax.fori_loop(0, ni // GROUP, step, 0, unroll=4)
    pltpu.make_async_copy(held, out, sem).wait()


def call(kernel, name, inputs, outputs, scratch=(), limit=16, flops=0, moved=1 << 20, in_spec=VMEM, out_spec=VMEM):
    inputs = list(inputs)
    results = pl.pallas_call(
        kernel,
        in_specs=[in_spec] * len(inputs),
        out_specs=[out_spec] * len(outputs),
        out_shape=outputs,
        scratch_shapes=list(scratch),
        compiler_params=pltpu.CompilerParams(vmem_limit_bytes=limit * MIB),
        cost_estimate=pl.CostEstimate(flops=flops, bytes_accessed=moved, transcendentals=0),
        name=name,
    )(*inputs)
    return list(results)


def body(sizes, blocks, pattern, occupied, ligand):
    n_aux, n_orb, n_ao = sizes
    aux_rows, _, nu_width = blocks.shape
    owners = n_aux * n_orb
    ni = NOCC // owners
    q_total = aux_rows * owners
    panel_width = occupied.shape[1]
    width = ligand.shape[1]
    bf16 = functools.partial(jax.ShapeDtypeStruct, dtype=jnp.bfloat16)
    f32 = functools.partial(jax.ShapeDtypeStruct, dtype=jnp.float32)

    across = [(a, n_aux - 1 - a) for a in range(n_aux)]
    swap = [(c, 1 - c) for c in range(n_ao)]
    pattern = jnp.swapaxes(pattern, 1, 2)
    in_hbm = functools.partial(pltpu.with_memory_space_constraint, memory_space=pltpu.HBM)
    hbm = pl.BlockSpec(memory_space=pltpu.HBM)
    masked, part = call(
        masked_kernel,
        "masked_blocks",
        (in_hbm(pattern), in_hbm(blocks), in_hbm(occupied)),
        [bf16(blocks.shape), bf16((NB // n_ao, panel_width))],
        [
            pltpu.VMEM(blocks.shape, jnp.bfloat16),
            pltpu.SMEM(pattern.shape, pattern.dtype),
            pltpu.SemaphoreType.DMA((3,)),
        ],
        in_spec=hbm,
    )
    far_masked = lax.ppermute(masked, "aux", across)
    mine = lax.ppermute(part, "orb", swap)
    theirs = lax.ppermute(mine, "ao", swap)
    panel, orbitals = call(
        panel_kernel,
        "own_panel",
        (in_hbm(occupied), in_hbm(ligand)),
        [bf16(occupied.shape), bf16((NB // n_ao, width))],
        [pltpu.SemaphoreType.DMA((2,))],
        in_spec=hbm,
    )

    def square(messages):
        arrived = [messages[0]]
        for message, d in zip(messages[1:], (1, 3, 2)):
            moves = [
                (a * n_orb + o, (a ^ (d >> 1)) * n_orb + (o ^ (d & 1))) for a in range(n_aux) for o in range(n_orb)
            ]
            arrived.append(lax.ppermute(message, ("aux", "orb"), moves))
        return arrived

    work = 2 * NB * panel_width * nu_width * aux_rows
    messages = [bf16((aux_rows, ni, nu_width))] * 4
    turned, *own = call(
        own_kernel, "own_half", (panel, mine, theirs, masked), [bf16((4, ni, NB))] + messages, flops=work
    )
    own_here = square(own)
    value = call(
        density_kernel,
        "density_terms",
        (panel, mine, theirs, masked, turned, *own),
        [f32((aux_rows, 128))],
        [pltpu.VMEM(occupied.shape, jnp.bfloat16)],
        flops=work,
    )[0]
    value_there = lax.ppermute(value, "ao", swap)
    density = (value[:, 0] + value_there[:, 0]) / math.sqrt(NOCC)
    far = call(far_kernel, "far_half", (value, far_masked, turned), messages, flops=work)
    far_here = square(far)

    shape = (4 * aux_rows, ni, width)
    kept_and_given = [f32(shape), bf16(shape)]
    side = [bf16((ni // GROUP, nu_width, 4 * aux_rows * GROUP))]
    pair_work = 2 * shape[0] * ni * nu_width * width
    own_kept, own_given, own_rows = call(
        pair_and_turn_kernel,
        "own_pairs",
        (value_there, far[0], orbitals, *own_here),
        kept_and_given + side,
        flops=pair_work,
    )
    own_pairs = (own_kept, lax.ppermute(own_given, "ao", swap))
    all_here = call(
        mark_kernel, "far_rows_here", far_here, [f32((8, 128))], flops=1 << 34, in_spec=pl.BlockSpec(memory_space=pl.ANY)
    )[0]
    far_kept, far_given = call(
        pair_kernel, "far_pairs", (all_here, own_pairs[1], orbitals, *far_here), kept_and_given, flops=pair_work
    )
    far_pairs = (far_kept, lax.ppermute(far_given, "ao", swap))
    far_rows = call(turn_kernel, "far_turned", far_here, side)[0]

    result = (ni, nu_width, width)
    cross_terms = call(
        functools.partial(cross_kernel, 1.0 / math.sqrt(q_total)),
        "cross_terms",
        (own_rows, far_rows, *own_pairs, *far_pairs),
        [f32(result)],
        [pltpu.VMEM(result, jnp.float32), pltpu.SemaphoreType.DMA],
        limit=32,
        flops=32 * q_total * ni * nu_width * width,
        moved=18 * MIB,
        out_spec=pl.BlockSpec(memory_space=pltpu.HBM),
    )[0]
    return (density, cross_terms)


def plain_body(blocks, pattern, occupied, ligand):
    panels = lax.all_gather(occupied, "orb", axis=1, tiled=True)
    aux_rows = blocks.shape[0]
    nu_width = blocks.shape[2]
    nu_blocks = pattern.shape[2]
    opened = pattern[0].astype(jnp.bfloat16)
    masked = blocks.reshape(aux_rows, NBLK, BLK, nu_blocks, BLK) * opened[None, :, None, :, None]
    masked = masked.reshape(aux_rows, NB, nu_width)
    transformed = jnp.einsum(
        "qmn,mi->qin", masked, panels, preferred_element_type=jnp.float32
    ).astype(jnp.bfloat16)
    nu_start = lax.axis_index("ao") * nu_width
    own_rows = lax.dynamic_slice_in_dim(panels, nu_start, nu_width, 0)
    partial_value = jnp.einsum(
        "qin,ni->q", transformed, own_rows, preferred_element_type=jnp.float32
    )
    density = lax.psum(partial_value, "ao") / math.sqrt(NOCC)
    arrived = lax.all_to_all(transformed, ("aux", "orb"), split_axis=1, concat_axis=0, tiled=True)
    own_ligand = lax.dynamic_slice_in_dim(ligand, nu_start, nu_width, 0)
    pair_part = jnp.einsum("qin,nj->qij", arrived, own_ligand, preferred_element_type=jnp.float32)
    mixed_pairs = lax.psum(pair_part, "ao").astype(jnp.bfloat16)
    crossed = jnp.einsum("qin,qij->inj", arrived, mixed_pairs, preferred_element_type=jnp.float32)
    cross_terms = crossed / math.sqrt(arrived.shape[0])
    return (density, cross_terms)


def solution(mesh):
    sizes = (mesh.shape["aux"], mesh.shape["orb"], mesh.shape["ao"])
    kernels = sizes == (4, 2, 2)
    return jax.shard_map(
        functools.partial(body, sizes) if kernels else plain_body,
        mesh=mesh,
        in_specs=(
            P(("pose", "aux", "orb"), None, "ao"),
            P(("pose", "aux", "orb"), None, "ao"),
            P(None, "orb"),
            P(None, "pose"),
        ),
        out_specs=(P(("pose", "aux", "orb")), P(("pose", "aux", "orb"), "ao", None)),
        check_vma=False,
    )
```

```python
import functools
import math

import jax
import jax.numpy as jnp
from jax import lax
from jax.experimental import pallas as pl
from jax.experimental.pallas import tpu as pltpu
from jax.sharding import PartitionSpec as P

NOCC = 1024
BLK = 128
NBLK = 4
NB = 512
GROUP = 16
MIB = 1024 * 1024
VMEM = pl.BlockSpec(memory_space=pltpu.VMEM)


def masked_kernel(pattern, blocks, occupied, masked, part, held, opened, sems):
    aux_rows, _, nu_width = blocks.shape
    moves = ((blocks, held), (pattern, opened), (occupied.at[own_half_of(part.shape[0])], part))
    copies = [pltpu.make_async_copy(source, target, sems.at[k]) for k, (source, target) in enumerate(moves)]
    for copy in copies:
        copy.start()
    copies[0].wait()
    copies[1].wait()
    for q in range(aux_rows):
        for m in range(NBLK):
            for n in range(nu_width // BLK):
                rows, columns = pl.ds(m * BLK, BLK), pl.ds(n * BLK, BLK)
                tile = held[q, rows, columns]
                masked[q, rows, columns] = jnp.where(opened[0, n, m] != 0, tile, jnp.zeros_like(tile))
    for copy in copies[2:]:
        copy.wait()


def own_half_of(length):
    return pl.ds(pl.multiple_of(lax.axis_index("ao") * length, length), length)


def panel_kernel(occupied, ligand, panel, orbitals, sems):
    moves = ((occupied, panel), (ligand.at[own_half_of(orbitals.shape[0])], orbitals))
    copies = [pltpu.make_async_copy(source, target, sems.at[k]) for k, (source, target) in enumerate(moves)]
    for copy in copies:
        copy.start()
    for copy in copies:
        copy.wait()


def half_into(outs, turned, masked):
    for d, out in enumerate(outs):
        for q in range(out.shape[0]):
            out[q] = jnp.dot(turned[d], masked[q], preferred_element_type=jnp.float32).astype(jnp.bfloat16)


def own_kernel(occupied, mine, theirs, masked, turned, *outs):
    aux, orb, ao = (lax.axis_index(name) for name in ("aux", "orb", "ao"))
    ni = turned.shape[1]
    here = 2 * (aux & 1) + orb
    place = lambda s: jnp.where((here ^ s) == 0, 0, lax.rem((here ^ s) + 1, 3) + 1)
    near = orb == aux // 2

    @pl.when(near)
    def _():
        for s in range(turned.shape[0]):
            turned[place(s)] = occupied[:, s * ni : (s + 1) * ni].T

    @pl.when(jnp.logical_not(near))
    def _():
        depth = mine.shape[0]
        for e, rows in enumerate((mine, theirs)):
            first = pl.multiple_of((ao ^ e) * depth, depth)
            for s in range(turned.shape[0]):
                turned[place(s), :, pl.ds(first, depth)] = rows[:, s * ni : (s + 1) * ni].T

    half_into(outs, turned, masked)


def density_kernel(occupied, mine, theirs, masked, turned, *refs):
    messages, out, panel = refs[:-2], refs[-2], refs[-1]
    aux_rows, ni, nu_width = messages[0].shape
    depth = mine.shape[0]
    own = own_half_of(nu_width)
    near = lax.axis_index("orb") == lax.axis_index("aux") // 2

    @pl.when(near)
    def _():
        for e, rows in enumerate((mine, theirs)):
            panel[pl.ds(pl.multiple_of((lax.axis_index("ao") ^ e) * depth, depth), depth), :] = rows[...]

    @pl.when(jnp.logical_not(near))
    def _():
        panel[...] = occupied[...]

    totals = [0.0] * aux_rows
    for d, message in enumerate(messages):
        rows = turned[d, :, own].astype(jnp.float32)
        for q in range(aux_rows):
            totals[q] += jnp.sum(rows * message[q].astype(jnp.float32))
    for s in range(4):
        rows = panel[:, s * ni : (s + 1) * ni].T
        weights = panel[own, s * ni : (s + 1) * ni].T.astype(jnp.float32)
        for q in range(aux_rows):
            result = jnp.dot(rows, masked[q], preferred_element_type=jnp.float32).astype(jnp.bfloat16)
            totals[q] += jnp.sum(weights * result.astype(jnp.float32))
    for q in range(aux_rows):
        out[q : q + 1, :] = jnp.full((1, out.shape[1]), totals[q], jnp.float32)


def far_kernel(before, masked, turned, *outs):
    half_into(outs, turned, masked)


def pair_kernel(before, earlier, ligand, *refs):
    arrived, own, sent = refs[:-2], refs[-2], refs[-1]
    aux_rows, ni, nu_width = arrived[0].shape
    width = ligand.shape[1]
    for k, message in enumerate(arrived):
        part = jnp.dot(
            message[...].reshape(aux_rows * ni, nu_width), ligand[...], preferred_element_type=jnp.float32
        ).reshape(aux_rows, ni, width)
        own[k * aux_rows : (k + 1) * aux_rows] = part
        sent[k * aux_rows : (k + 1) * aux_rows] = part.astype(jnp.bfloat16)


def mark_kernel(*refs):
    refs[-1][...] = jnp.zeros_like(refs[-1])


def turn_kernel(*refs):
    messages, out = refs[:-1], refs[-1]
    nu_width = messages[0].shape[2]
    for g in range(out.shape[0]):
        here = pl.ds(g * GROUP, GROUP)
        out[g] = jnp.concatenate([x[:, here, :].reshape(-1, nu_width) for x in messages], axis=0).T


def pair_and_turn_kernel(before, earlier, ligand, *refs):
    pair_kernel(before, earlier, ligand, *refs[:-1])
    turn_kernel(*refs[:-3], refs[-1])


def cross_kernel(scale, near, far, *refs):
    pairs, (out, held, sem) = refs[:4], refs[4:]
    ni, _, width = out.shape

    def step(g, carry):
        here = pl.ds(pl.multiple_of(g * GROUP, GROUP), GROUP)
        turned = jnp.concatenate([near[g], far[g]], axis=1)
        summed = [pairs[j][:, here, :] + pairs[j + 1][:, here, :].astype(jnp.float32) for j in (0, 2)]
        summed = jnp.concatenate([(x * scale).astype(jnp.bfloat16) for x in summed], axis=0)
        row = lax.broadcasted_iota(jnp.int32, (1, GROUP, width), 1)
        zero = jnp.zeros_like(summed)
        for i in range(0, GROUP, 2):
            both = [jnp.where(row == i + e, summed, zero).reshape(-1, width) for e in (0, 1)]
            result = jnp.dot(turned, jnp.concatenate(both, axis=1), preferred_element_type=jnp.float32)
            held[g * GROUP + i] = result[:, :width]
            held[g * GROUP + i + 1] = result[:, width:]
            if i % 4 == 2:
                done = pl.ds(g * GROUP + i - 2, 4)
                pltpu.make_async_copy(held.at[done], out.at[done], sem).start()
        return carry

    lax.fori_loop(0, ni // GROUP, step, 0, unroll=4)
    pltpu.make_async_copy(held, out, sem).wait()


def call(kernel, name, inputs, outputs, scratch=(), limit=16, flops=0, moved=1 << 20, in_spec=VMEM, out_spec=VMEM):
    inputs = list(inputs)
    results = pl.pallas_call(
        kernel,
        in_specs=[in_spec] * len(inputs),
        out_specs=[out_spec] * len(outputs),
        out_shape=outputs,
        scratch_shapes=list(scratch),
        compiler_params=pltpu.CompilerParams(vmem_limit_bytes=limit * MIB),
        cost_estimate=pl.CostEstimate(flops=flops, bytes_accessed=moved, transcendentals=0),
        name=name,
    )(*inputs)
    return list(results)


def body(sizes, blocks, pattern, occupied, ligand):
    n_aux, n_orb, n_ao = sizes
    aux_rows, _, nu_width = blocks.shape
    owners = n_aux * n_orb
    ni = NOCC // owners
    q_total = aux_rows * owners
    panel_width = occupied.shape[1]
    width = ligand.shape[1]
    bf16 = functools.partial(jax.ShapeDtypeStruct, dtype=jnp.bfloat16)
    f32 = functools.partial(jax.ShapeDtypeStruct, dtype=jnp.float32)

    across = [(a, n_aux - 1 - a) for a in range(n_aux)]
    swap = [(c, 1 - c) for c in range(n_ao)]
    pattern = jnp.swapaxes(pattern, 1, 2)
    in_hbm = functools.partial(pltpu.with_memory_space_constraint, memory_space=pltpu.HBM)
    hbm = pl.BlockSpec(memory_space=pltpu.HBM)
    masked, part = call(
        masked_kernel,
        "masked_blocks",
        (in_hbm(pattern), in_hbm(blocks), in_hbm(occupied)),
        [bf16(blocks.shape), bf16((NB // n_ao, panel_width))],
        [
            pltpu.VMEM(blocks.shape, jnp.bfloat16),
            pltpu.SMEM(pattern.shape, pattern.dtype),
            pltpu.SemaphoreType.DMA((3,)),
        ],
        in_spec=hbm,
    )
    far_masked = lax.ppermute(masked, "aux", across)
    mine = lax.ppermute(part, "orb", swap)
    theirs = lax.ppermute(mine, "ao", swap)
    panel, orbitals = call(
        panel_kernel,
        "own_panel",
        (in_hbm(occupied), in_hbm(ligand)),
        [bf16(occupied.shape), bf16((NB // n_ao, width))],
        [pltpu.SemaphoreType.DMA((2,))],
        in_spec=hbm,
    )

    def square(messages):
        arrived = [messages[0]]
        for message, d in zip(messages[1:], (2, 3, 1)):
            moves = [
                (a * n_orb + o, (a ^ (d >> 1)) * n_orb + (o ^ (d & 1))) for a in range(n_aux) for o in range(n_orb)
            ]
            arrived.append(lax.ppermute(message, ("aux", "orb"), moves))
        return arrived

    work = 2 * NB * panel_width * nu_width * aux_rows
    messages = [bf16((aux_rows, ni, nu_width))] * 4
    turned, *own = call(
        own_kernel, "own_half", (panel, mine, theirs, masked), [bf16((4, ni, NB))] + messages, flops=work
    )
    own_here = square(own)
    value = call(
        density_kernel,
        "density_terms",
        (panel, mine, theirs, masked, turned, *own),
        [f32((aux_rows, 128))],
        [pltpu.VMEM(occupied.shape, jnp.bfloat16)],
        flops=work,
    )[0]
    value_there = lax.ppermute(value, "ao", swap)
    density = (value[:, 0] + value_there[:, 0]) / math.sqrt(NOCC)
    far = call(far_kernel, "far_half", (value, far_masked, turned), messages, flops=work)
    far_here = square(far)

    shape = (4 * aux_rows, ni, width)
    kept_and_given = [f32(shape), bf16(shape)]
    side = [bf16((ni // GROUP, nu_width, 4 * aux_rows * GROUP))]
    pair_work = 2 * shape[0] * ni * nu_width * width
    own_kept, own_given, own_rows = call(
        pair_and_turn_kernel,
        "own_pairs",
        (value_there, far[0], orbitals, *own_here),
        kept_and_given + side,
        flops=pair_work,
    )
    own_pairs = (own_kept, lax.ppermute(own_given, "ao", swap))
    all_here = call(
        mark_kernel, "far_rows_here", far_here, [f32((8, 128))], flops=1 << 34, in_spec=pl.BlockSpec(memory_space=pl.ANY)
    )[0]
    far_kept, far_given = call(
        pair_kernel, "far_pairs", (all_here, own_pairs[1], orbitals, *far_here), kept_and_given, flops=pair_work
    )
    far_pairs = (far_kept, lax.ppermute(far_given, "ao", swap))
    far_rows = call(turn_kernel, "far_turned", far_here, side)[0]

    result = (ni, nu_width, width)
    cross_terms = call(
        functools.partial(cross_kernel, 1.0 / math.sqrt(q_total)),
        "cross_terms",
        (own_rows, far_rows, *own_pairs, *far_pairs),
        [f32(result)],
        [pltpu.VMEM(result, jnp.float32), pltpu.SemaphoreType.DMA],
        limit=32,
        flops=32 * q_total * ni * nu_width * width,
        moved=18 * MIB,
        out_spec=pl.BlockSpec(memory_space=pltpu.HBM),
    )[0]
    return (density, cross_terms)


def plain_body(blocks, pattern, occupied, ligand):
    panels = lax.all_gather(occupied, "orb", axis=1, tiled=True)
    aux_rows = blocks.shape[0]
    nu_width = blocks.shape[2]
    nu_blocks = pattern.shape[2]
    opened = pattern[0].astype(jnp.bfloat16)
    masked = blocks.reshape(aux_rows, NBLK, BLK, nu_blocks, BLK) * opened[None, :, None, :, None]
    masked = masked.reshape(aux_rows, NB, nu_width)
    transformed = jnp.einsum(
        "qmn,mi->qin", masked, panels, preferred_element_type=jnp.float32
    ).astype(jnp.bfloat16)
    nu_start = lax.axis_index("ao") * nu_width
    own_rows = lax.dynamic_slice_in_dim(panels, nu_start, nu_width, 0)
    partial_value = jnp.einsum(
        "qin,ni->q", transformed, own_rows, preferred_element_type=jnp.float32
    )
    density = lax.psum(partial_value, "ao") / math.sqrt(NOCC)
    arrived = lax.all_to_all(transformed, ("aux", "orb"), split_axis=1, concat_axis=0, tiled=True)
    own_ligand = lax.dynamic_slice_in_dim(ligand, nu_start, nu_width, 0)
    pair_part = jnp.einsum("qin,nj->qij", arrived, own_ligand, preferred_element_type=jnp.float32)
    mixed_pairs = lax.psum(pair_part, "ao").astype(jnp.bfloat16)
    crossed = jnp.einsum("qin,qij->inj", arrived, mixed_pairs, preferred_element_type=jnp.float32)
    cross_terms = crossed / math.sqrt(arrived.shape[0])
    return (density, cross_terms)


def solution(mesh):
    sizes = (mesh.shape["aux"], mesh.shape["orb"], mesh.shape["ao"])
    kernels = sizes == (4, 2, 2)
    return jax.shard_map(
        functools.partial(body, sizes) if kernels else plain_body,
        mesh=mesh,
        in_specs=(
            P(("pose", "aux", "orb"), None, "ao"),
            P(("pose", "aux", "orb"), None, "ao"),
            P(None, "orb"),
            P(None, "pose"),
        ),
        out_specs=(P(("pose", "aux", "orb")), P(("pose", "aux", "orb"), "ao", None)),
        check_vma=False,
    )
```

```python
import functools
import math

import jax
import jax.numpy as jnp
from jax import lax
from jax.experimental import pallas as pl
from jax.experimental.pallas import tpu as pltpu
from jax.sharding import PartitionSpec as P

NOCC = 1024
BLK = 128
NBLK = 4
NB = 512
GROUP = 16
MIB = 1024 * 1024
VMEM = pl.BlockSpec(memory_space=pltpu.VMEM)


def masked_kernel(pattern, blocks, occupied, masked, part, held, opened, sems):
    aux_rows, _, nu_width = blocks.shape
    moves = ((blocks, held), (pattern, opened), (occupied.at[own_half_of(part.shape[0])], part))
    copies = [pltpu.make_async_copy(source, target, sems.at[k]) for k, (source, target) in enumerate(moves)]
    for copy in copies:
        copy.start()
    copies[0].wait()
    copies[1].wait()
    for q in range(aux_rows):
        for m in range(NBLK):
            for n in range(nu_width // BLK):
                rows, columns = pl.ds(m * BLK, BLK), pl.ds(n * BLK, BLK)
                tile = held[q, rows, columns]
                masked[q, rows, columns] = jnp.where(opened[0, n, m] != 0, tile, jnp.zeros_like(tile))
    for copy in copies[2:]:
        copy.wait()


def own_half_of(length):
    return pl.ds(pl.multiple_of(lax.axis_index("ao") * length, length), length)


def panel_kernel(occupied, ligand, panel, orbitals, sems):
    moves = ((occupied, panel), (ligand.at[own_half_of(orbitals.shape[0])], orbitals))
    copies = [pltpu.make_async_copy(source, target, sems.at[k]) for k, (source, target) in enumerate(moves)]
    for copy in copies:
        copy.start()
    for copy in copies:
        copy.wait()


def half_into(outs, turned, masked):
    for d, out in enumerate(outs):
        for q in range(out.shape[0]):
            out[q] = jnp.dot(turned[d], masked[q], preferred_element_type=jnp.float32).astype(jnp.bfloat16)


def own_kernel(occupied, mine, theirs, masked, turned, *outs):
    aux, orb, ao = (lax.axis_index(name) for name in ("aux", "orb", "ao"))
    ni = turned.shape[1]
    here = 2 * (aux & 1) + orb
    place = lambda s: (4 - (here ^ s)) & 3
    near = orb == aux // 2

    @pl.when(near)
    def _():
        for s in range(turned.shape[0]):
            turned[place(s)] = occupied[:, s * ni : (s + 1) * ni].T

    @pl.when(jnp.logical_not(near))
    def _():
        depth = mine.shape[0]
        for e, rows in enumerate((mine, theirs)):
            first = pl.multiple_of((ao ^ e) * depth, depth)
            for s in range(turned.shape[0]):
                turned[place(s), :, pl.ds(first, depth)] = rows[:, s * ni : (s + 1) * ni].T

    half_into(outs, turned, masked)


def density_kernel(occupied, mine, theirs, masked, turned, *refs):
    messages, out, panel = refs[:-2], refs[-2], refs[-1]
    aux_rows, ni, nu_width = messages[0].shape
    depth = mine.shape[0]
    own = own_half_of(nu_width)
    near = lax.axis_index("orb") == lax.axis_index("aux") // 2

    @pl.when(near)
    def _():
        for e, rows in enumerate((mine, theirs)):
            panel[pl.ds(pl.multiple_of((lax.axis_index("ao") ^ e) * depth, depth), depth), :] = rows[...]

    @pl.when(jnp.logical_not(near))
    def _():
        panel[...] = occupied[...]

    totals = [0.0] * aux_rows
    for d, message in enumerate(messages):
        rows = turned[d, :, own].astype(jnp.float32)
        for q in range(aux_rows):
            totals[q] += jnp.sum(rows * message[q].astype(jnp.float32))
    for s in range(4):
        rows = panel[:, s * ni : (s + 1) * ni].T
        weights = panel[own, s * ni : (s + 1) * ni].T.astype(jnp.float32)
        for q in range(aux_rows):
            result = jnp.dot(rows, masked[q], preferred_element_type=jnp.float32).astype(jnp.bfloat16)
            totals[q] += jnp.sum(weights * result.astype(jnp.float32))
    for q in range(aux_rows):
        out[q : q + 1, :] = jnp.full((1, out.shape[1]), totals[q], jnp.float32)


def far_kernel(before, masked, turned, *outs):
    half_into(outs, turned, masked)


def pair_kernel(before, earlier, ligand, *refs):
    arrived, own, sent = refs[:-2], refs[-2], refs[-1]
    aux_rows, ni, nu_width = arrived[0].shape
    width = ligand.shape[1]
    for k, message in enumerate(arrived):
        part = jnp.dot(
            message[...].reshape(aux_rows * ni, nu_width), ligand[...], preferred_element_type=jnp.float32
        ).reshape(aux_rows, ni, width)
        own[k * aux_rows : (k + 1) * aux_rows] = part
        sent[k * aux_rows : (k + 1) * aux_rows] = part.astype(jnp.bfloat16)


def mark_kernel(*refs):
    refs[-1][...] = jnp.zeros_like(refs[-1])


def turn_kernel(*refs):
    messages, out = refs[:-1], refs[-1]
    nu_width = messages[0].shape[2]
    for g in range(out.shape[0]):
        here = pl.ds(g * GROUP, GROUP)
        out[g] = jnp.concatenate([x[:, here, :].reshape(-1, nu_width) for x in messages], axis=0).T


def pair_and_turn_kernel(before, earlier, ligand, *refs):
    pair_kernel(before, earlier, ligand, *refs[:-1])
    turn_kernel(*refs[:-3], refs[-1])


def cross_kernel(scale, near, far, *refs):
    pairs, (out, held, sem) = refs[:4], refs[4:]
    ni, _, width = out.shape

    def step(g, carry):
        here = pl.ds(pl.multiple_of(g * GROUP, GROUP), GROUP)
        turned = jnp.concatenate([near[g], far[g]], axis=1)
        summed = [pairs[j][:, here, :] + pairs[j + 1][:, here, :].astype(jnp.float32) for j in (0, 2)]
        summed = jnp.concatenate([(x * scale).astype(jnp.bfloat16) for x in summed], axis=0)
        row = lax.broadcasted_iota(jnp.int32, (1, GROUP, width), 1)
        zero = jnp.zeros_like(summed)
        for i in range(0, GROUP, 2):
            both = [jnp.where(row == i + e, summed, zero).reshape(-1, width) for e in (0, 1)]
            result = jnp.dot(turned, jnp.concatenate(both, axis=1), preferred_element_type=jnp.float32)
            held[g * GROUP + i] = result[:, :width]
            held[g * GROUP + i + 1] = result[:, width:]
            done = pl.ds(g * GROUP + i, 2)
            pltpu.make_async_copy(held.at[done], out.at[done], sem).start()
        return carry

    lax.fori_loop(0, ni // GROUP, step, 0, unroll=4)
    pltpu.make_async_copy(held, out, sem).wait()


def call(kernel, name, inputs, outputs, scratch=(), limit=16, flops=0, moved=1 << 20, in_spec=VMEM, out_spec=VMEM):
    inputs = list(inputs)
    results = pl.pallas_call(
        kernel,
        in_specs=[in_spec] * len(inputs),
        out_specs=[out_spec] * len(outputs),
        out_shape=outputs,
        scratch_shapes=list(scratch),
        compiler_params=pltpu.CompilerParams(vmem_limit_bytes=limit * MIB),
        cost_estimate=pl.CostEstimate(flops=flops, bytes_accessed=moved, transcendentals=0),
        name=name,
    )(*inputs)
    return list(results)


def body(sizes, blocks, pattern, occupied, ligand):
    n_aux, n_orb, n_ao = sizes
    aux_rows, _, nu_width = blocks.shape
    owners = n_aux * n_orb
    ni = NOCC // owners
    q_total = aux_rows * owners
    panel_width = occupied.shape[1]
    width = ligand.shape[1]
    bf16 = functools.partial(jax.ShapeDtypeStruct, dtype=jnp.bfloat16)
    f32 = functools.partial(jax.ShapeDtypeStruct, dtype=jnp.float32)

    across = [(a, n_aux - 1 - a) for a in range(n_aux)]
    swap = [(c, 1 - c) for c in range(n_ao)]
    pattern = jnp.swapaxes(pattern, 1, 2)
    in_hbm = functools.partial(pltpu.with_memory_space_constraint, memory_space=pltpu.HBM)
    hbm = pl.BlockSpec(memory_space=pltpu.HBM)
    masked, part = call(
        masked_kernel,
        "masked_blocks",
        (in_hbm(pattern), in_hbm(blocks), in_hbm(occupied)),
        [bf16(blocks.shape), bf16((NB // n_ao, panel_width))],
        [
            pltpu.VMEM(blocks.shape, jnp.bfloat16),
            pltpu.SMEM(pattern.shape, pattern.dtype),
            pltpu.SemaphoreType.DMA((3,)),
        ],
        in_spec=hbm,
    )
    far_masked = lax.ppermute(masked, "aux", across)
    mine = lax.ppermute(part, "orb", swap)
    theirs = lax.ppermute(mine, "ao", swap)
    panel, orbitals = call(
        panel_kernel,
        "own_panel",
        (in_hbm(occupied), in_hbm(ligand)),
        [bf16(occupied.shape), bf16((NB // n_ao, width))],
        [pltpu.SemaphoreType.DMA((2,))],
        in_spec=hbm,
    )

    def square(messages):
        arrived = [messages[0]]
        for message, d in zip(messages[1:], (3, 2, 1)):
            moves = [
                (a * n_orb + o, (a ^ (d >> 1)) * n_orb + (o ^ (d & 1))) for a in range(n_aux) for o in range(n_orb)
            ]
            arrived.append(lax.ppermute(message, ("aux", "orb"), moves))
        return arrived

    work = 2 * NB * panel_width * nu_width * aux_rows
    messages = [bf16((aux_rows, ni, nu_width))] * 4
    turned, *own = call(
        own_kernel, "own_half", (panel, mine, theirs, masked), [bf16((4, ni, NB))] + messages, flops=work
    )
    own_here = square(own)
    value = call(
        density_kernel,
        "density_terms",
        (panel, mine, theirs, masked, turned, *own),
        [f32((aux_rows, 128))],
        [pltpu.VMEM(occupied.shape, jnp.bfloat16)],
        flops=work,
    )[0]
    value_there = lax.ppermute(value, "ao", swap)
    density = (value[:, 0] + value_there[:, 0]) / math.sqrt(NOCC)
    far = call(far_kernel, "far_half", (value, far_masked, turned), messages, flops=work)
    far_here = square(far)

    shape = (4 * aux_rows, ni, width)
    kept_and_given = [f32(shape), bf16(shape)]
    side = [bf16((ni // GROUP, nu_width, 4 * aux_rows * GROUP))]
    pair_work = 2 * shape[0] * ni * nu_width * width
    own_kept, own_given, own_rows = call(
        pair_and_turn_kernel,
        "own_pairs",
        (value_there, far[0], orbitals, *own_here),
        kept_and_given + side,
        flops=pair_work,
    )
    own_pairs = (own_kept, lax.ppermute(own_given, "ao", swap))
    all_here = call(
        mark_kernel, "far_rows_here", far_here, [f32((8, 128))], flops=1 << 34, in_spec=pl.BlockSpec(memory_space=pl.ANY)
    )[0]
    far_kept, far_given = call(
        pair_kernel, "far_pairs", (all_here, own_pairs[1], orbitals, *far_here), kept_and_given, flops=pair_work
    )
    far_pairs = (far_kept, lax.ppermute(far_given, "ao", swap))
    far_rows = call(turn_kernel, "far_turned", far_here, side)[0]

    result = (ni, nu_width, width)
    cross_terms = call(
        functools.partial(cross_kernel, 1.0 / math.sqrt(q_total)),
        "cross_terms",
        (own_rows, far_rows, *own_pairs, *far_pairs),
        [f32(result)],
        [pltpu.VMEM(result, jnp.float32), pltpu.SemaphoreType.DMA],
        limit=32,
        flops=32 * q_total * ni * nu_width * width,
        moved=18 * MIB,
        out_spec=pl.BlockSpec(memory_space=pltpu.HBM),
    )[0]
    return (density, cross_terms)


def plain_body(blocks, pattern, occupied, ligand):
    panels = lax.all_gather(occupied, "orb", axis=1, tiled=True)
    aux_rows = blocks.shape[0]
    nu_width = blocks.shape[2]
    nu_blocks = pattern.shape[2]
    opened = pattern[0].astype(jnp.bfloat16)
    masked = blocks.reshape(aux_rows, NBLK, BLK, nu_blocks, BLK) * opened[None, :, None, :, None]
    masked = masked.reshape(aux_rows, NB, nu_width)
    transformed = jnp.einsum(
        "qmn,mi->qin", masked, panels, preferred_element_type=jnp.float32
    ).astype(jnp.bfloat16)
    nu_start = lax.axis_index("ao") * nu_width
    own_rows = lax.dynamic_slice_in_dim(panels, nu_start, nu_width, 0)
    partial_value = jnp.einsum(
        "qin,ni->q", transformed, own_rows, preferred_element_type=jnp.float32
    )
    density = lax.psum(partial_value, "ao") / math.sqrt(NOCC)
    arrived = lax.all_to_all(transformed, ("aux", "orb"), split_axis=1, concat_axis=0, tiled=True)
    own_ligand = lax.dynamic_slice_in_dim(ligand, nu_start, nu_width, 0)
    pair_part = jnp.einsum("qin,nj->qij", arrived, own_ligand, preferred_element_type=jnp.float32)
    mixed_pairs = lax.psum(pair_part, "ao").astype(jnp.bfloat16)
    crossed = jnp.einsum("qin,qij->inj", arrived, mixed_pairs, preferred_element_type=jnp.float32)
    cross_terms = crossed / math.sqrt(arrived.shape[0])
    return (density, cross_terms)


def solution(mesh):
    sizes = (mesh.shape["aux"], mesh.shape["orb"], mesh.shape["ao"])
    kernels = sizes == (4, 2, 2)
    return jax.shard_map(
        functools.partial(body, sizes) if kernels else plain_body,
        mesh=mesh,
        in_specs=(
            P(("pose", "aux", "orb"), None, "ao"),
            P(("pose", "aux", "orb"), None, "ao"),
            P(None, "orb"),
            P(None, "pose"),
        ),
        out_specs=(P(("pose", "aux", "orb")), P(("pose", "aux", "orb"), "ao", None)),
        check_vma=False,
    )
```
